32 devices in a mesh: dp: 8 (over z, core), fsdp: 4 (over y, x).
Axes of the slice: x: 2, y: 2, z: 4, core: 2. Of those that a mesh axis runs over, the one named last changes fastest.
Arguments:
- tokens: bfloat16 [64, 384, 1024], P(('dp', 'fsdp')), may hold values from -6 to 6
- text_states: bfloat16 [64, 128, 1024], P(('dp', 'fsdp')), may hold values from -6 to 6
- caption_len: int32 [64], P(('dp', 'fsdp')), may hold values from 1 to 128, as said below
- out_grad: bfloat16 [64, 384, 1024], P(('dp', 'fsdp')), may hold values from -6 to 6
- norm1_gain: bfloat16 [1024], P(('dp', 'fsdp')), may hold values from 0.099609375 to 1.8984375
- norm1_bias: bfloat16 [1024], P(('dp', 'fsdp')), may hold values from -3 to 3
- qkv_weight: bfloat16 [1024, 3072], P(('dp', 'fsdp')), may hold values from -0.1875 to 0.1875
- self_out: bfloat16 [1024, 1024], P(('dp', 'fsdp')), may hold values from -0.75 to 0.75
- norm2_gain: bfloat16 [1024], P(('dp', 'fsdp')), may hold values from 0.099609375 to 1.8984375
- norm2_bias: bfloat16 [1024], P(('dp', 'fsdp')), may hold values from -3 to 3
- cross_query: bfloat16 [1024, 1024], P(('dp', 'fsdp')), may hold values from -0.1875 to 0.1875
- cross_kv: bfloat16 [1024, 2048], P(('dp', 'fsdp')), may hold values from -0.1875 to 0.1875
- cross_out: bfloat16 [1024, 1024], P(('dp', 'fsdp')), may hold values from -0.375 to 0.375
- norm3_gain: bfloat16 [1024], P(('dp', 'fsdp')), may hold values from 0.099609375 to 1.8984375
- norm3_bias: bfloat16 [1024], P(('dp', 'fsdp')), may hold values from -3 to 3
- ff_in: bfloat16 [1024, 4096], P(('dp', 'fsdp')), may hold values from -0.1875 to 0.1875
- ff_in_bias: bfloat16 [4096], P(('dp', 'fsdp')), may hold values from -3 to 3
- ff_out: bfloat16 [4096, 1024], P(('dp', 'fsdp')), may hold values from -0.09375 to 0.09375
- ff_out_bias: bfloat16 [1024], P(('dp', 'fsdp')), may hold values from -3 to 3
Outputs:
- result: bfloat16 [64, 384, 1024], P(('dp', 'fsdp'))
- tokens_grad: bfloat16 [64, 384, 1024], P(('dp', 'fsdp'))
- text_grad: bfloat16 [64, 128, 1024], P(('dp', 'fsdp'))
- norm1_gain_grad: float32 [1024], P(('dp', 'fsdp'))
- norm1_bias_grad: float32 [1024], P(('dp', 'fsdp'))
- qkv_weight_grad: float32 [1024, 3072], P(('dp', 'fsdp'))
- self_out_grad: float32 [1024, 1024], P(('dp', 'fsdp'))
- norm2_gain_grad: float32 [1024], P(('dp', 'fsdp'))
- norm2_bias_grad: float32 [1024], P(('dp', 'fsdp'))
- cross_query_grad: float32 [1024, 1024], P(('dp', 'fsdp'))
- cross_kv_grad: float32 [1024, 2048], P(('dp', 'fsdp'))
- cross_out_grad: float32 [1024, 1024], P(('dp', 'fsdp'))
- norm3_gain_grad: float32 [1024], P(('dp', 'fsdp'))
- norm3_bias_grad: float32 [1024], P(('dp', 'fsdp'))
- ff_in_grad: float32 [1024, 4096], P(('dp', 'fsdp'))
- ff_in_bias_grad: float32 [4096], P(('dp', 'fsdp'))
- ff_out_grad: float32 [4096, 1024], P(('dp', 'fsdp'))
- ff_out_bias_grad: float32 [1024], P(('dp', 'fsdp'))
The draws below stay inside these ranges and needn't reach their ends.
Inputs may be any that keep to these rules, and one draw needn't show every extreme that they name: `caption_len`: each item's caption length; some item's is exactly 128.
All inputs are finite; a program needn't handle non-finite values.
Results may differ from the reference program's by a relative error of at most 0.017.
Values may be sent and summed in bfloat16 or wider, within the bound.
No kernel may reach another device: no remote copies, remote signals or barrier semaphores. Data moves between devices by JAX's collectives and lax.ppermute only.
A program may use at most 320 MiB of HBM per device.

```python
import jax
import jax.numpy as jnp
from jax import lax

D = 1024
FF = 4096
HEADS = 16
HEADDIM = 64
TEXT = 128
SEQ = 384
ITEMS = 64


def draw_caption_len(key, part):
    key = jax.random.fold_in(key, 7)
    first_key, second_key, third_key = jax.random.split(key, 3)
    levels = TEXT.bit_length() - 1
    power = jax.random.randint(first_key, (ITEMS,), 0, levels + 1)
    ceiling = jnp.left_shift(jnp.ones((ITEMS,), jnp.int32), power)
    lengths = 1 + jax.random.randint(second_key, (ITEMS,), 0, ceiling)
    lengths = jnp.minimum(lengths, TEXT)
    chosen = jax.random.randint(third_key, (), 0, ITEMS)
    positions = jnp.arange(ITEMS, dtype=jnp.int32)
    return jnp.where(positions == chosen, TEXT, lengths).astype(jnp.int32)


def strengthened(entries, stream_key, source, target, parts, factor):
    def block_of(axis_at):
        return (jnp.arange(entries.shape[axis_at]) // (entries.shape[axis_at] // parts)).reshape((-1,) + (1,) * (entries.ndim - 1 - axis_at))

    first = jax.random.permutation(stream_key, parts)[block_of(target)]
    second = (block_of(target) + parts // 2) % parts
    return jnp.where((block_of(source) == first) | (block_of(source) == second), factor * entries, entries)


def steps_of(stream_key, shape, cuts, least, largest):
    level = 1.0
    for dim, shards_of in cuts:
        steps = jax.random.uniform(jax.random.fold_in(jax.random.fold_in(stream_key, 6), dim), (shards_of,), jnp.float32, least / len(cuts), largest / len(cuts))
        level = level * jnp.repeat(jnp.exp(steps), shape[dim] // shards_of).reshape((-1,) + (1,) * (len(shape) - 1 - dim))
    return level


def bell_draw(own_key, dims, scale, limit, pieces=(), kind=jnp.bfloat16):
    entries = scale * jax.random.normal(own_key, dims, jnp.float32)
    if pieces:
        entries = entries * steps_of(own_key, dims, pieces, -0.22, 0.18)
    return jnp.clip(entries, -limit, limit).astype(kind)


def bell_draw_with(key, dims, deviation, reach, shards, heavy, held_as=jnp.bfloat16):
    result = deviation * jax.random.normal(key, dims, jnp.float32)
    if shards:
        result = result * steps_of(key, dims, shards, -0.22, 0.18)
    return jnp.clip(strengthened(result, jax.random.fold_in(key, 3), *heavy), -reach, reach).astype(held_as)


def setup_inputs(seed: int = 0) -> dict:
    key_list = jax.random.split(jax.random.key(seed), 20)
    tokens = bell_draw(key_list[0], (ITEMS, SEQ, D), 1.0, 6.0, ((0, 32),))
    text_states = bell_draw(key_list[1], (ITEMS, TEXT, D), 1.0, 6.0, ((0, 32),))
    caption_len = draw_caption_len(jax.random.fold_in(key_list[19], 71), 0)
    out_grad = bell_draw_with(key_list[3], (ITEMS, SEQ, D), 1.0, 6.0, ((0, 32),), (0, 2, 32, 2.75))
    norm1_gain = jnp.clip(1.0 + 0.18 * jax.random.normal(key_list[4], (D,), jnp.float32), 0.099609375, 1.8984375).astype(jnp.bfloat16)
    norm1_bias = bell_draw(key_list[5], (D,), 0.5, 3.0, ((0, 32),))
    qkv_weight = bell_draw(key_list[6], (D, 3 * D), D ** -0.5, 0.1875, ((0, 32),))
    self_out = bell_draw(key_list[7], (D, D), (D // 16) ** -0.5, 0.75, ((0, 32),))
    norm2_gain = jnp.clip(1.0 + 0.18 * jax.random.normal(key_list[8], (D,), jnp.float32), 0.099609375, 1.8984375).astype(jnp.bfloat16)
    norm2_bias = bell_draw(key_list[9], (D,), 0.5, 3.0, ((0, 32),))
    cross_query = bell_draw(key_list[10], (D, D), D ** -0.5, 0.1875, ((0, 32),))
    cross_kv = bell_draw(key_list[11], (D, 2 * D), D ** -0.5, 0.1875, ((0, 32),))
    cross_out = bell_draw(key_list[12], (D, D), (D // 4) ** -0.5, 0.375, ((0, 32),))
    norm3_gain = jnp.clip(1.0 + 0.18 * jax.random.normal(key_list[13], (D,), jnp.float32), 0.099609375, 1.8984375).astype(jnp.bfloat16)
    norm3_bias = bell_draw(key_list[14], (D,), 0.5, 3.0, ((0, 32),))
    ff_in = bell_draw(key_list[15], (D, FF), D ** -0.5, 0.1875, ((0, 32),))
    ff_in_bias = bell_draw(key_list[16], (FF,), 0.5, 3.0, ((0, 32),))
    ff_out = bell_draw(key_list[17], (FF, D), FF ** -0.5, 0.09375, ((0, 32),))
    ff_out_bias = bell_draw(key_list[18], (D,), 0.5, 3.0, ((0, 32),))
    return dict(tokens=tokens, text_states=text_states, caption_len=caption_len, out_grad=out_grad, norm1_gain=norm1_gain, norm1_bias=norm1_bias, qkv_weight=qkv_weight, self_out=self_out, norm2_gain=norm2_gain, norm2_bias=norm2_bias, cross_query=cross_query, cross_kv=cross_kv, cross_out=cross_out, norm3_gain=norm3_gain, norm3_bias=norm3_bias, ff_in=ff_in, ff_in_bias=ff_in_bias, ff_out=ff_out, ff_out_bias=ff_out_bias)


EPSILON = 1e-05
NEGATIVE = -1e+30
HIGHEST = lax.Precision.HIGHEST

@jax.custom_vjp
def low(v):
    return lax.optimization_barrier(v.astype(jnp.bfloat16)).astype(jnp.float32)

@jax.custom_vjp
def low_back(v):
    return v

def low_keep(v):
    return (low(v), None)

def low_pass(kept, grad):
    return (grad,)

def back_keep(v):
    return (v, None)

def back_low(kept, grad):
    return (low(grad),)
low.defvjp(low_keep, low_pass)
low_back.defvjp(back_keep, back_low)

def matmul(first_matrix, second_matrix):
    return jnp.dot(first_matrix, second_matrix, precision=HIGHEST)

def layer_norm(values, gain, bias):
    center = values - lax.optimization_barrier(jnp.mean(values, axis=-1, keepdims=True))
    spread = lax.optimization_barrier(jnp.mean(center * center, axis=-1, keepdims=True))
    return center * lax.rsqrt(spread + EPSILON) * gain + bias

def attend(query_rows, key_rows, value_rows, allowed):
    row_count = query_rows.shape[0]
    query_heads = query_rows.reshape(row_count, HEADS, HEADDIM)
    key_heads = key_rows.reshape(key_rows.shape[0], HEADS, HEADDIM)
    value_heads = value_rows.reshape(value_rows.shape[0], HEADS, HEADDIM)
    scores = jnp.einsum('qhd,khd->hqk', query_heads, key_heads, precision=HIGHEST) * HEADDIM ** (-0.5)
    scores = low_back(scores)
    scores = jnp.where(allowed[None], scores, NEGATIVE)
    row_max = lax.optimization_barrier(jnp.max(scores, axis=-1, keepdims=True))
    weights = jnp.exp(scores - row_max)
    probability = low(weights / lax.optimization_barrier(jnp.sum(weights, axis=-1, keepdims=True)))
    attended = jnp.einsum('hqk,khd->qhd', probability, value_heads, precision=HIGHEST)
    return low(low_back(attended.reshape(row_count, HEADS * HEADDIM)))

def layer_block(params, token_rows, text_rows, caption_length):
    norm1_gain, norm1_bias, qkv_weight, self_out, norm2_gain, norm2_bias, cross_query, cross_kv, cross_out, norm3_gain, norm3_bias, ff_in, ff_in_bias, ff_out, ff_out_bias = params
    row_count = token_rows.shape[0]
    model_width = token_rows.shape[1]
    normed = low(layer_norm(token_rows, norm1_gain, norm1_bias))
    projected = low(low_back(matmul(normed, qkv_weight)))
    causal = lax.broadcasted_iota(jnp.int32, (row_count, row_count), 0) >= lax.broadcasted_iota(jnp.int32, (row_count, row_count), 1)
    attended = attend(projected[:, :model_width], projected[:, model_width:2 * model_width], projected[:, 2 * model_width:], causal)
    after_self = token_rows + low_back(matmul(attended, self_out))
    normed = low(layer_norm(after_self, norm2_gain, norm2_bias))
    query_rows = low(low_back(matmul(normed, cross_query)))
    text_kv = low(low_back(matmul(text_rows, cross_kv)))
    visible = lax.broadcasted_iota(jnp.int32, (row_count, text_rows.shape[0]), 1) < caption_length
    attended = attend(query_rows, text_kv[:, :model_width], text_kv[:, model_width:], visible)
    after_cross = after_self + low_back(matmul(attended, cross_out))
    normed = low(layer_norm(after_cross, norm3_gain, norm3_bias))
    before = low_back(matmul(normed, ff_in) + ff_in_bias)
    middle = low(jax.nn.gelu(before, approximate=True))
    return after_cross + low_back(matmul(middle, ff_out) + ff_out_bias)

def reference(tokens, text_states, caption_len, out_grad, norm1_gain, norm1_bias, qkv_weight, self_out, norm2_gain, norm2_bias, cross_query, cross_kv, cross_out, norm3_gain, norm3_bias, ff_in, ff_in_bias, ff_out, ff_out_bias):
    params = tuple((member.astype(jnp.float32) for member in (norm1_gain, norm1_bias, qkv_weight, self_out, norm2_gain, norm2_bias, cross_query, cross_kv, cross_out, norm3_gain, norm3_bias, ff_in, ff_in_bias, ff_out, ff_out_bias)))
    item_count = tokens.shape[0]
    group_size = 8
    group_count = item_count // group_size
    caption_groups = caption_len.reshape(group_count, group_size).astype(jnp.int32)

    def run_group(weights, token_group, text_group, length_group):
        return jax.vmap(lambda token_rows, text_rows, caption_length: layer_block(weights, token_rows, text_rows, caption_length))(token_group, text_group, length_group)
    checked = jax.checkpoint(run_group)

    def forward(weights, token_values, text_values):
        token_groups = token_values.reshape(group_count, group_size, SEQ, D)
        text_groups = text_values.reshape(group_count, group_size, TEXT, D)
        outputs = lax.map(lambda group_parts: checked(weights, group_parts[0], group_parts[1], group_parts[2]), (token_groups, text_groups, caption_groups))
        return outputs.reshape(item_count, SEQ, D)
    outcome, pullback = jax.vjp(forward, params, tokens.astype(jnp.float32), text_states.astype(jnp.float32))
    grad_terms, token_grad, text_grad = pullback(out_grad.astype(jnp.float32))
    return (outcome.astype(jnp.bfloat16), token_grad.astype(jnp.bfloat16), text_grad.astype(jnp.bfloat16), grad_terms[0], grad_terms[1], grad_terms[2], grad_terms[3], grad_terms[4], grad_terms[5], grad_terms[6], grad_terms[7], grad_terms[8], grad_terms[9], grad_terms[10], grad_terms[11], grad_terms[12], grad_terms[13], grad_terms[14])
```

```python
import functools

import jax
import jax.numpy as jnp
from jax import lax
from jax.experimental import pallas as pl
from jax.experimental.pallas import tpu as pltpu
from jax.sharding import PartitionSpec as P

HEADS = 16
EPSILON = 1e-05
NEGATIVE = -1e30
AXES = ("dp", "fsdp")
F32 = jnp.float32
BF16 = jnp.bfloat16


class Place:
    def __init__(self, line_count, plane_count):
        self.lines = line_count
        self.planes = plane_count
        self.bits = [1 << k for k in range(plane_count.bit_length() - 1)]
        dp = lax.axis_index("dp")
        self.line = dp // 2
        self.core = dp % 2
        self.plane = lax.axis_index("fsdp")

    def _pairs(self, target):
        pairs = []
        for line in range(self.lines):
            for core in range(2):
                for plane in range(self.planes):
                    l, c, p = target(line, core, plane)
                    pairs.append(
                        (
                            (line * 2 + core) * self.planes + plane,
                            (l * 2 + c) * self.planes + p,
                        )
                    )
        return pairs

    def shift_line(self, value, step):
        return lax.ppermute(
            value, AXES, self._pairs(lambda l, c, p: ((l + step) % self.lines, c, p))
        )

    def swap_plane(self, value, bit):
        return lax.ppermute(value, AXES, self._pairs(lambda l, c, p: (l, c, p ^ bit)))

    def swap_core(self, value):
        return lax.ppermute(value, AXES, self._pairs(lambda l, c, p: (l, 1 - c, p)))


def interleave(pieces, slots):
    count = len(pieces)
    outer, rows, width = pieces[0].shape
    tile = 2048 if width % 2048 == 0 else 1024

    def body(slots_ref, *refs):
        out_ref = refs[count]
        for k in range(count):
            out_ref[0, pl.ds(slots_ref[k], 1)] = refs[k][...]

    return pl.pallas_call(
        body,
        out_shape=jax.ShapeDtypeStruct((outer, count, rows, width), pieces[0].dtype),
        grid_spec=pltpu.PrefetchScalarGridSpec(
            num_scalar_prefetch=1,
            grid=(outer, width // tile),
            in_specs=[pl.BlockSpec((1, rows, tile), lambda a, n, s: (a, 0, n))] * count,
            out_specs=pl.BlockSpec((1, count, rows, tile), lambda a, n, s: (a, 0, 0, n)),
        ),
        name="interleave",
    )(slots.astype(jnp.int32), *pieces)


def gather(place, shard, order):
    rows, width = shard.shape
    steps = [shard] + [place.shift_line(shard, s) for s in range(1, place.lines)]
    held = interleave(
        [piece[None] for piece in steps],
        (place.line - jnp.arange(place.lines)) % place.lines,
    ).reshape(place.lines, rows, width)
    pieces, masks = [held], [0]
    for bit in order:
        pieces = pieces + [place.swap_plane(piece, bit) for piece in pieces]
        masks = masks + [mask ^ bit for mask in masks]
    half = interleave(pieces, jnp.array(masks) ^ place.plane)
    half = half.reshape(place.lines, place.planes * rows, width)
    other = place.swap_core(half)
    return interleave([half, other], jnp.array([0, 1]) ^ place.core)


def gather_small(place, shard):
    line_pieces = jnp.stack(
        [shard] + [place.shift_line(shard, s) for s in range(1, place.lines)]
    )
    held = line_pieces[(place.line - jnp.arange(place.lines)) % place.lines]
    pieces, masks = held[None], [0]
    for bit in place.bits:
        pieces = jnp.concatenate([pieces, place.swap_plane(pieces, bit)])
        masks = masks + [mask ^ bit for mask in masks]
    inverse = [masks.index(m) for m in range(len(masks))]
    half = pieces[jnp.array(inverse)[jnp.arange(place.planes) ^ place.plane]]
    both = jnp.stack([half, place.swap_core(half)])[jnp.arange(2) ^ place.core]
    return both.transpose(2, 0, 1, 3, 4)[:, :, :, 0]


def scatter(place, terms, order, kind):
    width = terms.shape[1]
    rows = terms.shape[0] // (place.lines * 2 * place.planes)
    halves = terms.reshape(place.lines, 2, place.planes * rows, width)
    mine = lax.dynamic_index_in_dim(halves, place.core, 1, keepdims=False)
    other = lax.dynamic_index_in_dim(halves, 1 - place.core, 1, keepdims=False)
    arrived = place.swap_core(other.astype(kind))
    total = (mine.astype(F32) + arrived.astype(F32)).astype(kind)
    total = total.reshape(place.lines, place.planes, rows, width)
    parts = {
        mask: lax.dynamic_index_in_dim(total, place.plane ^ mask, 1, keepdims=False)
        for mask in range(place.planes)
    }
    for bit in reversed(order):
        kept = [mask for mask in parts if not mask & bit]
        arrivals = {mask: place.swap_plane(parts[mask ^ bit], bit) for mask in kept}
        parts = {
            mask: (parts[mask].astype(F32) + arrivals[mask].astype(F32)).astype(kind)
            for mask in kept
        }
    total = parts[0]
    result = lax.dynamic_index_in_dim(total, place.line, 0, keepdims=False).astype(F32)
    for step in range(1, place.lines):
        sent = lax.dynamic_index_in_dim(
            total, (place.line + step) % place.lines, 0, keepdims=False
        )
        result = result + place.shift_line(sent, step).astype(F32)
    return result


def nt(first, second):
    return lax.dot_general(first, second, (((1,), (1,)), ((), ())), preferred_element_type=F32)


def tn(first, second):
    return lax.dot_general(first, second, (((0,), (0,)), ((), ())), preferred_element_type=F32)


def nn(first, second):
    return lax.dot_general(first, second, (((1,), (0,)), ((), ())), preferred_element_type=F32)


def lanes_of(head, shape):
    lane = lax.broadcasted_iota(jnp.int32, shape, 1)
    return (lane >= head * (shape[1] // 2)) & (lane < (head + 1) * (shape[1] // 2))


def self_forward_body(query_ref, key_ref, value_ref, out_ref, lse_ref, *, scaling, block):
    rows, lanes = query_ref.shape[1:]
    for start in range(0, rows, block):
        seen = start + block
        total = None
        for head in range(2):
            query = query_ref[0, start:seen]
            query = jnp.where(lanes_of(head, query.shape), query * scaling, 0).astype(BF16)
            scores = nt(query, key_ref[0, :seen])
            row = lax.broadcasted_iota(jnp.int32, scores.shape, 0) + start
            column = lax.broadcasted_iota(jnp.int32, scores.shape, 1)
            scores = jnp.where(column <= row, scores, NEGATIVE)
            top = jnp.max(scores, axis=1, keepdims=True)
            weights = jnp.exp(scores - top)
            summed = jnp.sum(weights, axis=1, keepdims=True)
            probability = (weights * (1.0 / summed)).astype(BF16)
            value = value_ref[0, :seen]
            value = jnp.where(lanes_of(head, value.shape), value, 0).astype(BF16)
            part = nn(probability, value)
            total = part if total is None else total + part
            lse_ref[0, head, start:seen] = top + jnp.log(summed)
        out_ref[0, start:seen] = total.astype(BF16)


def self_attention(projected, heads):
    items, rows, triple = projected.shape
    pairs = heads // 2
    lanes = triple // 3 // pairs
    scaling = (triple // 3 // heads) ** (-0.5)
    spec = lambda third: pl.BlockSpec((1, rows, lanes), lambda b, p: (b, 0, third * pairs + p))
    return pl.pallas_call(
        functools.partial(self_forward_body, scaling=scaling, block=128),
        grid=(items, pairs),
        out_shape=[
            jax.ShapeDtypeStruct((items, rows, triple // 3), BF16),
            jax.ShapeDtypeStruct((items, heads, rows, 1), F32),
        ],
        in_specs=[spec(0), spec(1), spec(2)],
        out_specs=[spec(0), pl.BlockSpec((1, 2, rows, 1), lambda b, p: (b, p, 0, 0))],
        cost_estimate=pl.CostEstimate(
            flops=4 * items * rows * rows * triple // 3,
            bytes_accessed=items * rows * triple * 3,
            transcendentals=items * heads * rows * rows,
        ),
        name="self_attention",
    )(projected, projected, projected)


def self_backward_body(
    query_ref, key_ref, value_ref, grad_ref, lse_ref, query_out, key_out, value_out, *, scaling, block
):
    rows, lanes = query_ref.shape[1:]
    key_sum = [None] * (rows // block)
    value_sum = [None] * (rows // block)
    for start in range(0, rows, block):
        seen = start + block
        query_total = None
        for head in range(2):
            query = query_ref[0, start:seen]
            query = jnp.where(lanes_of(head, query.shape), query * scaling, 0).astype(BF16)
            grad = grad_ref[0, start:seen]
            grad = jnp.where(lanes_of(head, grad.shape), grad, 0).astype(BF16)
            key = key_ref[0, :seen]
            key_own = jnp.where(lanes_of(head, key.shape), key * scaling, 0).astype(BF16)
            scores = nt(query, key)
            row = lax.broadcasted_iota(jnp.int32, scores.shape, 0) + start
            column = lax.broadcasted_iota(jnp.int32, scores.shape, 1)
            scores = jnp.where(column <= row, scores, NEGATIVE)
            probability = jnp.exp(scores - lse_ref[0, head, start:seen])
            prob_grad = nt(grad, value_ref[0, :seen])
            weighted = probability * prob_grad
            centre = jnp.sum(weighted, axis=1, keepdims=True)
            score_grad = (weighted - probability * centre).astype(BF16)
            part = nn(score_grad, key_own)
            query_total = part if query_total is None else query_total + part
            key_part = tn(score_grad, query)
            value_part = tn(probability.astype(BF16), grad)
            for at in range(0, seen, block):
                k = at // block
                key_block = key_part[at : at + block]
                value_block = value_part[at : at + block]
                key_sum[k] = key_block if key_sum[k] is None else key_sum[k] + key_block
                value_sum[k] = value_block if value_sum[k] is None else value_sum[k] + value_block
        query_out[0, start:seen] = query_total.astype(BF16)
    for k in range(rows // block):
        key_out[0, k * block : (k + 1) * block] = key_sum[k].astype(BF16)
        value_out[0, k * block : (k + 1) * block] = value_sum[k].astype(BF16)


def self_attention_grads(projected, grad, lse):
    items, rows, triple = projected.shape
    heads = lse.shape[1]
    pairs = heads // 2
    lanes = triple // 3 // pairs
    scaling = (triple // 3 // heads) ** (-0.5)
    spec = lambda third: pl.BlockSpec((1, rows, lanes), lambda b, p: (b, 0, third * pairs + p))
    part = jax.ShapeDtypeStruct((items, rows, triple // 3), BF16)
    return pl.pallas_call(
        functools.partial(self_backward_body, scaling=scaling, block=128),
        grid=(items, pairs),
        out_shape=[part, part, part],
        in_specs=[
            spec(0),
            spec(1),
            spec(2),
            spec(0),
            pl.BlockSpec((1, 2, rows, 1), lambda b, p: (b, p, 0, 0)),
        ],
        out_specs=[spec(0)] * 3,
        cost_estimate=pl.CostEstimate(
            flops=10 * items * rows * rows * triple // 3,
            bytes_accessed=items * rows * triple * 6,
            transcendentals=items * heads * rows * rows,
        ),
        name="self_attention_grads",
    )(projected, projected, projected, grad, lse)


def cross_forward_body(length_ref, query_ref, key_ref, value_ref, out_ref, lse_ref, *, scaling):
    length = length_ref[pl.program_id(0)]
    total = None
    for head in range(2):
        query = query_ref[0]
        query = jnp.where(lanes_of(head, query.shape), query * scaling, 0).astype(BF16)
        scores = nt(query, key_ref[0])
        column = lax.broadcasted_iota(jnp.int32, scores.shape, 1)
        scores = jnp.where(column < length, scores, NEGATIVE)
        top = jnp.max(scores, axis=1, keepdims=True)
        weights = jnp.exp(scores - top)
        summed = jnp.sum(weights, axis=1, keepdims=True)
        probability = (weights * (1.0 / summed)).astype(BF16)
        value = value_ref[0]
        value = jnp.where(lanes_of(head, value.shape), value, 0).astype(BF16)
        part = nn(probability, value)
        total = part if total is None else total + part
        lse_ref[0, head] = top + jnp.log(summed)
    out_ref[0] = total.astype(BF16)


def cross_attention(lengths, query, key_value, heads):
    items, rows, width = query.shape
    text = key_value.shape[1]
    pairs = heads // 2
    lanes = width // pairs
    scaling = (width // heads) ** (-0.5)
    query_spec = pl.BlockSpec((1, rows, lanes), lambda b, p: (b, 0, p))
    return pl.pallas_call(
        functools.partial(cross_forward_body, scaling=scaling),
        grid=(items, pairs),
        out_shape=[
            jax.ShapeDtypeStruct((items, rows, width), BF16),
            jax.ShapeDtypeStruct((items, heads, rows, 1), F32),
        ],
        in_specs=[
            pl.BlockSpec(memory_space=pltpu.SMEM),
            query_spec,
            pl.BlockSpec((1, text, lanes), lambda b, p: (b, 0, p)),
            pl.BlockSpec((1, text, lanes), lambda b, p: (b, 0, pairs + p)),
        ],
        out_specs=[query_spec, pl.BlockSpec((1, 2, rows, 1), lambda b, p: (b, p, 0, 0))],
        cost_estimate=pl.CostEstimate(
            flops=4 * items * rows * text * width,
            bytes_accessed=items * rows * width * 6,
            transcendentals=items * heads * rows * text,
        ),
        name="cross_attention",
    )(lengths, query, key_value, key_value)


def cross_backward_body(
    length_ref, query_ref, key_ref, value_ref, grad_ref, lse_ref, query_out, key_out, value_out, *, scaling
):
    length = length_ref[pl.program_id(0)]
    query_total = key_total = value_total = None
    for head in range(2):
        query = query_ref[0]
        query = jnp.where(lanes_of(head, query.shape), query * scaling, 0).astype(BF16)
        grad = grad_ref[0]
        grad = jnp.where(lanes_of(head, grad.shape), grad, 0).astype(BF16)
        key = key_ref[0]
        key_own = jnp.where(lanes_of(head, key.shape), key * scaling, 0).astype(BF16)
        scores = nt(query, key)
        column = lax.broadcasted_iota(jnp.int32, scores.shape, 1)
        scores = jnp.where(column < length, scores, NEGATIVE)
        probability = jnp.exp(scores - lse_ref[0, head])
        prob_grad = nt(grad, value_ref[0])
        weighted = probability * prob_grad
        centre = jnp.sum(weighted, axis=1, keepdims=True)
        score_grad = (weighted - probability * centre).astype(BF16)
        parts = (
            nn(score_grad, key_own),
            tn(score_grad, query),
            tn(probability.astype(BF16), grad),
        )
        if head == 0:
            query_total, key_total, value_total = parts
        else:
            query_total, key_total, value_total = (
                query_total + parts[0],
                key_total + parts[1],
                value_total + parts[2],
            )
    query_out[0] = query_total.astype(BF16)
    key_out[0] = key_total.astype(BF16)
    value_out[0] = value_total.astype(BF16)


def cross_attention_grads(lengths, query, key_value, grad, lse):
    items, rows, width = query.shape
    text = key_value.shape[1]
    heads = lse.shape[1]
    pairs = heads // 2
    lanes = width // pairs
    scaling = (width // heads) ** (-0.5)
    query_spec = pl.BlockSpec((1, rows, lanes), lambda b, p: (b, 0, p))
    text_spec = pl.BlockSpec((1, text, lanes), lambda b, p: (b, 0, p))
    return pl.pallas_call(
        functools.partial(cross_backward_body, scaling=scaling),
        grid=(items, pairs),
        out_shape=[
            jax.ShapeDtypeStruct((items, rows, width), BF16),
            jax.ShapeDtypeStruct((items, text, width), BF16),
            jax.ShapeDtypeStruct((items, text, width), BF16),
        ],
        in_specs=[
            pl.BlockSpec(memory_space=pltpu.SMEM),
            query_spec,
            text_spec,
            pl.BlockSpec((1, text, lanes), lambda b, p: (b, 0, pairs + p)),
            query_spec,
            pl.BlockSpec((1, 2, rows, 1), lambda b, p: (b, p, 0, 0)),
        ],
        out_specs=[query_spec, text_spec, text_spec],
        cost_estimate=pl.CostEstimate(
            flops=10 * items * rows * text * width,
            bytes_accessed=items * rows * width * 10,
            transcendentals=items * heads * rows * text,
        ),
        name="cross_attention_grads",
    )(lengths, query, key_value, key_value, grad, lse)


def norm_forward(values, gain, bias):
    center = values - jnp.mean(values, axis=-1, keepdims=True)
    inverse = lax.rsqrt(jnp.mean(center * center, axis=-1, keepdims=True) + EPSILON)
    scaled = center * inverse
    normed = (scaled * gain.astype(F32) + bias.astype(F32)).astype(BF16)
    return normed, scaled, inverse


def norm_backward(upstream, scaled, inverse, gain):
    gain_grad = jnp.sum(upstream * scaled, axis=0)
    bias_grad = jnp.sum(upstream, axis=0)
    weighted = upstream * gain.astype(F32)
    input_grad = inverse * (
        weighted
        - jnp.mean(weighted, axis=-1, keepdims=True)
        - scaled * jnp.mean(weighted * scaled, axis=-1, keepdims=True)
    )
    return input_grad, gain_grad, bias_grad


def product(first, second):
    return jnp.dot(first, second, preferred_element_type=F32)


def weight_grad(inputs, grads):
    return jnp.einsum("sa,sb->ab", inputs, grads, preferred_element_type=F32).astype(BF16)


def input_grad_of(grads, weight):
    return jnp.einsum("sb,ab->sa", grads, weight, preferred_element_type=F32)


def gelu_parts(values):
    return jax.nn.gelu(values, approximate=True)


def per_device(
    tokens,
    text_states,
    caption_len,
    out_grad,
    norm1_gain,
    norm1_bias,
    qkv_weight,
    self_out,
    norm2_gain,
    norm2_bias,
    cross_query,
    cross_kv,
    cross_out,
    norm3_gain,
    norm3_bias,
    ff_in,
    ff_in_bias,
    ff_out,
    ff_out_bias,
):
    place = Place(lax.axis_size("dp") // 2, lax.axis_size("fsdp"))
    items, rows, width = tokens.shape
    text = text_states.shape[1]
    row_count = items * rows

    small = (
        norm1_gain, norm1_bias, norm2_gain, norm2_bias, norm3_gain, norm3_bias, ff_in_bias, ff_out_bias
    )
    sizes = [vector.shape[0] for vector in small]
    packed = jnp.concatenate(small)
    used = packed.shape[0]
    padded = -(-used // 128) * 128
    packed = jnp.pad(packed, (0, padded - used)).reshape(1, padded)
    spread = gather_small(place, packed)
    vectors, at = [], 0
    for size in sizes:
        vectors.append(spread[..., at : at + size].reshape(-1))
        at += size
    (n1_gain, n1_bias, n2_gain, n2_bias, n3_gain, n3_bias, in_bias, out_bias) = vectors

    ahead, behind = place.bits, place.bits[::-1]

    def whole(shard, order):
        return gather(place, shard, order).reshape(-1, shard.shape[1])

    w_qkv = whole(qkv_weight, ahead)
    w_self_out = whole(self_out, behind)
    w_cross_kv = whole(cross_kv, behind)
    w_cross_query = whole(cross_query, ahead)
    w_cross_out = whole(cross_out, behind)
    w_ff_in = whole(ff_in, ahead)
    w_ff_out = whole(ff_out, behind)

    token_values = tokens.reshape(row_count, width).astype(F32)
    text_rows = text_states.reshape(items * text, width)
    normed1, scaled1, inverse1 = norm_forward(token_values, n1_gain, n1_bias)
    projected = product(normed1, w_qkv).astype(BF16).reshape(items, rows, -1)
    attended1, lse1 = self_attention(projected, HEADS)
    attended1 = attended1.reshape(row_count, width)
    after_self = token_values + product(attended1, w_self_out)
    text_kv = product(text_rows, w_cross_kv).astype(BF16).reshape(items, text, -1)
    normed2, scaled2, inverse2 = norm_forward(after_self, n2_gain, n2_bias)
    query2 = product(normed2, w_cross_query).astype(BF16).reshape(items, rows, width)
    attended2, lse2 = cross_attention(caption_len, query2, text_kv, HEADS)
    attended2 = attended2.reshape(row_count, width)
    after_cross = after_self + product(attended2, w_cross_out)
    normed3, scaled3, inverse3 = norm_forward(after_cross, n3_gain, n3_bias)
    before = product(normed3, w_ff_in) + in_bias.astype(F32)
    middle = gelu_parts(before).astype(BF16)
    result = (after_cross + (product(middle, w_ff_out) + out_bias.astype(F32))).astype(BF16)

    cot = out_grad.reshape(row_count, width)
    cot_values = cot.astype(F32)
    ff_out_bias_grad = jnp.sum(cot_values, axis=0)
    ff_out_grad = scatter(place, weight_grad(middle, cot), behind, BF16)
    middle_grad = input_grad_of(cot, w_ff_out)
    before_grad = jax.vjp(gelu_parts, before)[1](middle_grad)[0].astype(BF16)
    ff_in_bias_grad = jnp.sum(before_grad.astype(F32), axis=0)
    ff_in_grad = scatter(place, weight_grad(normed3, before_grad), ahead, BF16)
    norm_input, n3_gain_grad, n3_bias_grad = norm_backward(
        input_grad_of(before_grad, w_ff_in), scaled3, inverse3, n3_gain
    )
    cross_grad = cot_values + norm_input
    cross_round = cross_grad.astype(BF16)
    cross_out_grad = scatter(place, weight_grad(attended2, cross_round), behind, BF16)
    attended2_grad = input_grad_of(cross_round, w_cross_out).astype(BF16)
    query2_grad, key2_grad, value2_grad = cross_attention_grads(
        caption_len, query2, text_kv, attended2_grad.reshape(items, rows, width), lse2
    )
    query2_grad = query2_grad.reshape(row_count, width)
    text_kv_grad = jnp.concatenate([key2_grad, value2_grad], axis=2).reshape(items * text, -1)
    cross_query_grad = scatter(place, weight_grad(normed2, query2_grad), ahead, BF16)
    cross_kv_grad = scatter(place, weight_grad(text_rows, text_kv_grad), behind, BF16)
    text_grad = input_grad_of(text_kv_grad, w_cross_kv).astype(BF16)
    norm_input, n2_gain_grad, n2_bias_grad = norm_backward(
        input_grad_of(query2_grad, w_cross_query), scaled2, inverse2, n2_gain
    )
    self_grad = cross_grad + norm_input
    self_round = self_grad.astype(BF16)
    self_out_grad = scatter(place, weight_grad(attended1, self_round), ahead, BF16)
    attended1_grad = input_grad_of(self_round, w_self_out).astype(BF16)
    parts = self_attention_grads(projected, attended1_grad.reshape(items, rows, width), lse1)
    projected_grad = jnp.concatenate(parts, axis=2).reshape(row_count, -1)
    qkv_weight_grad = scatter(place, weight_grad(normed1, projected_grad), behind, BF16)
    norm_input, n1_gain_grad, n1_bias_grad = norm_backward(
        input_grad_of(projected_grad, w_qkv), scaled1, inverse1, n1_gain
    )
    tokens_grad = (self_grad + norm_input).astype(BF16)

    small_grads = (
        n1_gain_grad, n1_bias_grad, n2_gain_grad, n2_bias_grad, n3_gain_grad, n3_bias_grad,
        ff_in_bias_grad, ff_out_bias_grad,
    )
    owners = place.lines * 2 * place.planes
    grads = jnp.concatenate([grad.reshape(owners, -1) for grad in small_grads], axis=1)
    grads = jnp.pad(grads, ((0, 0), (0, padded - used)))
    owned = scatter(place, grads, ahead, F32)[0]
    own, at = [], 0
    for size in sizes:
        own.append(owned[at : at + size])
        at += size
    return (
        result.reshape(items, rows, width),
        tokens_grad.reshape(items, rows, width),
        text_grad.reshape(items, text, width),
        own[0],
        own[1],
        qkv_weight_grad,
        self_out_grad,
        own[2],
        own[3],
        cross_query_grad,
        cross_kv_grad,
        cross_out_grad,
        own[4],
        own[5],
        ff_in_grad,
        own[6],
        ff_out_grad,
        own[7],
    )


def solution(mesh):
    whole = P(AXES, None, None)
    matrix = P(AXES, None)
    vector = P(AXES)
    weights = (
        vector, vector, matrix, matrix, vector, vector, matrix, matrix, matrix, vector, vector, matrix,
        vector, matrix, vector,
    )
    return jax.shard_map(
        per_device,
        mesh=mesh,
        in_specs=(whole, whole, vector, whole) + weights,
        out_specs=(whole, whole, whole) + weights,
        check_vma=False,
    )
```

```python
import functools

import jax
import jax.numpy as jnp
from jax import lax
from jax.experimental import pallas as pl
from jax.experimental.pallas import tpu as pltpu
from jax.sharding import PartitionSpec as P

HEADS = 16
EPSILON = 1e-05
NEGATIVE = -1e30
AXES = ("dp", "fsdp")
F32 = jnp.float32
BF16 = jnp.bfloat16
LANES = 128
HBM_BYTES = 8000000
VMEM_MIB = {
    "project_qkv": 14,
    "self_attention": 11,
    "self_out_norm": 10,
    "project_query": 11,
    "cross_out_norm": 11,
    "hidden_layer": 14,
    "last_layer": 20,
    "hidden_grad": 14,
    "norm3_grad": 25,
    "cross_attention_grads": 10,
    "norm2_grad": 17,
    "self_attention_grads": 15,
    "norm1_grad": 20,
    "qkv_grad_other": 11,
    "qkv_grad_own": 17,
    "self_out_grad_own": 10,
    "cross_kv_grad_own": 10,
    "cross_query_grad_own": 10,
    "cross_out_grad_own": 10,
    "ff_in_grad_other": 14,
    "ff_in_grad_own": 22,
    "ff_out_grad_other": 11,
    "ff_out_grad_own": 23,
}


def nt(first, second):
    return lax.dot_general(first, second, (((1,), (1,)), ((), ())), preferred_element_type=F32)


def tn(first, second):
    return lax.dot_general(first, second, (((0,), (0,)), ((), ())), preferred_element_type=F32)


def nn(first, second):
    return lax.dot_general(first, second, (((1,), (0,)), ((), ())), preferred_element_type=F32)


def call(place, body, grid, in_specs, out_specs, out_shape, args, scratch=(), name=None, aliases=None):
    spec = pltpu.PrefetchScalarGridSpec(
        num_scalar_prefetch=1, grid=grid, in_specs=in_specs, out_specs=out_specs,
        scratch_shapes=list(scratch),
    )
    out_shape = jax.tree.map(
        lambda o: pltpu.HBM(o.shape, o.dtype) if o.size * o.dtype.itemsize >= HBM_BYTES else o, out_shape
    )
    out = pl.pallas_call(
        body, grid_spec=spec, out_shape=out_shape, name=name, input_output_aliases=aliases or {},
        cost_estimate=pl.CostEstimate(flops=1, bytes_accessed=1, transcendentals=0),
        compiler_params=pltpu.CompilerParams(vmem_limit_bytes=VMEM_MIB.get(name, 8) * 2**20),
    )(place.scalars, *[in_hbm(arg) for arg in args])
    return place.wait(out)


def in_hbm(value):
    if value.size * value.dtype.itemsize < HBM_BYTES:
        return value
    return pltpu.with_memory_space_constraint(value, pltpu.HBM)


class Place:
    def __init__(self, lines, planes, rows, lengths):
        self.lines = lines
        self.planes = planes
        self.bits = [1 << k for k in range(planes.bit_length() - 1)]
        self.line_bits = [1 << k for k in range(lines.bit_length() - 1)]
        dp = lax.axis_index("dp")
        self.line = dp // 2
        self.core = dp % 2
        self.plane = lax.axis_index("fsdp")
        self.relative = planes * rows % LANES == 0
        self.flip = (self.core if self.relative else jnp.zeros_like(self.core)).astype(jnp.int32)
        self.blocks = 2 * lines if self.relative else 2
        stages = len(self.bits)
        self.masks = [[0], [0]]
        for core in range(2):
            for stage in range(stages):
                bit = self.stage_bit(stage, core)
                self.masks[core] = self.masks[core] + [m ^ bit for m in self.masks[core]]
        masks = jnp.where(self.core == 0, jnp.array(self.masks[0]), jnp.array(self.masks[1]))
        self.plane_slots = (masks ^ self.plane).astype(jnp.int32)
        self.line_slots = ((self.line - jnp.arange(lines)) % lines).astype(jnp.int32)
        self.core_slots = (jnp.arange(2) ^ self.core).astype(jnp.int32)
        parts = [
            self.flip[None], lengths, self.plane_slots, self.line_slots, self.core_slots,
            (self.line ^ jnp.array(self.reversed_lines())).astype(jnp.int32),
        ]
        starts = [0]
        for part in parts:
            starts.append(starts[-1] + part.shape[0])
        _, self.at_length, self.at_plane, self.at_line, self.at_core, self.at_lines, _ = starts
        self.scalars = jnp.concatenate(parts)

    def wait(self, values):
        values, self.scalars = lax.optimization_barrier((values, self.scalars))
        return values

    def reversed_lines(self):
        order = [0]
        for bit in reversed(self.line_bits):
            order = order + [mask ^ bit for mask in order]
        return order

    def stage_bit(self, stage, core):
        return self.bits[(stage + core) % len(self.bits)]

    def _permute(self, value, target):
        pairs = []
        for line in range(self.lines):
            for core in range(2):
                for plane in range(self.planes):
                    l, c, p = target(line, core, plane)
                    pairs.append(
                        ((line * 2 + core) * self.planes + plane, (l * 2 + c) * self.planes + p)
                    )
        return lax.ppermute(value, AXES, pairs)

    def shift_line(self, value, step):
        return self._permute(value, lambda l, c, p: ((l + step) % self.lines, c, p))

    def swap_plane(self, value, stage):
        return self._permute(value, lambda l, c, p: (l, c, p ^ self.stage_bit(stage, c)))

    def swap_line(self, value, bit):
        return self._permute(value, lambda l, c, p: (l ^ bit, c, p))

    def swap_core(self, value):
        return self._permute(value, lambda l, c, p: (l, 1 - c, p))


def interleave(place, pieces, first):
    count = len(pieces)
    outer, rows, width = pieces[0].shape
    tile = width

    def body(slots_ref, *refs):
        out_ref = refs[count]
        for k in range(count):
            out_ref[0, pl.ds(slots_ref[first + k], 1)] = refs[k][...]

    moved = 2 * count * pieces[0].size * pieces[0].dtype.itemsize
    return call(
        place, body,
        (outer, width // tile),
        [pl.BlockSpec((1, rows, tile), lambda a, n, s: (a, 0, n))] * count,
        pl.BlockSpec((1, count, rows, tile), lambda a, n, s: (a, 0, 0, n)),
        jax.ShapeDtypeStruct((outer, count, rows, width), pieces[0].dtype),
        pieces,
        name="interleave",
    )


class Gather:
    def __init__(self, place, shard):
        self.place = place
        self.rows, self.width = shard.shape
        shard = place.wait(shard)
        self.pieces = [shard] + [place.shift_line(shard, s) for s in range(1, place.lines)]
        self.stage = 0

    def wait(self):
        self.pieces = self.place.wait(self.pieces)

    def join_line(self):
        place = self.place
        self.wait()
        held = interleave(place, [piece[None] for piece in self.pieces], place.at_line)
        self.pieces = [held.reshape(place.lines, self.rows, self.width)]
        self.swap()

    def swap(self):
        if self.stage:
            self.wait()
        self.pieces = self.pieces + [
            self.place.swap_plane(piece, self.stage) for piece in self.pieces
        ]
        self.stage += 1

    def join_plane(self):
        place = self.place
        while self.stage < len(place.bits):
            self.swap()
        self.wait()
        half = interleave(place, self.pieces, place.at_plane)
        self.own = half.reshape(place.lines, place.planes * self.rows, self.width)
        self.other = place.swap_core(self.own)

    def weight(self):
        place = self.place
        self.other = place.wait(self.other)
        if place.relative:
            return Weight(place, self.own[:, None], self.other[:, None])
        both = interleave(place, [self.own, self.other], place.at_core)
        return Weight(place, both.reshape(-1, self.width))


class Weight:
    def __init__(self, place, *arrays):
        self.full = len(arrays) == 1
        self.width = arrays[0].shape[-1]
        if self.full:
            arrays = (arrays[0].reshape(place.blocks // 2, 2, -1, self.width),) * 2
        self.arrays = arrays
        self.lines, _, self.rows, _ = arrays[0].shape
        self.half = self.lines * self.rows

    def specs(self, lines, columns, index, **more):
        def make(part):
            def index_map(*args):
                line, column = index(*args[:-1])
                which = args[-1][0] ^ part if self.full else 0
                return line, which, 0, column

            return pl.BlockSpec((lines, 1, self.rows, columns), index_map, **more)

        return [make(0), make(1)]


def rows_of(ref):
    lines, _, rows, columns = ref.shape
    return ref[...].reshape(lines * rows, columns)


def as_columns(place, vectors, rows):
    parts = jnp.concatenate([vector.reshape(-1, rows) for vector in vectors])
    return jnp.pad(parts, ((0, LANES - parts.shape[0]), (0, 0))).T


def as_table(place, sums, rows):
    owners = place.lines * 2 * place.planes
    parts = [
        vector.reshape(owners, -1, rows).transpose(1, 0, 2).reshape(-1, owners * rows)
        for vector in sums
    ]
    table = jnp.concatenate(parts)
    return jnp.pad(table, ((0, LANES - table.shape[0]), (0, 0))).astype(BF16)


def from_columns(place, weight, start, sizes, rows):
    parts = [array[..., start:] for array in weight.arrays]
    if not weight.full:
        swapped = place.core == 1
        parts = [
            jnp.concatenate([
                jnp.where(swapped, parts[1], parts[0]), jnp.where(swapped, parts[0], parts[1])
            ], axis=1)
        ]
    owners = place.lines * 2 * place.planes
    table = parts[0].reshape(owners, rows, LANES).transpose(2, 0, 1).astype(F32)
    vectors, at = [], 0
    for size in sizes:
        each = size // rows
        vectors.append(table[at : at + each].transpose(1, 0, 2).reshape(1, -1))
        at += each
    return vectors


class Scatter:
    def __init__(self, place, kept, sent):
        self.place = place
        self.kept = kept
        self.stages = [
            functools.partial(place.swap_plane, stage=stage)
            for stage in reversed(range(len(place.bits)))
        ] + [functools.partial(place.swap_line, bit=bit) for bit in place.line_bits]
        self.arrived = self.stages.pop(0)(place.wait(sent))

    def next(self):
        self.kept, sent = combine(self.place, self.kept, self.place.wait(self.arrived))
        self.arrived = self.stages.pop(0)(sent)

    def spread(self):
        place = self.place
        while len(self.stages) > len(place.line_bits):
            self.next()
        self.kept, *pieces = combine(place, self.kept, place.wait(self.arrived), apart=True)
        self.arrived = [
            place.swap_line(piece, mask) for piece, mask in zip(pieces, place.reversed_lines()[1:])
        ]
        self.stages = []

    def result(self):
        while self.stages:
            self.next()
        total = self.kept[0].astype(F32)
        for arrival in jax.tree.leaves(self.place.wait(self.arrived)):
            total = total + arrival[0].astype(F32)
        return total


def combine(place, kept, arrived, apart=False):
    count, rows, width = kept.shape
    each = 1 if apart else count // 2
    outs = count // each
    steps = 2 if kept.size > 2**18 and width % 256 == 0 else 1
    tile = width // steps

    def body(_, kept_ref, arrived_ref, *refs):
        total = (kept_ref[...].astype(F32) + arrived_ref[...].astype(F32)).astype(BF16)
        for k in range(outs):
            refs[k][...] = total[k * each : (k + 1) * each]

    def block(size):
        return pl.BlockSpec((size, rows, tile), lambda n, s: (0, 0, n))

    out = jax.ShapeDtypeStruct((each, rows, width), BF16)
    return call(
        place, body, (steps,), [block(count), block(count)], [block(each)] * outs, [out] * outs,
        (kept, arrived), name="combine",
    )


def relative_block(index, flip, blocks):
    return (index % 2 ^ flip) * (blocks // 2) + index // 2


def natural_block(index, flip, blocks):
    half = blocks // 2
    return index % half * 2 + (index // half ^ flip)


def block_slice(index, size):
    return pl.ds(pl.multiple_of(index * size, size), size)


def store_relative(ref, values, flip, blocks):
    size = values.shape[1] // blocks
    for k in range(blocks):
        at = relative_block(k, flip, blocks) if blocks > 2 else k
        ref[:, block_slice(at, size)] = values[:, k * size : (k + 1) * size].astype(ref.dtype)


def normalized(values):
    center = values - jnp.mean(values, axis=1, keepdims=True)
    inverse = lax.rsqrt(jnp.mean(center * center, axis=1, keepdims=True) + EPSILON)
    return center * inverse, inverse


def norm(place, values, gain, bias):
    count, width = values.shape
    block = 256
    blocks = place.blocks

    def body(flip_ref, values_ref, gain_ref, bias_ref, out_ref):
        hat, _ = normalized(values_ref[...].astype(F32))
        store_relative(out_ref, hat * gain_ref[...] + bias_ref[...], flip_ref[0], blocks)

    row = pl.BlockSpec((block, width), lambda m, s: (m, 0))
    vector = pl.BlockSpec((1, width), lambda m, s: (0, 0))
    return call(
        place, body, (count // block,), [row, vector, vector], row,
        jax.ShapeDtypeStruct((count, width), BF16), (values, gain, bias),
        name="norm",
    )


def relabel(place, values):
    count, width = values.shape
    blocks = place.blocks
    if blocks == 2:
        return values
    size = width // blocks

    def body(_, values_ref, out_ref):
        out_ref[...] = values_ref[...]

    return call(
        place, body, (blocks,),
        [pl.BlockSpec((count, size), lambda k, s: (0, k))],
        pl.BlockSpec((count, size), lambda k, s: (0, relative_block(k, s[0], blocks))),
        jax.ShapeDtypeStruct((count, width), values.dtype), (values,),
        name="relabel",
    )


def project(place, inputs, weight, start, width, tile=1024, name="project"):
    count, depth = inputs.shape
    half = depth // 2

    def body(_, inputs_ref, own_ref, other_ref, out_ref):
        total = nn(inputs_ref[:, :half], rows_of(own_ref)) + nn(inputs_ref[:, half:], rows_of(other_ref))
        out_ref[...] = total.astype(BF16)

    return call(
        place, body, (width // tile,),
        [pl.BlockSpec((count, depth), lambda n, s: (0, 0))]
        + weight.specs(weight.lines, tile, lambda n: (0, start // tile + n)),
        pl.BlockSpec((count, tile), lambda n, s: (0, n)),
        jax.ShapeDtypeStruct((count, width), BF16), (inputs, *weight.arrays),
        name=name,
    )


def project_norm(place, inputs, weight, start, base, gain, bias, name):
    count, depth = inputs.shape
    half = depth // 2
    width = base.shape[1]
    block = 256
    blocks = place.blocks

    def body(flip_ref, inputs_ref, own_ref, other_ref, base_ref, gain_ref, bias_ref, after_ref, out_ref):
        total = nn(inputs_ref[:, :half], rows_of(own_ref)) + nn(inputs_ref[:, half:], rows_of(other_ref))
        total = total + base_ref[...].astype(F32)
        after_ref[...] = total
        hat, _ = normalized(total)
        store_relative(out_ref, hat * gain_ref[...] + bias_ref[...], flip_ref[0], blocks)

    row = pl.BlockSpec((block, width), lambda m, s: (m, 0))
    vector = pl.BlockSpec((1, width), lambda m, s: (0, 0))
    return call(
        place, body, (count // block,),
        [pl.BlockSpec((block, depth), lambda m, s: (m, 0))]
        + weight.specs(weight.lines, width, lambda m: (0, start // width))
        + [row, vector, vector],
        [row, row],
        [jax.ShapeDtypeStruct((count, width), F32), jax.ShapeDtypeStruct((count, width), BF16)],
        (inputs, *weight.arrays, base, gain, bias),
        name=name,
    )


def hidden_layer(place, inputs, weight, bias):
    count, depth = inputs.shape
    half = depth // 2
    width = weight.width
    size = width // place.blocks

    def body(flip_ref, inputs_ref, own_ref, other_ref, bias_ref, middle_own, middle_other, slope_ref):
        scale = 0.7978845608028654
        for k, middle_ref in enumerate((middle_own, middle_other)):
            at = block_slice(k ^ flip_ref[0], size)
            upper = own_ref[:, 0, :, at].reshape(half, size)
            lower = other_ref[:, 0, :, at].reshape(half, size)
            before = nn(inputs_ref[:, :half], upper) + nn(inputs_ref[:, half:], lower)
            before = before + bias_ref[:, at]
            square = before * before
            half_sum = 0.5 + 0.5 * jnp.tanh(before * (scale + scale * 0.044715 * square))
            middle = before * half_sum
            middle_ref[...] = middle.astype(BF16)
            slope = half_sum + middle * (1.0 - half_sum) * (2.0 * scale + 6.0 * scale * 0.044715 * square)
            slope_ref[:, at] = slope.astype(BF16)

    column = pl.BlockSpec((count, size), lambda n, s: (0, n))
    return call(
        place, body, (place.blocks // 2,),
        [pl.BlockSpec((count, depth), lambda n, s: (0, 0))]
        + weight.specs(weight.lines, 2 * size, lambda n: (0, n))
        + [pl.BlockSpec((1, 2 * size), lambda n, s: (0, n))],
        [column, column, pl.BlockSpec((count, 2 * size), lambda n, s: (0, n))],
        [jax.ShapeDtypeStruct((count, width // 2), BF16)] * 2 + [jax.ShapeDtypeStruct((count, width), BF16)],
        (inputs, *weight.arrays, bias),
        name="hidden_layer",
    )


def last_layer(place, inputs, weight, bias, base):
    count, half = inputs[0].shape
    width = base.shape[1]
    steps = 4 if place.relative else 1
    size = half // steps

    def body(_, inputs_own, inputs_other, own_ref, other_ref, bias_ref, base_ref, out_ref, total_ref):
        step = pl.program_id(0)
        part = nn(inputs_own[...], rows_of(own_ref)) + nn(inputs_other[...], rows_of(other_ref))

        @pl.when(step == 0)
        def _():
            total_ref[...] = part

        @pl.when((step > 0) & (step < steps - 1))
        def _():
            total_ref[...] += part

        @pl.when(step == steps - 1)
        def _():
            total = total_ref[...] + part if steps > 1 else part
            out_ref[...] = (base_ref[...] + (total + bias_ref[...])).astype(BF16)

    column = pl.BlockSpec((count, size), lambda n, s: (0, n))
    rest = pl.BlockSpec((count, width), lambda n, s: (0, 0))
    return call(
        place, body, (steps,),
        [column, column]
        + weight.specs(weight.lines // steps, width, lambda n: (n, 0))
        + [pl.BlockSpec((1, width), lambda n, s: (0, 0)), rest],
        rest, jax.ShapeDtypeStruct((count, width), BF16), (*inputs, *weight.arrays, bias, base),
        scratch=[pltpu.VMEM((count, width), F32)],
        name="last_layer",
    )


def hidden_grad(place, grads, weight, slope):
    count, width = grads.shape
    hidden = slope.shape[1]
    pairs = place.blocks // 2
    size = hidden // place.blocks

    def body(flip_ref, grads_ref, own_ref, other_ref, slope_ref, out_ref, sum_ref):
        for k, weight_ref in enumerate((own_ref, other_ref)):
            at = block_slice(k ^ flip_ref[0], size)
            value = (nt(grads_ref[...], rows_of(weight_ref)) * slope_ref[:, at].astype(F32)).astype(BF16)
            out_ref[:, at] = value
            sum_ref[:, at] = jnp.sum(value.astype(F32), axis=0, keepdims=True)

    column = pl.BlockSpec((count, 2 * size), lambda n, s: (0, n))
    return call(
        place, body, (pairs,),
        [pl.BlockSpec((count, width), lambda n, s: (0, 0))]
        + weight.specs(1, width, lambda n: (n, 0))
        + [column],
        [column, pl.BlockSpec((1, 2 * size), lambda n, s: (0, n))],
        [jax.ShapeDtypeStruct((count, hidden), BF16), jax.ShapeDtypeStruct((1, hidden), F32)],
        (grads, *weight.arrays, slope),
        name="hidden_grad",
    )


def back_project(place, grads, weight, start, name):
    count, width = grads.shape
    half = weight.half
    block = 256

    def body(_, grads_ref, own_ref, other_ref, out_ref):
        out_ref[:, :half] = nt(grads_ref[...], rows_of(own_ref)).astype(BF16)
        out_ref[:, half:] = nt(grads_ref[...], rows_of(other_ref)).astype(BF16)

    return call(
        place, body, (count // block,),
        [pl.BlockSpec((block, width), lambda m, s: (m, 0))]
        + weight.specs(weight.lines, width, lambda m: (0, start // width)),
        pl.BlockSpec((block, 2 * half), lambda m, s: (m, 0)),
        jax.ShapeDtypeStruct((count, 2 * half), BF16), (grads, *weight.arrays),
        name=name,
    )


def back_project_natural(place, grads, weight, start, name):
    count, width = grads.shape
    half = weight.half
    block = 256
    blocks = place.blocks
    size = 2 * half // blocks

    def body(flip_ref, grads_ref, own_ref, other_ref, out_ref):
        for k, weight_ref in enumerate((own_ref, other_ref)):
            total = nt(grads_ref[...], rows_of(weight_ref)).astype(BF16)
            for b in range(blocks // 2):
                at = natural_block(k * (blocks // 2) + b, flip_ref[0], blocks) if blocks > 2 else k
                out_ref[:, block_slice(at, size)] = total[:, b * size : (b + 1) * size]

    return call(
        place, body, (count // block,),
        [pl.BlockSpec((block, width), lambda m, s: (m, 0))]
        + weight.specs(weight.lines, width, lambda m: (0, start // width)),
        pl.BlockSpec((block, 2 * half), lambda m, s: (m, 0)),
        jax.ShapeDtypeStruct((count, 2 * half), BF16), (grads, *weight.arrays),
        name=name,
    )


def back_project_norm(place, grads, weight, start, values, gain, base, kinds, name):
    count, width = grads.shape
    half = weight.half
    features = 2 * half
    block = 256
    blocks = place.blocks
    size = features // blocks

    def body(flip_ref, grads_ref, own_ref, other_ref, values_ref, gain_ref, base_ref, *refs):
        outs, sums_ref, upstream_ref = refs[: len(kinds)], refs[len(kinds)], refs[len(kinds) + 1]
        for k, weight_ref in enumerate((own_ref, other_ref)):
            total = nt(grads_ref[...], rows_of(weight_ref))
            for b in range(blocks // 2):
                at = natural_block(k * (blocks // 2) + b, flip_ref[0], blocks) if blocks > 2 else k
                upstream_ref[:, block_slice(at, size)] = total[:, b * size : (b + 1) * size]
        upstream = upstream_ref[...]
        hat, inverse = normalized(values_ref[...].astype(F32))
        weighted = upstream * gain_ref[...]
        base_values = base_ref[...].astype(F32)
        grad = base_values + inverse * (
            weighted
            - jnp.mean(weighted, axis=1, keepdims=True)
            - hat * jnp.mean(weighted * hat, axis=1, keepdims=True)
        )
        for out in outs:
            out[...] = grad.astype(out.dtype)

        @pl.when(pl.program_id(0) == 0)
        def _():
            sums_ref[...] = jnp.zeros_like(sums_ref)

        sums_ref[0:1] += jnp.sum(upstream * hat, axis=0, keepdims=True)
        sums_ref[1:2] += jnp.sum(upstream, axis=0, keepdims=True)
        sums_ref[2:3] += jnp.sum(base_values, axis=0, keepdims=True)

    row = pl.BlockSpec((block, features), lambda m, s: (m, 0))
    sums = pl.BlockSpec((8, features), lambda m, s: (0, 0))
    return call(
        place, body, (count // block,),
        [pl.BlockSpec((block, width), lambda m, s: (m, 0))]
        + weight.specs(
            weight.lines, width, lambda m: (0, start // width), pipeline_mode=pl.Buffered(1)
        )
        + [row, pl.BlockSpec((1, features), lambda m, s: (0, 0)), row],
        [row] * len(kinds) + [sums],
        [jax.ShapeDtypeStruct((count, features), kind) for kind in kinds]
        + [jax.ShapeDtypeStruct((8, features), F32)],
        (grads, *weight.arrays, values, gain, base),
        scratch=[pltpu.VMEM((block, features), F32)],
        name=name,
    )


def part_of(inputs, part):
    if isinstance(inputs, tuple):
        return inputs[part], 0, inputs[part].shape[1]
    return inputs, part, inputs.shape[1] // 2


def weight_part(place, inputs, grads, part, name, total=None, start=0, into=None):
    inputs, part, depth = part_of(inputs, part)
    count, width = grads.shape
    rows = min(1024, depth)
    tile = width if width <= 1024 else width // 2
    steps = depth // rows

    def body(_, inputs_ref, grads_ref, *refs):
        refs[-1][...] = tn(inputs_ref[...], grads_ref[...]).astype(BF16)

    return call(
        place, body, (steps, width // tile),
        [
            pl.BlockSpec((count, rows), lambda k, n, s: (0, part * steps + k)),
            pl.BlockSpec((count, tile), lambda k, n, s: (0, n)),
        ]
        + [pl.BlockSpec(memory_space=pl.ANY)] * (into is not None),
        pl.BlockSpec((rows, tile), lambda k, n, s: (k, start // tile + n)),
        jax.ShapeDtypeStruct((depth, total or width), BF16),
        (inputs, grads) + ((into,) if into is not None else ()),
        name=name, aliases={3: 0} if into is not None else {},
    )


def weight_sums(place, inputs, grads, arrived, name, total=None, start=0, into=None):
    inputs, _, depth = part_of(inputs, 0)
    count, width = grads.shape
    planes, lines = place.planes, place.lines
    each = depth // (lines * planes)
    tile = width if width * depth <= 2**19 else width // 2
    first, arrived = arrived
    pieces = planes // 2 * lines

    def body(slots_ref, inputs_ref, grads_ref, arrived_ref, *refs):
        kept_ref, sent_ref, total_ref = refs[-3:]
        total_ref[...] = tn(inputs_ref[...], grads_ref[...]) + arrived_ref[...].astype(F32)
        for k in range(planes):
            out_ref = kept_ref if k < planes // 2 else sent_ref
            for n in range(lines):
                line = slots_ref[place.at_lines + n]
                here = pl.multiple_of((line * planes + slots_ref[place.at_plane + k]) * each, each)
                out_ref[k % (planes // 2) * lines + n] = total_ref[pl.ds(here, each)].astype(BF16)

    block = pl.BlockSpec((pieces, each, tile), lambda n, s: (0, 0, start // tile + n))
    out = jax.ShapeDtypeStruct((pieces, each, total or width), BF16)
    return call(
        place, body, (width // tile,),
        [
            pl.BlockSpec((count, depth), lambda n, s: (0, 0)),
            pl.BlockSpec((count, tile), lambda n, s: (0, n)),
            pl.BlockSpec((depth, tile), lambda n, s: (0, first // tile + n)),
        ]
        + [pl.BlockSpec(memory_space=pl.ANY)] * (2 if into is not None else 0),
        [block, block], [out, out], (inputs, grads, arrived) + (tuple(into) if into is not None else ()),
        scratch=[pltpu.VMEM((depth, tile), F32)],
        name=name, aliases={4: 0, 5: 1} if into is not None else {},
    )


class WeightGrad:
    def __init__(self, place, inputs, grads, names):
        if not isinstance(inputs, list):
            inputs, grads, names = [inputs], [grads], [names]
        self.place = place
        self.inputs, self.grads, self.names = inputs, grads, names
        self.starts = [sum(grad.shape[1] for grad in grads[:k]) for k in range(len(grads))]
        total = sum(grad.shape[1] for grad in grads)
        sides = []
        for part in (1,) if place.relative else (1, 0):
            into = None
            for k, name in enumerate(names):
                into = weight_part(
                    place, inputs[k], grads[k], part, name + ("_own", "_other")[part], total,
                    self.starts[k], into,
                )
            sides.append(into)
        first = sides[0]
        if not place.relative:
            each = first.shape[0] // place.lines
            both = jnp.concatenate(sides[::-1]).reshape(place.lines, 2, each, -1)
            self.own = lax.dynamic_index_in_dim(both, place.core, 1, keepdims=False)
            first = lax.dynamic_index_in_dim(both, 1 - place.core, 1, keepdims=False)
            first = first.reshape(-1, total)
        self.arrived = place.swap_core(first)

    def sums(self, more=None):
        place = self.place
        parts = [self] if more is None else [self, more]
        arrived = [place.wait(part.arrived) for part in parts]
        total = sum(value.shape[1] for value in arrived)
        if place.relative:
            into, before = None, 0
            for part, value in zip(parts, arrived):
                for k, name in enumerate(part.names):
                    into = weight_sums(
                        place, part.inputs[k], part.grads[k], (part.starts[k], value), name + "_own",
                        total, before + part.starts[k], into,
                    )
                before += value.shape[1]
            return into
        own = jnp.concatenate([part.own for part in parts], axis=2)
        sums = own.astype(F32) + jnp.concatenate(arrived, axis=1).astype(F32).reshape(own.shape)
        sums = sums.astype(BF16).reshape(place.lines, place.planes, -1, total)
        sums = sums.transpose(1, 0, 2, 3)[place.plane_slots]
        sums = sums[:, place.line ^ jnp.array(place.reversed_lines())]
        return jnp.split(sums.reshape(place.planes * place.lines, -1, total), 2)


def own_lanes(head, values, scaling=None):
    lane = lax.broadcasted_iota(jnp.int32, values.shape, 1)
    size = values.shape[1] // 2
    scaled = values if scaling is None else values * scaling
    return jnp.where((lane >= head * size) & (lane < (head + 1) * size), scaled, 0).astype(BF16)


def softmax(scores):
    weights = jnp.exp(scores - jnp.max(scores, axis=1, keepdims=True))
    return weights * (1.0 / jnp.sum(weights, axis=1, keepdims=True))


def relative_lanes(place, width):
    per = width // place.blocks // LANES

    def column(p, flip):
        return relative_block(p // per, flip, place.blocks) * per + p % per

    return column


def lane_block(k):
    return slice(k * LANES, (k + 1) * LANES)


def attention(place, query, key_value, starts, items, per, masked, name):
    count = query.shape[0]
    rows, keys = count // items, key_value.shape[0] // items
    pairs = HEADS // 2
    width = pairs * LANES
    scaling = (width // HEADS) ** (-0.5)
    column = relative_lanes(place, width)

    def body(scalars_ref, query_ref, key_ref, value_ref, out_ref, prob_ref):
        for k in range(per):
            total = 0.0
            for head in range(2):
                scores = nt(own_lanes(head, query_ref[:, lane_block(k)], scaling), key_ref[:, lane_block(k)])
                weights = softmax(masked(scores, scalars_ref, pl.program_id(0))).astype(BF16)
                prob_ref[0, 2 * k + head] = weights
                total = total + nn(weights, own_lanes(head, value_ref[:, lane_block(k)]))
            at = column(pl.program_id(1) * per + k, scalars_ref[0])
            out_ref[:, block_slice(at, LANES)] = total.astype(BF16)

    spec = lambda size, start: pl.BlockSpec((size, per * LANES), lambda b, p, s: (b, start // per + p))
    return call(
        place, body, (items, pairs // per),
        [spec(rows, 0), spec(keys, starts[0]), spec(keys, starts[1])],
        [
            pl.BlockSpec((rows, width), lambda b, p, s: (b, 0)),
            pl.BlockSpec((1, 2 * per, rows, keys), lambda b, p, s: (b, p, 0, 0)),
        ],
        [
            jax.ShapeDtypeStruct((count, width), BF16),
            jax.ShapeDtypeStruct((items, HEADS, rows, keys), BF16),
        ],
        (query, key_value, key_value),
        name=name,
    )


def attention_grads(place, query, key_value, starts, probability, grad, out_widths, items, per, name):
    count = query.shape[0]
    rows, keys = count // items, key_value.shape[0] // items
    pairs = HEADS // 2
    width = pairs * LANES
    scaling = (width // HEADS) ** (-0.5)
    column = relative_lanes(place, width)
    alone = len(out_widths) == 1

    def body(scalars_ref, query_ref, key_ref, value_ref, prob_ref, grad_ref, *outs):
        for k in range(per):
            pair = pl.program_id(1) * per + k
            at = block_slice(column(pair, scalars_ref[0]), LANES)
            query_total = key_total = value_total = 0.0
            for head in range(2):
                weights = prob_ref[0, 2 * k + head]
                own_grad = own_lanes(head, grad_ref[:, at])
                prob_grad = nt(own_grad, value_ref[:, lane_block(k)])
                wide = weights.astype(F32)
                weighted = wide * prob_grad
                centre = jnp.sum(weighted, axis=1, keepdims=True)
                score_grad = (weighted - wide * centre).astype(BF16)
                query_total = query_total + nn(
                    score_grad, own_lanes(head, key_ref[:, lane_block(k)], scaling)
                )
                key_total = key_total + tn(
                    score_grad, own_lanes(head, query_ref[:, lane_block(k)], scaling)
                )
                value_total = value_total + tn(weights, own_grad)
            first = pairs if alone else 0
            outs[0][:, block_slice(pair, LANES)] = query_total.astype(BF16)
            outs[-1][:, block_slice(first + pair, LANES)] = key_total.astype(BF16)
            outs[-1][:, block_slice(first + pairs + pair, LANES)] = value_total.astype(BF16)

    spec = lambda size, start: pl.BlockSpec((size, per * LANES), lambda b, p, s: (b, start // per + p))
    heights = [rows] if alone else [rows, keys]
    return call(
        place, body, (items, pairs // per),
        [
            spec(rows, 0), spec(keys, starts[0]), spec(keys, starts[1]),
            pl.BlockSpec((1, 2 * per, rows, keys), lambda b, p, s: (b, p, 0, 0)),
            pl.BlockSpec((rows, width), lambda b, p, s: (b, 0)),
        ],
        [
            pl.BlockSpec((height, wide), lambda b, p, s: (b, 0))
            for height, wide in zip(heights, out_widths)
        ],
        [
            jax.ShapeDtypeStruct((items * height, wide), BF16)
            for height, wide in zip(heights, out_widths)
        ],
        (query, key_value, key_value, probability, grad),
        name=name,
    )


def causal(scores, scalars_ref, item):
    row = lax.broadcasted_iota(jnp.int32, scores.shape, 0)
    column = lax.broadcasted_iota(jnp.int32, scores.shape, 1)
    return jnp.where(column <= row, scores, NEGATIVE)


def visible(first_length):
    def masked(scores, scalars_ref, item):
        column = lax.broadcasted_iota(jnp.int32, scores.shape, 1)
        return jnp.where(column < scalars_ref[first_length + item], scores, NEGATIVE)

    return masked


def per_device(
    tokens,
    text_states,
    caption_len,
    out_grad,
    norm1_gain,
    norm1_bias,
    qkv_weight,
    self_out,
    norm2_gain,
    norm2_bias,
    cross_query,
    cross_kv,
    cross_out,
    norm3_gain,
    norm3_bias,
    ff_in,
    ff_in_bias,
    ff_out,
    ff_out_bias,
):
    place = Place(lax.axis_size("dp") // 2, lax.axis_size("fsdp"), qkv_weight.shape[0], caption_len)
    items, rows, width = tokens.shape
    text = text_states.shape[1]
    count = items * rows
    values0 = tokens.reshape(count, width)
    text_rows = text_states.reshape(items * text, width)
    cot = out_grad.reshape(count, width)

    small = (
        norm1_gain, norm1_bias, norm2_gain, norm2_bias, norm3_gain, norm3_bias, ff_in_bias, ff_out_bias
    )
    sizes = [vector.shape[0] for vector in small]
    middle_group = jnp.concatenate([cross_kv, cross_query, cross_out, self_out], axis=1)
    at_kv, at_query, at_cross, at_self = 0, 2 * width, 3 * width, 4 * width

    shard_rows = qkv_weight.shape[0]
    mid_group = Gather(place, middle_group)
    full_qkv = lax.all_gather(
        jnp.concatenate([qkv_weight, as_columns(place, small, shard_rows)], axis=1),
        AXES, axis=0, tiled=True,
    )
    mid_group.join_line()
    full_in = lax.all_gather(place.wait(ff_in), AXES, axis=0, tiled=True)
    out_group = Gather(place, ff_out)
    text_relative = relabel(place, text_rows)
    mid_group.swap()
    out_group.join_line()
    w_qkv = Weight(place, place.wait(full_qkv))
    (gain1, bias1, gain2, bias2, gain3, bias3, in_bias, out_bias) = from_columns(
        place, w_qkv, 3 * width, sizes, shard_rows
    )
    normed1 = norm(place, values0, gain1, bias1)
    mid_group.join_plane()
    projected = project(place, normed1, w_qkv, 0, 3 * width, name="project_qkv")
    pairs = HEADS // 2
    attended1, probs1 = attention(
        place, projected, projected, (pairs, 2 * pairs), items, 4, causal, "self_attention"
    )
    w_mid = mid_group.weight()
    values1, normed2 = project_norm(
        place, attended1, w_mid, at_self, values0, gain2, bias2, "self_out_norm"
    )
    out_group.swap()
    text_kv = project(place, text_relative, w_mid, at_kv, 2 * width, name="project_text")
    query2 = project(place, normed2, w_mid, at_query, width, name="project_query")
    attended2, probs2 = attention(
        place, query2, text_kv, (0, pairs), items, 4, visible(place.at_length), "cross_attention"
    )
    values2, normed3 = project_norm(
        place, attended2, w_mid, at_cross, values1, gain3, bias3, "cross_out_norm"
    )
    w_in = Weight(place, place.wait(full_in))
    *middle, slope = hidden_layer(place, normed3, w_in, in_bias)
    out_group.join_plane()
    ff_out_terms = WeightGrad(place, tuple(middle), cot, "ff_out_grad")
    w_out = out_group.weight()

    before_grad, in_bias_sum = hidden_grad(place, cot, w_out, slope)
    ff_out_own = ff_out_terms.sums()
    ff_in_terms = WeightGrad(place, normed3, before_grad, "ff_in_grad")

    ff_out_sums = Scatter(place, *ff_out_own)
    cross_grad, cross_round, sums3 = back_project_norm(
        place, before_grad, w_in, 0, values2, gain3, cot, (F32, BF16), "norm3_grad"
    )
    ff_in_own = ff_in_terms.sums()
    attended2_grad = back_project(place, cross_round, w_mid, at_cross, "attended2_grad")
    query2_grad, text_kv_grad = attention_grads(
        place, query2, text_kv, (0, pairs), probs2, attended2_grad, (width, 2 * width), items, 4,
        "cross_attention_grads",
    )
    ff_out_sums.next()
    middle_terms = WeightGrad(
        place,
        [text_relative, normed2, attended2],
        [text_kv_grad, query2_grad, cross_round],
        ["cross_kv_grad", "cross_query_grad", "cross_out_grad"],
    )

    ff_in_sums = Scatter(place, *ff_in_own)
    self_grad, self_round, sums2 = back_project_norm(
        place, query2_grad, w_mid, at_query, values1, gain2, cross_grad, (F32, BF16), "norm2_grad"
    )
    middle_own = middle_terms.sums()
    attended1_grad = back_project(place, self_round, w_mid, at_self, "attended1_grad")
    (projected_grad,) = attention_grads(
        place, projected, projected, (pairs, 2 * pairs), probs1, attended1_grad, (3 * width,), items, 2,
        "self_attention_grads",
    )
    ff_out_sums.next()
    ff_in_sums.next()
    last_terms = WeightGrad(
        place, [normed1, attended1], [projected_grad, self_round], ["qkv_grad", "self_out_grad"]
    )

    middle_sums = Scatter(place, *middle_own)
    tokens_grad, sums1 = back_project_norm(
        place, projected_grad, w_qkv, 0, values0, gain1, self_grad, (BF16,), "norm1_grad"
    )
    table = relabel(place, as_table(place, (
        sums1[0], sums1[1], sums2[0], sums2[1], sums3[0], sums3[1], in_bias_sum[0], sums3[2]
    ), shard_rows))
    small_terms = WeightGrad(place, table, jnp.eye(LANES, dtype=BF16), "small_grad")
    ff_out_sums.next()
    last_own = last_terms.sums(small_terms)
    ff_in_sums.next()
    middle_sums.next()

    last_sums = Scatter(place, *last_own)
    text_grad = back_project_natural(place, text_kv_grad, w_mid, at_kv, "text_grad")
    result = last_layer(place, middle, w_out, out_bias, values2)
    ff_in_sums.next()
    ff_out_grad = ff_out_sums.result()
    middle_sums.next()
    last_sums.next()
    last_sums.next()
    middle_sums.next()
    ff_in_grad = ff_in_sums.result()
    last_sums.next()
    middle_grads = middle_sums.result()
    last_grads = last_sums.result()
    small_grads = last_grads[:, 4 * width :].T
    own, at = [], 0
    for size in sizes:
        own.append(small_grads[at : at + size // shard_rows].reshape(-1))
        at += size // shard_rows
    return (
        result.reshape(items, rows, width),
        tokens_grad.reshape(items, rows, width),
        text_grad.reshape(items, text, width),
        own[0],
        own[1],
        last_grads[:, : 3 * width],
        last_grads[:, 3 * width : 4 * width],
        own[2],
        own[3],
        middle_grads[:, at_query : at_query + width],
        middle_grads[:, at_kv : at_kv + 2 * width],
        middle_grads[:, at_cross : at_cross + width],
        own[4],
        own[5],
        ff_in_grad,
        own[6],
        ff_out_grad,
        own[7],
    )


def solution(mesh):
    whole = P(AXES, None, None)
    matrix = P(AXES, None)
    vector = P(AXES)
    weights = (
        vector, vector, matrix, matrix, vector, vector, matrix, matrix, matrix, vector, vector, matrix,
        vector, matrix, vector,
    )
    return jax.shard_map(
        per_device,
        mesh=mesh,
        in_specs=(whole, whole, vector, whole) + weights,
        out_specs=(whole, whole, whole) + weights,
        check_vma=False,
    )
```

```python
import functools

import jax
import jax.numpy as jnp
from jax import lax
from jax.experimental import pallas as pl
from jax.experimental.pallas import tpu as pltpu
from jax.sharding import PartitionSpec as P

HEADS = 16
EPSILON = 1e-05
NEGATIVE = -1e30
AXES = ("dp", "fsdp")
F32 = jnp.float32
BF16 = jnp.bfloat16
LANES = 128
HBM_BYTES = 6400000
VMEM_MIB = {
    "project_qkv": 14,
    "self_attention": 11,
    "self_out_norm": 10,
    "project_query": 11,
    "cross_out_norm": 11,
    "hidden_layer": 14,
    "last_layer": 20,
    "hidden_grad": 14,
    "norm3_grad": 25,
    "cross_attention_grads": 10,
    "norm2_grad": 17,
    "self_attention_grads": 22,
    "norm1_grad": 20,
    "qkv_grad_other": 11,
    "qkv_grad_own": 17,
    "self_out_grad_own": 10,
    "cross_kv_grad_own": 10,
    "cross_query_grad_own": 10,
    "cross_out_grad_own": 10,
    "ff_in_grad_other": 14,
    "ff_in_grad_own": 22,
    "ff_out_grad_other": 11,
    "ff_out_grad_own": 23,
}


def nt(first, second):
    return lax.dot_general(first, second, (((1,), (1,)), ((), ())), preferred_element_type=F32)


def tn(first, second):
    return lax.dot_general(first, second, (((0,), (0,)), ((), ())), preferred_element_type=F32)


def nn(first, second):
    return lax.dot_general(first, second, (((1,), (0,)), ((), ())), preferred_element_type=F32)


def call(place, body, grid, in_specs, out_specs, out_shape, args, scratch=(), name=None, aliases=None):
    spec = pltpu.PrefetchScalarGridSpec(
        num_scalar_prefetch=1, grid=grid, in_specs=in_specs, out_specs=out_specs,
        scratch_shapes=list(scratch),
    )
    out_shape = jax.tree.map(
        lambda o: pltpu.HBM(o.shape, o.dtype) if is_large(o) else o, out_shape
    )
    out = pl.pallas_call(
        body, grid_spec=spec, out_shape=out_shape, name=name, input_output_aliases=aliases or {},
        cost_estimate=pl.CostEstimate(flops=1, bytes_accessed=1, transcendentals=0),
        compiler_params=pltpu.CompilerParams(vmem_limit_bytes=(VMEM_MIB.get(name, 8) if place.relative else 48) * 2**20),
    )(place.scalars, *[in_hbm(arg) for arg in args])
    return place.wait(out)


def is_large(value):
    return isinstance(value, (jax.Array, jax.ShapeDtypeStruct)) and (
        value.size * value.dtype.itemsize >= HBM_BYTES
    )


def pinned(value):
    return pltpu.with_memory_space_constraint(value, pltpu.HBM)


def in_hbm(value):
    if not is_large(value):
        return value
    return pinned(value)


class Place:
    def __init__(self, lines, planes, rows, lengths):
        self.lines = lines
        self.planes = planes
        self.bits = [1 << k for k in range(planes.bit_length() - 1)]
        self.line_bits = [1 << k for k in range(lines.bit_length() - 1)]
        dp = lax.axis_index("dp")
        self.line = dp // 2
        self.core = dp % 2
        self.plane = lax.axis_index("fsdp")
        self.relative = planes * rows % LANES == 0
        self.flip = (self.core if self.relative else jnp.zeros_like(self.core)).astype(jnp.int32)
        self.blocks = 2 * lines if self.relative else 2
        stages = len(self.bits)
        self.masks = [[0], [0]]
        for core in range(2):
            for stage in range(stages):
                bit = self.stage_bit(stage, core)
                self.masks[core] = self.masks[core] + [m ^ bit for m in self.masks[core]]
        masks = jnp.where(self.core == 0, jnp.array(self.masks[0]), jnp.array(self.masks[1]))
        self.plane_slots = (masks ^ self.plane).astype(jnp.int32)
        self.line_slots = ((self.line - jnp.arange(lines)) % lines).astype(jnp.int32)
        self.core_slots = (jnp.arange(2) ^ self.core).astype(jnp.int32)
        parts = [
            self.flip[None], lengths, self.plane_slots, self.line_slots, self.core_slots,
            (self.line ^ jnp.array(self.reversed_lines())).astype(jnp.int32),
        ]
        starts = [0]
        for part in parts:
            starts.append(starts[-1] + part.shape[0])
        _, self.at_length, self.at_plane, self.at_line, self.at_core, self.at_lines, _ = starts
        self.scalars = jnp.concatenate(parts)

    def wait(self, values):
        values, self.scalars = lax.optimization_barrier((values, self.scalars))
        return values

    def reversed_lines(self):
        order = [0]
        for bit in reversed(self.line_bits):
            order = order + [mask ^ bit for mask in order]
        return order

    def stage_bit(self, stage, core):
        return self.bits[(stage + core) % len(self.bits)]

    def _permute(self, value, target):
        pairs = []
        for line in range(self.lines):
            for core in range(2):
                for plane in range(self.planes):
                    l, c, p = target(line, core, plane)
                    pairs.append(
                        ((line * 2 + core) * self.planes + plane, (l * 2 + c) * self.planes + p)
                    )
        return lax.ppermute(value, AXES, pairs)

    def shift_line(self, value, step):
        return self._permute(value, lambda l, c, p: ((l + step) % self.lines, c, p))

    def swap_plane(self, value, stage):
        return self._permute(value, lambda l, c, p: (l, c, p ^ self.stage_bit(stage, c)))

    def swap_line(self, value, bit):
        return self._permute(value, lambda l, c, p: (l ^ bit, c, p))

    def swap_core(self, value):
        return self._permute(value, lambda l, c, p: (l, 1 - c, p))


def interleave(place, pieces, first):
    count = len(pieces)
    outer, rows, width = pieces[0].shape
    tile = width

    def body(slots_ref, *refs):
        out_ref = refs[count]
        for k in range(count):
            out_ref[0, pl.ds(slots_ref[first + k], 1)] = refs[k][...]

    moved = 2 * count * pieces[0].size * pieces[0].dtype.itemsize
    return call(
        place, body,
        (outer, width // tile),
        [pl.BlockSpec((1, rows, tile), lambda a, n, s: (a, 0, n))] * count,
        pl.BlockSpec((1, count, rows, tile), lambda a, n, s: (a, 0, 0, n)),
        jax.ShapeDtypeStruct((outer, count, rows, width), pieces[0].dtype),
        pieces,
        name="interleave",
    )


class Gather:
    def __init__(self, place, shard):
        self.place = place
        self.rows, self.width = shard.shape
        shard = place.wait(shard)
        self.pieces = [shard] + [place.shift_line(shard, s) for s in range(1, place.lines)]
        self.stage = 0

    def wait(self):
        self.pieces = self.place.wait(self.pieces)

    def join_line(self):
        place = self.place
        self.wait()
        held = interleave(place, [piece[None] for piece in self.pieces], place.at_line)
        self.pieces = [held.reshape(place.lines, self.rows, self.width)]
        self.swap()

    def swap(self):
        if self.stage:
            self.wait()
        self.pieces = self.pieces + [
            self.place.swap_plane(piece, self.stage) for piece in self.pieces
        ]
        self.stage += 1

    def join_plane(self):
        place = self.place
        while self.stage < len(place.bits):
            self.swap()
        self.wait()
        half = interleave(place, self.pieces, place.at_plane)
        self.own = half.reshape(place.lines, place.planes * self.rows, self.width)
        self.other = place.swap_core(self.own)

    def weight(self):
        place = self.place
        self.other = place.wait(self.other)
        if place.relative:
            return Weight(place, self.own[:, None], self.other[:, None])
        both = interleave(place, [self.own, self.other], place.at_core)
        return Weight(place, both.reshape(-1, self.width))


class Weight:
    def __init__(self, place, *arrays):
        self.full = len(arrays) == 1
        self.width = arrays[0].shape[-1]
        if self.full:
            arrays = (arrays[0].reshape(place.blocks // 2, 2, -1, self.width),) * 2
        self.arrays = arrays
        self.lines, _, self.rows, _ = arrays[0].shape
        self.half = self.lines * self.rows

    def specs(self, lines, columns, index, **more):
        def make(part):
            def index_map(*args):
                line, column = index(*args[:-1])
                which = args[-1][0] ^ part if self.full else 0
                return line, which, 0, column

            return pl.BlockSpec((lines, 1, self.rows, columns), index_map, **more)

        return [make(0), make(1)]


def rows_of(ref):
    lines, _, rows, columns = ref.shape
    return ref[...].reshape(lines * rows, columns)


def as_columns(place, vectors, rows):
    parts = jnp.concatenate([vector.reshape(-1, rows) for vector in vectors])
    return jnp.pad(parts, ((0, LANES - parts.shape[0]), (0, 0))).T


def as_table(place, sums, rows):
    owners = place.lines * 2 * place.planes
    parts = [
        vector.reshape(owners, -1, rows).transpose(1, 0, 2).reshape(-1, owners * rows)
        for vector in sums
    ]
    table = jnp.concatenate(parts)
    return jnp.pad(table, ((0, LANES - table.shape[0]), (0, 0))).astype(BF16)


def from_table(place, table, sizes, rows):
    owners = place.lines * 2 * place.planes
    vectors, at = [], 0
    for size in sizes:
        each = size // rows
        part = table[at : at + each]
        if each > 1:
            part = part.reshape(each, owners, rows).transpose(1, 0, 2)
        vectors.append(part.reshape(1, -1))
        at += each
    return vectors


class Scatter:
    def __init__(self, place, kept, sent):
        self.place = place
        self.kept = kept
        self.stages = [
            functools.partial(place.swap_plane, stage=stage)
            for stage in reversed(range(len(place.bits)))
        ] + [functools.partial(place.swap_line, bit=bit) for bit in place.line_bits]
        self.arrived = self.stages.pop(0)(place.wait(sent))

    def next(self):
        self.kept, sent = combine(self.place, self.kept, self.place.wait(self.arrived))
        self.arrived = self.stages.pop(0)(sent)

    def spread(self):
        place = self.place
        while len(self.stages) > len(place.line_bits):
            self.next()
        self.kept, *pieces = combine(place, self.kept, place.wait(self.arrived), apart=True)
        self.arrived = [
            place.swap_line(piece, mask) for piece, mask in zip(pieces, place.reversed_lines()[1:])
        ]
        self.stages = []

    def result(self):
        while self.stages:
            self.next()
        total = self.kept[0].astype(F32)
        for arrival in jax.tree.leaves(self.place.wait(self.arrived)):
            total = total + arrival[0].astype(F32)
        return total


def combine(place, kept, arrived, apart=False):
    count, rows, width = kept.shape
    each = 1 if apart else count // 2
    outs = count // each
    steps = 2 if kept.size > 2**18 and width % 256 == 0 else 1
    tile = width // steps

    def body(_, kept_ref, arrived_ref, *refs):
        total = (kept_ref[...].astype(F32) + arrived_ref[...].astype(F32)).astype(BF16)
        for k in range(outs):
            refs[k][...] = total[k * each : (k + 1) * each]

    def block(size):
        return pl.BlockSpec((size, rows, tile), lambda n, s: (0, 0, n))

    out = jax.ShapeDtypeStruct((each, rows, width), BF16)
    return call(
        place, body, (steps,), [block(count), block(count)], [block(each)] * outs, [out] * outs,
        (kept, arrived), name="combine",
    )


def relative_block(index, flip, blocks):
    return (index % 2 ^ flip) * (blocks // 2) + index // 2


def natural_block(index, flip, blocks):
    half = blocks // 2
    return index % half * 2 + (index // half ^ flip)


def block_slice(index, size):
    return pl.ds(pl.multiple_of(index * size, size), size)


def store_relative(ref, values, flip, blocks):
    size = values.shape[1] // blocks
    for k in range(blocks):
        at = relative_block(k, flip, blocks) if blocks > 2 else k
        ref[:, block_slice(at, size)] = values[:, k * size : (k + 1) * size].astype(ref.dtype)


def normalized(values):
    center = values - jnp.mean(values, axis=1, keepdims=True)
    inverse = lax.rsqrt(jnp.mean(center * center, axis=1, keepdims=True) + EPSILON)
    return center * inverse, inverse


def norm(place, values, weight, start):
    count, width = values.shape
    block = 256
    blocks = place.blocks

    def body(flip_ref, values_ref, columns_ref, out_ref, table_ref):
        @pl.when(pl.program_id(0) == 0)
        def _():
            table_ref[...] = columns_ref[...].reshape(width, LANES).astype(F32).T

        hat, _ = normalized(values_ref[...].astype(F32))
        store_relative(out_ref, hat * table_ref[0:1] + table_ref[1:2], flip_ref[0], blocks)

    row = pl.BlockSpec((block, width), lambda m, s: (m, 0))
    lines, _, rows, _ = weight.arrays[0].shape
    return call(
        place, body, (count // block,),
        [row, pl.BlockSpec((lines, 2, rows, LANES), lambda m, s: (0, 0, 0, start // LANES))],
        [row, pl.BlockSpec((LANES, width), lambda m, s: (0, 0))],
        [jax.ShapeDtypeStruct((count, width), BF16), jax.ShapeDtypeStruct((LANES, width), F32)],
        (values, weight.arrays[0]), name="norm",
    )


def relabel(place, values):
    count, width = values.shape
    blocks = place.blocks
    if blocks == 2:
        return values
    size = width // blocks

    def body(_, values_ref, out_ref):
        out_ref[...] = values_ref[...]

    return call(
        place, body, (blocks,),
        [pl.BlockSpec((count, size), lambda k, s: (0, k))],
        pl.BlockSpec((count, size), lambda k, s: (0, relative_block(k, s[0], blocks))),
        jax.ShapeDtypeStruct((count, width), values.dtype), (values,),
        name="relabel",
    )


def project(place, inputs, weight, start, width, tile=1024, name="project"):
    count, depth = inputs.shape
    half = depth // 2

    def body(_, inputs_ref, own_ref, other_ref, out_ref):
        total = nn(inputs_ref[:, :half], rows_of(own_ref)) + nn(inputs_ref[:, half:], rows_of(other_ref))
        out_ref[...] = total.astype(BF16)

    return call(
        place, body, (width // tile,),
        [pl.BlockSpec((count, depth), lambda n, s: (0, 0))]
        + weight.specs(weight.lines, tile, lambda n: (0, start // tile + n)),
        pl.BlockSpec((count, tile), lambda n, s: (0, n)),
        jax.ShapeDtypeStruct((count, width), BF16), (inputs, *weight.arrays),
        name=name,
    )


def project_norm(place, inputs, weight, start, base, gain, bias, name):
    count, depth = inputs.shape
    half = depth // 2
    width = base.shape[1]
    block = 256
    blocks = place.blocks

    def body(flip_ref, inputs_ref, own_ref, other_ref, base_ref, gain_ref, bias_ref, after_ref, out_ref):
        total = nn(inputs_ref[:, :half], rows_of(own_ref)) + nn(inputs_ref[:, half:], rows_of(other_ref))
        total = total + base_ref[...].astype(F32)
        after_ref[...] = total
        hat, _ = normalized(total)
        store_relative(out_ref, hat * gain_ref[...] + bias_ref[...], flip_ref[0], blocks)

    row = pl.BlockSpec((block, width), lambda m, s: (m, 0))
    vector = pl.BlockSpec((1, width), lambda m, s: (0, 0))
    return call(
        place, body, (count // block,),
        [pl.BlockSpec((block, depth), lambda m, s: (m, 0))]
        + weight.specs(weight.lines, width, lambda m: (0, start // width))
        + [row, vector, vector],
        [row, row],
        [pltpu.HBM((count, width), F32), jax.ShapeDtypeStruct((count, width), BF16)],
        (inputs, *weight.arrays, pinned(base), gain, bias),
        name=name,
    )


def hidden_layer(place, inputs, weight, bias):
    count, depth = inputs.shape
    half = depth // 2
    width = weight.width
    size = width // place.blocks

    def body(flip_ref, inputs_ref, own_ref, other_ref, bias_ref, middle_own, middle_other, slope_ref):
        scale = 0.7978845608028654
        for k, middle_ref in enumerate((middle_own, middle_other)):
            at = block_slice(k ^ flip_ref[0], size)
            upper = own_ref[:, 0, :, at].reshape(half, size)
            lower = other_ref[:, 0, :, at].reshape(half, size)
            before = nn(inputs_ref[:, :half], upper) + nn(inputs_ref[:, half:], lower)
            before = before + bias_ref[:, at]
            square = before * before
            half_sum = 0.5 + 0.5 * jnp.tanh(before * (scale + scale * 0.044715 * square))
            middle = before * half_sum
            middle_ref[...] = middle.astype(BF16)
            slope = half_sum + middle * (1.0 - half_sum) * (2.0 * scale + 6.0 * scale * 0.044715 * square)
            slope_ref[:, at] = slope.astype(BF16)

    column = pl.BlockSpec((count, size), lambda n, s: (0, n))
    return call(
        place, body, (place.blocks // 2,),
        [pl.BlockSpec((count, depth), lambda n, s: (0, 0))]
        + weight.specs(weight.lines, 2 * size, lambda n: (0, n))
        + [pl.BlockSpec((1, 2 * size), lambda n, s: (0, n))],
        [column, column, pl.BlockSpec((count, 2 * size), lambda n, s: (0, n))],
        [jax.ShapeDtypeStruct((count, width // 2), BF16)] * 2 + [pltpu.HBM((count, width), BF16)],
        (inputs, *weight.arrays, bias),
        name="hidden_layer",
    )


def last_layer(place, inputs, weight, bias, base):
    count, half = inputs[0].shape
    width = base.shape[1]
    steps = 4 if place.relative else 1
    size = half // steps

    def body(_, inputs_own, inputs_other, own_ref, other_ref, bias_ref, base_ref, out_ref, total_ref):
        step = pl.program_id(0)
        part = nn(inputs_own[...], rows_of(own_ref)) + nn(inputs_other[...], rows_of(other_ref))

        @pl.when(step == 0)
        def _():
            total_ref[...] = part

        @pl.when((step > 0) & (step < steps - 1))
        def _():
            total_ref[...] += part

        @pl.when(step == steps - 1)
        def _():
            total = total_ref[...] + part if steps > 1 else part
            out_ref[...] = (base_ref[...] + (total + bias_ref[...])).astype(BF16)

    column = pl.BlockSpec((count, size), lambda n, s: (0, n))
    rest = pl.BlockSpec((count, width), lambda n, s: (0, 0))
    return call(
        place, body, (steps,),
        [column, column]
        + weight.specs(weight.lines // steps, width, lambda n: (n, 0))
        + [pl.BlockSpec((1, width), lambda n, s: (0, 0)), rest],
        rest, jax.ShapeDtypeStruct((count, width), BF16), (*inputs, *weight.arrays, bias, base),
        scratch=[pltpu.VMEM((count, width), F32)],
        name="last_layer",
    )


def hidden_grad(place, grads, weight, slope):
    count, width = grads.shape
    hidden = slope.shape[1]
    pairs = place.blocks // 2
    size = hidden // place.blocks

    def body(flip_ref, grads_ref, own_ref, other_ref, slope_ref, out_ref, sum_ref):
        for k, weight_ref in enumerate((own_ref, other_ref)):
            at = block_slice(k ^ flip_ref[0], size)
            value = (nt(grads_ref[...], rows_of(weight_ref)) * slope_ref[:, at].astype(F32)).astype(BF16)
            out_ref[:, at] = value
            sum_ref[:, at] = jnp.sum(value.astype(F32), axis=0, keepdims=True)

    column = pl.BlockSpec((count, 2 * size), lambda n, s: (0, n))
    return call(
        place, body, (pairs,),
        [pl.BlockSpec((count, width), lambda n, s: (0, 0))]
        + weight.specs(1, width, lambda n: (n, 0))
        + [column],
        [column, pl.BlockSpec((1, 2 * size), lambda n, s: (0, n))],
        [jax.ShapeDtypeStruct((count, hidden), BF16), jax.ShapeDtypeStruct((1, hidden), F32)],
        (grads, *weight.arrays, pinned(slope)),
        name="hidden_grad",
    )


def back_project(place, grads, weight, start, name):
    count, width = grads.shape
    half = weight.half
    block = 256

    def body(_, grads_ref, own_ref, other_ref, out_ref):
        out_ref[:, :half] = nt(grads_ref[...], rows_of(own_ref)).astype(BF16)
        out_ref[:, half:] = nt(grads_ref[...], rows_of(other_ref)).astype(BF16)

    return call(
        place, body, (count // block,),
        [pl.BlockSpec((block, width), lambda m, s: (m, 0))]
        + weight.specs(weight.lines, width, lambda m: (0, start // width)),
        pl.BlockSpec((block, 2 * half), lambda m, s: (m, 0)),
        jax.ShapeDtypeStruct((count, 2 * half), BF16), (grads, *weight.arrays),
        name=name,
    )


def back_project_natural(place, grads, weight, start, name):
    count, width = grads.shape
    half = weight.half
    block = 256
    blocks = place.blocks
    size = 2 * half // blocks

    def body(flip_ref, grads_ref, own_ref, other_ref, out_ref):
        for k, weight_ref in enumerate((own_ref, other_ref)):
            total = nt(grads_ref[...], rows_of(weight_ref)).astype(BF16)
            for b in range(blocks // 2):
                at = natural_block(k * (blocks // 2) + b, flip_ref[0], blocks) if blocks > 2 else k
                out_ref[:, block_slice(at, size)] = total[:, b * size : (b + 1) * size]

    return call(
        place, body, (count // block,),
        [pl.BlockSpec((block, width), lambda m, s: (m, 0))]
        + weight.specs(weight.lines, width, lambda m: (0, start // width)),
        pl.BlockSpec((block, 2 * half), lambda m, s: (m, 0)),
        jax.ShapeDtypeStruct((count, 2 * half), BF16), (grads, *weight.arrays),
        name=name,
    )


def back_project_norm(place, grads, weight, start, values, gain, base, kinds, name):
    count, width = grads.shape
    half = weight.half
    features = 2 * half
    block = 256
    blocks = place.blocks
    size = features // blocks

    def body(flip_ref, grads_ref, own_ref, other_ref, values_ref, gain_ref, base_ref, *refs):
        outs, sums_ref, upstream_ref = refs[: len(kinds)], refs[len(kinds)], refs[len(kinds) + 1]
        for k, weight_ref in enumerate((own_ref, other_ref)):
            total = nt(grads_ref[...], rows_of(weight_ref))
            for b in range(blocks // 2):
                at = natural_block(k * (blocks // 2) + b, flip_ref[0], blocks) if blocks > 2 else k
                upstream_ref[:, block_slice(at, size)] = total[:, b * size : (b + 1) * size]
        upstream = upstream_ref[...]
        hat, inverse = normalized(values_ref[...].astype(F32))
        weighted = upstream * gain_ref[...]
        base_values = base_ref[...].astype(F32)
        grad = base_values + inverse * (
            weighted
            - jnp.mean(weighted, axis=1, keepdims=True)
            - hat * jnp.mean(weighted * hat, axis=1, keepdims=True)
        )
        for out in outs:
            out[...] = grad.astype(out.dtype)

        @pl.when(pl.program_id(0) == 0)
        def _():
            sums_ref[...] = jnp.zeros_like(sums_ref)

        sums_ref[0:1] += jnp.sum(upstream * hat, axis=0, keepdims=True)
        sums_ref[1:2] += jnp.sum(upstream, axis=0, keepdims=True)
        sums_ref[2:3] += jnp.sum(base_values, axis=0, keepdims=True)

    row = pl.BlockSpec((block, features), lambda m, s: (m, 0))
    sums = pl.BlockSpec((8, features), lambda m, s: (0, 0))
    return call(
        place, body, (count // block,),
        [pl.BlockSpec((block, width), lambda m, s: (m, 0))]
        + weight.specs(
            weight.lines, width, lambda m: (0, start // width), pipeline_mode=pl.Buffered(1)
        )
        + [row, pl.BlockSpec((1, features), lambda m, s: (0, 0)), row],
        [row] * len(kinds) + [sums],
        [(pltpu.HBM if kind == F32 else jax.ShapeDtypeStruct)((count, features), kind) for kind in kinds]
        + [jax.ShapeDtypeStruct((8, features), F32)],
        (pinned(grads) if width > 2 * features else grads, *weight.arrays, pinned(values), gain, pinned(base)),
        scratch=[pltpu.VMEM((block, features), F32)],
        name=name,
    )


def part_of(inputs, part):
    if isinstance(inputs, tuple):
        return inputs[part], 0, inputs[part].shape[1]
    return inputs, part, inputs.shape[1] // 2


def weight_part(place, inputs, grads, part, name, total=None, start=0, into=None):
    inputs, part, depth = part_of(inputs, part)
    count, width = grads.shape
    rows = min(1024, depth)
    tile = width if width <= 1024 else width // 2
    steps = depth // rows

    def body(_, inputs_ref, grads_ref, *refs):
        refs[-1][...] = tn(inputs_ref[...], grads_ref[...]).astype(BF16)

    return call(
        place, body, (steps, width // tile),
        [
            pl.BlockSpec((count, rows), lambda k, n, s: (0, part * steps + k)),
            pl.BlockSpec((count, tile), lambda k, n, s: (0, n)),
        ]
        + [pl.BlockSpec(memory_space=pl.ANY)] * (into is not None),
        pl.BlockSpec((rows, tile), lambda k, n, s: (k, start // tile + n)),
        jax.ShapeDtypeStruct((depth, total or width), BF16),
        (inputs, grads) + ((into,) if into is not None else ()),
        name=name, aliases={3: 0} if into is not None else {},
    )


def weight_sums(place, inputs, grads, arrived, name, total=None, start=0, into=None):
    inputs, _, depth = part_of(inputs, 0)
    count, width = grads.shape
    planes, lines = place.planes, place.lines
    each = depth // (lines * planes)
    tile = width if width * depth <= 2**19 else width // 2
    first, arrived = arrived
    pieces = planes // 2 * lines

    def body(slots_ref, inputs_ref, grads_ref, arrived_ref, *refs):
        kept_ref, sent_ref, total_ref = refs[-3:]
        total_ref[...] = tn(inputs_ref[...], grads_ref[...]) + arrived_ref[...].astype(F32)
        for k in range(planes):
            out_ref = kept_ref if k < planes // 2 else sent_ref
            for n in range(lines):
                line = slots_ref[place.at_lines + n]
                here = pl.multiple_of((line * planes + slots_ref[place.at_plane + k]) * each, each)
                out_ref[k % (planes // 2) * lines + n] = total_ref[pl.ds(here, each)].astype(BF16)

    block = pl.BlockSpec((pieces, each, tile), lambda n, s: (0, 0, start // tile + n))
    out = jax.ShapeDtypeStruct((pieces, each, total or width), BF16)
    return call(
        place, body, (width // tile,),
        [
            pl.BlockSpec((count, depth), lambda n, s: (0, 0)),
            pl.BlockSpec((count, tile), lambda n, s: (0, n)),
            pl.BlockSpec((depth, tile), lambda n, s: (0, first // tile + n)),
        ]
        + [pl.BlockSpec(memory_space=pl.ANY)] * (2 if into is not None else 0),
        [block, block], [out, out], (inputs, grads, arrived) + (tuple(into) if into is not None else ()),
        scratch=[pltpu.VMEM((depth, tile), F32)],
        name=name, aliases={4: 0, 5: 1} if into is not None else {},
    )


class WeightGrad:
    def __init__(self, place, inputs, grads, names):
        if not isinstance(inputs, list):
            inputs, grads, names = [inputs], [grads], [names]
        self.place = place
        self.inputs, self.grads, self.names = inputs, grads, names
        self.starts = [sum(grad.shape[1] for grad in grads[:k]) for k in range(len(grads))]
        total = sum(grad.shape[1] for grad in grads)
        sides = []
        for part in (1,) if place.relative else (1, 0):
            into = None
            for k, name in enumerate(names):
                into = weight_part(
                    place, inputs[k], grads[k], part, name + ("_own", "_other")[part], total,
                    self.starts[k], into,
                )
            sides.append(into)
        first = sides[0]
        if not place.relative:
            each = first.shape[0] // place.lines
            both = jnp.concatenate(sides[::-1]).reshape(place.lines, 2, each, -1)
            self.own = lax.dynamic_index_in_dim(both, place.core, 1, keepdims=False)
            first = lax.dynamic_index_in_dim(both, 1 - place.core, 1, keepdims=False)
            first = first.reshape(-1, total)
        self.arrived = place.swap_core(first)

    def sums(self, more=None):
        place = self.place
        parts = [self] if more is None else [self, more]
        arrived = [place.wait(part.arrived) for part in parts]
        total = sum(value.shape[1] for value in arrived)
        if place.relative:
            into, before = None, 0
            for part, value in zip(parts, arrived):
                for k, name in enumerate(part.names):
                    into = weight_sums(
                        place, part.inputs[k], part.grads[k], (part.starts[k], value), name + "_own",
                        total, before + part.starts[k], into,
                    )
                before += value.shape[1]
            return into
        own = jnp.concatenate([part.own for part in parts], axis=2)
        sums = own.astype(F32) + jnp.concatenate(arrived, axis=1).astype(F32).reshape(own.shape)
        sums = sums.astype(BF16).reshape(place.lines, place.planes, -1, total)
        sums = sums.transpose(1, 0, 2, 3)[place.plane_slots]
        sums = sums[:, place.line ^ jnp.array(place.reversed_lines())]
        return jnp.split(sums.reshape(place.planes * place.lines, -1, total), 2)


def own_lanes(head, values, scaling=None):
    lane = lax.broadcasted_iota(jnp.int32, values.shape, 1)
    size = values.shape[1] // 2
    scaled = values if scaling is None else values * scaling
    return jnp.where((lane >= head * size) & (lane < (head + 1) * size), scaled, 0).astype(BF16)


def softmax(scores):
    weights = jnp.exp(scores - jnp.max(scores, axis=1, keepdims=True))
    return weights * (1.0 / jnp.sum(weights, axis=1, keepdims=True))


def relative_lanes(place, width):
    per = width // place.blocks // LANES

    def column(p, flip):
        return relative_block(p // per, flip, place.blocks) * per + p % per

    return column


def lane_block(k):
    return slice(k * LANES, (k + 1) * LANES)


def attention(place, query, key_value, starts, items, per, masked, name):
    count = query.shape[0]
    rows, keys = count // items, key_value.shape[0] // items
    pairs = HEADS // 2
    width = pairs * LANES
    scaling = (width // HEADS) ** (-0.5)
    column = relative_lanes(place, width)

    def body(scalars_ref, query_ref, key_ref, value_ref, out_ref, prob_ref):
        for k in range(per):
            total = 0.0
            for head in range(2):
                scores = nt(own_lanes(head, query_ref[:, lane_block(k)], scaling), key_ref[:, lane_block(k)])
                weights = softmax(masked(scores, scalars_ref, pl.program_id(0))).astype(BF16)
                prob_ref[0, 2 * k + head] = weights
                total = total + nn(weights, own_lanes(head, value_ref[:, lane_block(k)]))
            at = column(pl.program_id(1) * per + k, scalars_ref[0])
            out_ref[:, block_slice(at, LANES)] = total.astype(BF16)

    spec = lambda size, start: pl.BlockSpec((size, per * LANES), lambda b, p, s: (b, start // per + p))
    return call(
        place, body, (items, pairs // per),
        [spec(rows, 0), spec(keys, starts[0]), spec(keys, starts[1])],
        [
            pl.BlockSpec((rows, width), lambda b, p, s: (b, 0)),
            pl.BlockSpec((1, 2 * per, rows, keys), lambda b, p, s: (b, p, 0, 0)),
        ],
        [
            jax.ShapeDtypeStruct((count, width), BF16),
            pltpu.HBM((items, HEADS, rows, keys), BF16),
        ],
        (query, key_value, key_value),
        name=name,
    )


def attention_grads(place, query, key_value, starts, probability, grad, out_widths, items, per, name):
    count = query.shape[0]
    rows, keys = count // items, key_value.shape[0] // items
    pairs = HEADS // 2
    width = pairs * LANES
    scaling = (width // HEADS) ** (-0.5)
    column = relative_lanes(place, width)
    alone = len(out_widths) == 1

    def body(scalars_ref, query_ref, key_ref, value_ref, prob_ref, grad_ref, *outs):
        for k in range(per):
            pair = pl.program_id(1) * per + k
            at = block_slice(column(pair, scalars_ref[0]), LANES)
            query_total = key_total = value_total = 0.0
            for head in range(2):
                weights = prob_ref[0, 2 * k + head]
                own_grad = own_lanes(head, grad_ref[:, at])
                prob_grad = nt(own_grad, value_ref[:, lane_block(k)])
                wide = weights.astype(F32)
                weighted = wide * prob_grad
                centre = jnp.sum(weighted, axis=1, keepdims=True)
                score_grad = (weighted - wide * centre).astype(BF16)
                query_total = query_total + nn(
                    score_grad, own_lanes(head, key_ref[:, lane_block(k)], scaling)
                )
                key_total = key_total + tn(
                    score_grad, own_lanes(head, query_ref[:, lane_block(k)], scaling)
                )
                value_total = value_total + tn(weights, own_grad)
            first = pairs if alone else 0
            outs[0][:, block_slice(pair, LANES)] = query_total.astype(BF16)
            outs[-1][:, block_slice(first + pair, LANES)] = key_total.astype(BF16)
            outs[-1][:, block_slice(first + pairs + pair, LANES)] = value_total.astype(BF16)

    spec = lambda size, start: pl.BlockSpec((size, per * LANES), lambda b, p, s: (b, start // per + p))
    heights = [rows] if alone else [rows, keys]
    return call(
        place, body, (items, pairs // per),
        [
            spec(rows, 0), spec(keys, starts[0]), spec(keys, starts[1]),
            pl.BlockSpec((1, 2 * per, rows, keys), lambda b, p, s: (b, p, 0, 0)),
            pl.BlockSpec((rows, width), lambda b, p, s: (b, 0)),
        ],
        [
            pl.BlockSpec((height, wide), lambda b, p, s: (b, 0))
            for height, wide in zip(heights, out_widths)
        ],
        [
            jax.ShapeDtypeStruct((items * height, wide), BF16)
            for height, wide in zip(heights, out_widths)
        ],
        (query, key_value, key_value, pinned(probability), grad),
        name=name,
    )


def causal(scores, scalars_ref, item):
    row = lax.broadcasted_iota(jnp.int32, scores.shape, 0)
    column = lax.broadcasted_iota(jnp.int32, scores.shape, 1)
    return jnp.where(column <= row, scores, NEGATIVE)


def visible(first_length):
    def masked(scores, scalars_ref, item):
        column = lax.broadcasted_iota(jnp.int32, scores.shape, 1)
        return jnp.where(column < scalars_ref[first_length + item], scores, NEGATIVE)

    return masked


def per_device(
    tokens,
    text_states,
    caption_len,
    out_grad,
    norm1_gain,
    norm1_bias,
    qkv_weight,
    self_out,
    norm2_gain,
    norm2_bias,
    cross_query,
    cross_kv,
    cross_out,
    norm3_gain,
    norm3_bias,
    ff_in,
    ff_in_bias,
    ff_out,
    ff_out_bias,
):
    place = Place(lax.axis_size("dp") // 2, lax.axis_size("fsdp"), qkv_weight.shape[0], caption_len)
    items, rows, width = tokens.shape
    text = text_states.shape[1]
    count = items * rows
    values0 = tokens.reshape(count, width)
    text_rows = text_states.reshape(items * text, width)
    cot = out_grad.reshape(count, width)

    small = (
        norm1_gain, norm1_bias, norm2_gain, norm2_bias, norm3_gain, norm3_bias, ff_in_bias, ff_out_bias
    )
    sizes = [vector.shape[0] for vector in small]
    middle_group = jnp.concatenate([cross_kv, cross_query, cross_out, self_out], axis=1)
    at_kv, at_query, at_cross, at_self = 0, 2 * width, 3 * width, 4 * width

    shard_rows = qkv_weight.shape[0]
    mid_group = Gather(place, middle_group)
    full_qkv = lax.all_gather(
        jnp.concatenate([qkv_weight, as_columns(place, small, shard_rows)], axis=1),
        AXES, axis=0, tiled=True,
    )
    mid_group.join_line()
    full_out = lax.all_gather(place.wait(ff_out), AXES, axis=0, tiled=True)
    in_group = Gather(place, ff_in)
    text_relative = relabel(place, text_rows)
    mid_group.swap()
    in_group.join_line()
    mid_group.join_plane()
    w_qkv = Weight(place, place.wait(full_qkv))
    normed1, table = norm(place, values0, w_qkv, 3 * width)
    (gain1, bias1, gain2, bias2, gain3, bias3, in_bias, out_bias) = from_table(
        place, table, sizes, shard_rows
    )
    projected = project(place, normed1, w_qkv, 0, 3 * width, name="project_qkv")
    w_mid = mid_group.weight()
    text_kv = project(place, text_relative, w_mid, at_kv, 2 * width, name="project_text")
    in_group.swap()
    pairs = HEADS // 2
    attended1, probs1 = attention(
        place, projected, projected, (pairs, 2 * pairs), items, 4, causal, "self_attention"
    )
    values1, normed2 = project_norm(
        place, attended1, w_mid, at_self, values0, gain2, bias2, "self_out_norm"
    )
    query2 = project(place, normed2, w_mid, at_query, width, name="project_query")
    attended2, probs2 = attention(
        place, query2, text_kv, (0, pairs), items, 4, visible(place.at_length), "cross_attention"
    )
    in_group.join_plane()
    values2, normed3 = project_norm(
        place, attended2, w_mid, at_cross, values1, gain3, bias3, "cross_out_norm"
    )
    w_in = in_group.weight()
    *middle, slope = hidden_layer(place, normed3, w_in, in_bias)
    ff_out_terms = WeightGrad(place, tuple(middle), cot, "ff_out_grad")
    w_out = Weight(place, place.wait(full_out))

    before_grad, in_bias_sum = hidden_grad(place, cot, w_out, slope)
    ff_out_own = ff_out_terms.sums()
    ff_in_terms = WeightGrad(place, normed3, before_grad, "ff_in_grad")

    ff_out_sums = Scatter(place, *ff_out_own)
    cross_grad, cross_round, sums3 = back_project_norm(
        place, before_grad, w_in, 0, values2, gain3, cot, (F32, BF16), "norm3_grad"
    )
    ff_in_own = ff_in_terms.sums()
    attended2_grad = back_project(place, cross_round, w_mid, at_cross, "attended2_grad")
    query2_grad, text_kv_grad = attention_grads(
        place, query2, text_kv, (0, pairs), probs2, attended2_grad, (width, 2 * width), items, 4,
        "cross_attention_grads",
    )
    ff_out_sums.next()
    middle_terms = WeightGrad(
        place,
        [text_relative, normed2, attended2],
        [text_kv_grad, query2_grad, cross_round],
        ["cross_kv_grad", "cross_query_grad", "cross_out_grad"],
    )

    ff_in_sums = Scatter(place, *ff_in_own)
    self_grad, self_round, sums2 = back_project_norm(
        place, query2_grad, w_mid, at_query, values1, gain2, cross_grad, (F32, BF16), "norm2_grad"
    )
    middle_own = middle_terms.sums()
    attended1_grad = back_project(place, self_round, w_mid, at_self, "attended1_grad")
    (projected_grad,) = attention_grads(
        place, projected, projected, (pairs, 2 * pairs), probs1, attended1_grad, (3 * width,), items, 4,
        "self_attention_grads",
    )
    ff_out_sums.next()
    ff_in_sums.next()
    last_terms = WeightGrad(
        place, [normed1, attended1], [projected_grad, self_round], ["qkv_grad", "self_out_grad"]
    )

    middle_sums = Scatter(place, *middle_own)
    tokens_grad, sums1 = back_project_norm(
        place, projected_grad, w_qkv, 0, values0, gain1, self_grad, (BF16,), "norm1_grad"
    )
    table = relabel(place, as_table(place, (
        sums1[0], sums1[1], sums2[0], sums2[1], sums3[0], sums3[1], in_bias_sum[0], sums3[2]
    ), shard_rows))
    small_terms = WeightGrad(place, table, jnp.eye(LANES, dtype=BF16), "small_grad")
    ff_out_sums.next()
    last_own = last_terms.sums(small_terms)
    ff_in_sums.next()
    middle_sums.next()

    last_sums = Scatter(place, *last_own)
    text_grad = back_project_natural(place, text_kv_grad, w_mid, at_kv, "text_grad")
    result = last_layer(place, middle, w_out, out_bias, values2)
    ff_in_sums.next()
    ff_out_grad = ff_out_sums.result()
    middle_sums.next()
    last_sums.next()
    last_sums.next()
    middle_sums.next()
    ff_in_grad = ff_in_sums.result()
    last_sums.next()
    middle_grads = middle_sums.result()
    last_grads = last_sums.result()
    small_grads = last_grads[:, 4 * width :].T
    own, at = [], 0
    for size in sizes:
        own.append(small_grads[at : at + size // shard_rows].reshape(-1))
        at += size // shard_rows
    return (
        result.reshape(items, rows, width),
        tokens_grad.reshape(items, rows, width),
        text_grad.reshape(items, text, width),
        own[0],
        own[1],
        last_grads[:, : 3 * width],
        last_grads[:, 3 * width : 4 * width],
        own[2],
        own[3],
        middle_grads[:, at_query : at_query + width],
        middle_grads[:, at_kv : at_kv + 2 * width],
        middle_grads[:, at_cross : at_cross + width],
        own[4],
        own[5],
        ff_in_grad,
        own[6],
        ff_out_grad,
        own[7],
    )


def solution(mesh):
    whole = P(AXES, None, None)
    matrix = P(AXES, None)
    vector = P(AXES)
    weights = (
        vector, vector, matrix, matrix, vector, vector, matrix, matrix, matrix, vector, vector, matrix,
        vector, matrix, vector,
    )
    return jax.shard_map(
        per_device,
        mesh=mesh,
        in_specs=(whole, whole, vector, whole) + weights,
        out_specs=(whole, whole, whole) + weights,
        check_vma=False,
    )
```

```python
import functools

import jax
import jax.numpy as jnp
from jax import lax
from jax.experimental import pallas as pl
from jax.experimental.pallas import tpu as pltpu
from jax.sharding import PartitionSpec as P

HEADS = 16
EPSILON = 1e-05
NEGATIVE = -1e30
AXES = ("dp", "fsdp")
F32 = jnp.float32
BF16 = jnp.bfloat16
LANES = 128
HBM_BYTES = 6400000
VMEM_MIB = {
    "project_qkv": 14,
    "self_attention": 11,
    "self_out_norm": 10,
    "project_query": 11,
    "cross_out_norm": 11,
    "hidden_layer": 14,
    "last_layer": 20,
    "hidden_grad": 14,
    "norm3_grad": 25,
    "cross_attention_grads": 13,
    "norm2_grad": 17,
    "self_attention_grads": 25,
    "norm1_grad": 20,
    "qkv_grad_other": 11,
    "qkv_grad_own": 17,
    "self_out_grad_own": 10,
    "cross_kv_grad_own": 10,
    "cross_query_grad_own": 10,
    "cross_out_grad_own": 10,
    "ff_in_grad_other": 14,
    "ff_in_grad_own": 22,
    "ff_out_grad_other": 11,
    "ff_out_grad_own": 23,
}


def nt(first, second):
    return lax.dot_general(first, second, (((1,), (1,)), ((), ())), preferred_element_type=F32)


def tn(first, second):
    return lax.dot_general(first, second, (((0,), (0,)), ((), ())), preferred_element_type=F32)


def nn(first, second):
    return lax.dot_general(first, second, (((1,), (0,)), ((), ())), preferred_element_type=F32)


def call(place, body, grid, in_specs, out_specs, out_shape, args, scratch=(), name=None, aliases=None):
    spec = pltpu.PrefetchScalarGridSpec(
        num_scalar_prefetch=1, grid=grid, in_specs=in_specs, out_specs=out_specs,
        scratch_shapes=list(scratch),
    )
    out_shape = jax.tree.map(
        lambda o: pltpu.HBM(o.shape, o.dtype) if is_large(o) else o, out_shape
    )
    out = pl.pallas_call(
        body, grid_spec=spec, out_shape=out_shape, name=name, input_output_aliases=aliases or {},
        cost_estimate=pl.CostEstimate(flops=1, bytes_accessed=1, transcendentals=0),
        compiler_params=pltpu.CompilerParams(vmem_limit_bytes=(VMEM_MIB.get(name, 8) if place.relative else 48) * 2**20),
    )(place.scalars, *[in_hbm(arg) for arg in args])
    return place.wait(out)


def is_large(value):
    return isinstance(value, (jax.Array, jax.ShapeDtypeStruct)) and (
        value.size * value.dtype.itemsize >= HBM_BYTES
    )


def pinned(value):
    return pltpu.with_memory_space_constraint(value, pltpu.HBM)


def in_hbm(value):
    if not is_large(value):
        return value
    return pinned(value)


class Place:
    def __init__(self, lines, planes, rows, lengths):
        self.lines = lines
        self.planes = planes
        self.bits = [1 << k for k in range(planes.bit_length() - 1)]
        self.line_bits = [1 << k for k in range(lines.bit_length() - 1)]
        dp = lax.axis_index("dp")
        self.line = dp // 2
        self.core = dp % 2
        self.plane = lax.axis_index("fsdp")
        self.relative = planes * rows % LANES == 0
        self.flip = (self.core if self.relative else jnp.zeros_like(self.core)).astype(jnp.int32)
        self.blocks = 2 * lines if self.relative else 2
        stages = len(self.bits)
        self.masks = [[0], [0]]
        for core in range(2):
            for stage in range(stages):
                bit = self.stage_bit(stage, core)
                self.masks[core] = self.masks[core] + [m ^ bit for m in self.masks[core]]
        masks = jnp.where(self.core == 0, jnp.array(self.masks[0]), jnp.array(self.masks[1]))
        self.plane_slots = (masks ^ self.plane).astype(jnp.int32)
        self.line_slots = ((self.line - jnp.arange(lines)) % lines).astype(jnp.int32)
        self.core_slots = (jnp.arange(2) ^ self.core).astype(jnp.int32)
        parts = [
            self.flip[None], lengths, self.plane_slots, self.line_slots, self.core_slots,
            (self.line ^ jnp.array(self.reversed_lines())).astype(jnp.int32),
        ]
        starts = [0]
        for part in parts:
            starts.append(starts[-1] + part.shape[0])
        _, self.at_length, self.at_plane, self.at_line, self.at_core, self.at_lines, _ = starts
        self.scalars = jnp.concatenate(parts)

    def wait(self, values):
        values, self.scalars = lax.optimization_barrier((values, self.scalars))
        return values

    def reversed_lines(self):
        order = [0]
        for bit in reversed(self.line_bits):
            order = order + [mask ^ bit for mask in order]
        return order

    def stage_bit(self, stage, core):
        return self.bits[(stage + core) % len(self.bits)]

    def _permute(self, value, target):
        pairs = []
        for line in range(self.lines):
            for core in range(2):
                for plane in range(self.planes):
                    l, c, p = target(line, core, plane)
                    pairs.append(
                        ((line * 2 + core) * self.planes + plane, (l * 2 + c) * self.planes + p)
                    )
        return lax.ppermute(value, AXES, pairs)

    def shift_line(self, value, step):
        return self._permute(value, lambda l, c, p: ((l + step) % self.lines, c, p))

    def swap_plane(self, value, stage):
        return self._permute(value, lambda l, c, p: (l, c, p ^ self.stage_bit(stage, c)))

    def swap_line(self, value, bit):
        return self._permute(value, lambda l, c, p: (l ^ bit, c, p))

    def swap_core(self, value):
        return self._permute(value, lambda l, c, p: (l, 1 - c, p))


def interleave(place, pieces, first):
    count = len(pieces)
    outer, rows, width = pieces[0].shape
    tile = width

    def body(slots_ref, *refs):
        out_ref = refs[count]
        for k in range(count):
            out_ref[0, pl.ds(slots_ref[first + k], 1)] = refs[k][...]

    moved = 2 * count * pieces[0].size * pieces[0].dtype.itemsize
    return call(
        place, body,
        (outer, width // tile),
        [pl.BlockSpec((1, rows, tile), lambda a, n, s: (a, 0, n))] * count,
        pl.BlockSpec((1, count, rows, tile), lambda a, n, s: (a, 0, 0, n)),
        jax.ShapeDtypeStruct((outer, count, rows, width), pieces[0].dtype),
        pieces,
        name="interleave",
    )


class Gather:
    def __init__(self, place, shard):
        self.place = place
        self.rows, self.width = shard.shape
        shard = place.wait(shard)
        self.pieces = [shard] + [place.shift_line(shard, s) for s in range(1, place.lines)]
        self.stage = 0

    def wait(self):
        self.pieces = self.place.wait(self.pieces)

    def join_line(self):
        place = self.place
        self.wait()
        held = interleave(place, [piece[None] for piece in self.pieces], place.at_line)
        self.pieces = [held.reshape(place.lines, self.rows, self.width)]
        self.swap()

    def swap(self):
        if self.stage:
            self.wait()
        self.pieces = self.pieces + [
            self.place.swap_plane(piece, self.stage) for piece in self.pieces
        ]
        self.stage += 1

    def join_plane(self):
        place = self.place
        while self.stage < len(place.bits):
            self.swap()
        self.wait()
        half = interleave(place, self.pieces, place.at_plane)
        self.own = half.reshape(place.lines, place.planes * self.rows, self.width)
        self.other = place.swap_core(self.own)

    def weight(self):
        place = self.place
        self.other = place.wait(self.other)
        if place.relative:
            return Weight(place, self.own[:, None], self.other[:, None])
        both = interleave(place, [self.own, self.other], place.at_core)
        return Weight(place, both.reshape(-1, self.width))


class Weight:
    def __init__(self, place, *arrays):
        self.full = len(arrays) == 1
        self.width = arrays[0].shape[-1]
        if self.full:
            arrays = (arrays[0].reshape(place.blocks // 2, 2, -1, self.width),) * 2
        self.arrays = arrays
        self.lines, _, self.rows, _ = arrays[0].shape
        self.half = self.lines * self.rows

    def specs(self, lines, columns, index, **more):
        def make(part):
            def index_map(*args):
                line, column = index(*args[:-1])
                which = args[-1][0] ^ part if self.full else 0
                return line, which, 0, column

            return pl.BlockSpec((lines, 1, self.rows, columns), index_map, **more)

        return [make(0), make(1)]


def rows_of(ref):
    lines, _, rows, columns = ref.shape
    return ref[...].reshape(lines * rows, columns)


def as_columns(place, vectors, rows):
    parts = jnp.concatenate([vector.reshape(-1, rows) for vector in vectors])
    return jnp.pad(parts, ((0, LANES - parts.shape[0]), (0, 0))).T


def as_table(place, sums, rows):
    owners = place.lines * 2 * place.planes
    parts = [
        vector.reshape(owners, -1, rows).transpose(1, 0, 2).reshape(-1, owners * rows)
        for vector in sums
    ]
    table = jnp.concatenate(parts)
    return jnp.pad(table, ((0, LANES - table.shape[0]), (0, 0))).astype(BF16)


def from_table(place, table, sizes, rows):
    owners = place.lines * 2 * place.planes
    vectors, at = [], 0
    for size in sizes:
        each = size // rows
        part = table[at : at + each]
        if each > 1:
            part = part.reshape(each, owners, rows).transpose(1, 0, 2)
        vectors.append(part.reshape(1, -1))
        at += each
    return vectors


class Scatter:
    def __init__(self, place, kept, sent):
        self.place = place
        self.kept = kept
        self.stages = [
            functools.partial(place.swap_plane, stage=stage)
            for stage in reversed(range(len(place.bits)))
        ] + [functools.partial(place.swap_line, bit=bit) for bit in place.line_bits]
        self.arrived = self.stages.pop(0)(place.wait(sent))

    def next(self):
        self.kept, sent = combine(self.place, self.kept, self.place.wait(self.arrived))
        self.arrived = self.stages.pop(0)(sent)

    def result(self, *widths):
        while self.stages:
            self.next()
        arrived = self.place.wait(self.arrived)
        parts, at = [], 0
        for width in widths:
            here = slice(at, at + width)
            parts.append(self.kept[0][:, here].astype(F32) + arrived[0][:, here].astype(F32))
            at += width
        return parts


def combine(place, kept, arrived):
    count, rows, width = kept.shape
    each = count // 2
    outs = count // each
    steps = 2 if kept.size > 2**18 and width % 256 == 0 else 1
    tile = width // steps

    def body(_, kept_ref, arrived_ref, *refs):
        total = (kept_ref[...].astype(F32) + arrived_ref[...].astype(F32)).astype(BF16)
        for k in range(outs):
            refs[k][...] = total[k * each : (k + 1) * each]

    def block(size):
        return pl.BlockSpec((size, rows, tile), lambda n, s: (0, 0, n))

    out = jax.ShapeDtypeStruct((each, rows, width), BF16)
    return call(
        place, body, (steps,), [block(count), block(count)], [block(each)] * outs, [out] * outs,
        (kept, arrived), name="combine",
    )


def relative_block(index, flip, blocks):
    return (index % 2 ^ flip) * (blocks // 2) + index // 2


def natural_block(index, flip, blocks):
    half = blocks // 2
    return index % half * 2 + (index // half ^ flip)


def block_slice(index, size):
    return pl.ds(pl.multiple_of(index * size, size), size)


def store_relative(ref, values, flip, blocks):
    size = values.shape[1] // blocks
    for k in range(blocks):
        at = relative_block(k, flip, blocks) if blocks > 2 else k
        ref[:, block_slice(at, size)] = values[:, k * size : (k + 1) * size].astype(ref.dtype)


def normalized(values):
    center = values - jnp.mean(values, axis=1, keepdims=True)
    inverse = lax.rsqrt(jnp.mean(center * center, axis=1, keepdims=True) + EPSILON)
    return center * inverse, inverse


def norm(place, values, weight, start):
    count, width = values.shape
    block = 256
    blocks = place.blocks

    def body(flip_ref, values_ref, columns_ref, out_ref, table_ref):
        @pl.when(pl.program_id(0) == 0)
        def _():
            table_ref[...] = columns_ref[...].reshape(width, LANES).astype(F32).T

        hat, _ = normalized(values_ref[...].astype(F32))
        store_relative(out_ref, hat * table_ref[0:1] + table_ref[1:2], flip_ref[0], blocks)

    row = pl.BlockSpec((block, width), lambda m, s: (m, 0))
    lines, _, rows, _ = weight.arrays[0].shape
    return call(
        place, body, (count // block,),
        [row, pl.BlockSpec((lines, 2, rows, LANES), lambda m, s: (0, 0, 0, start // LANES))],
        [row, pl.BlockSpec((LANES, width), lambda m, s: (0, 0))],
        [jax.ShapeDtypeStruct((count, width), BF16), jax.ShapeDtypeStruct((LANES, width), F32)],
        (values, weight.arrays[0]), name="norm",
    )


def relabel(place, values):
    count, width = values.shape
    blocks = place.blocks
    if blocks == 2:
        return values
    size = width // blocks

    def body(_, values_ref, out_ref):
        out_ref[...] = values_ref[...]

    return call(
        place, body, (blocks,),
        [pl.BlockSpec((count, size), lambda k, s: (0, k))],
        pl.BlockSpec((count, size), lambda k, s: (0, relative_block(k, s[0], blocks))),
        jax.ShapeDtypeStruct((count, width), values.dtype), (values,),
        name="relabel",
    )


def project(place, inputs, weight, start, width, tile=1024, name="project"):
    count, depth = inputs.shape
    half = depth // 2

    def body(_, inputs_ref, own_ref, other_ref, out_ref):
        total = nn(inputs_ref[:, :half], rows_of(own_ref)) + nn(inputs_ref[:, half:], rows_of(other_ref))
        out_ref[...] = total.astype(BF16)

    return call(
        place, body, (width // tile,),
        [pl.BlockSpec((count, depth), lambda n, s: (0, 0))]
        + weight.specs(weight.lines, tile, lambda n: (0, start // tile + n)),
        pl.BlockSpec((count, tile), lambda n, s: (0, n)),
        jax.ShapeDtypeStruct((count, width), BF16), (inputs, *weight.arrays),
        name=name,
    )


def project_norm(place, inputs, weight, start, base, gain, bias, name):
    count, depth = inputs.shape
    half = depth // 2
    width = base.shape[1]
    block = 256
    blocks = place.blocks

    def body(flip_ref, inputs_ref, own_ref, other_ref, base_ref, gain_ref, bias_ref, after_ref, out_ref):
        total = nn(inputs_ref[:, :half], rows_of(own_ref)) + nn(inputs_ref[:, half:], rows_of(other_ref))
        total = total + base_ref[...].astype(F32)
        after_ref[...] = total
        hat, _ = normalized(total)
        store_relative(out_ref, hat * gain_ref[...] + bias_ref[...], flip_ref[0], blocks)

    row = pl.BlockSpec((block, width), lambda m, s: (m, 0))
    vector = pl.BlockSpec((1, width), lambda m, s: (0, 0))
    return call(
        place, body, (count // block,),
        [pl.BlockSpec((block, depth), lambda m, s: (m, 0))]
        + weight.specs(weight.lines, width, lambda m: (0, start // width))
        + [row, vector, vector],
        [row, row],
        [pltpu.HBM((count, width), F32), jax.ShapeDtypeStruct((count, width), BF16)],
        (inputs, *weight.arrays, pinned(base), gain, bias),
        name=name,
    )


def hidden_layer(place, inputs, weight, bias):
    count, depth = inputs.shape
    half = depth // 2
    width = weight.width
    size = width // place.blocks

    def body(flip_ref, inputs_ref, own_ref, other_ref, bias_ref, middle_own, middle_other, slope_ref):
        scale = 0.7978845608028654
        for k, middle_ref in enumerate((middle_own, middle_other)):
            at = block_slice(k ^ flip_ref[0], size)
            upper = own_ref[:, 0, :, at].reshape(half, size)
            lower = other_ref[:, 0, :, at].reshape(half, size)
            before = nn(inputs_ref[:, :half], upper) + nn(inputs_ref[:, half:], lower)
            before = before + bias_ref[:, at]
            square = before * before
            half_sum = 0.5 + 0.5 * jnp.tanh(before * (scale + scale * 0.044715 * square))
            middle = before * half_sum
            middle_ref[...] = middle.astype(BF16)
            slope = half_sum + middle * (1.0 - half_sum) * (2.0 * scale + 6.0 * scale * 0.044715 * square)
            slope_ref[:, at] = slope.astype(BF16)

    column = pl.BlockSpec((count, size), lambda n, s: (0, n))
    return call(
        place, body, (place.blocks // 2,),
        [pl.BlockSpec((count, depth), lambda n, s: (0, 0))]
        + weight.specs(weight.lines, 2 * size, lambda n: (0, n))
        + [pl.BlockSpec((1, 2 * size), lambda n, s: (0, n))],
        [column, column, pl.BlockSpec((count, 2 * size), lambda n, s: (0, n))],
        [jax.ShapeDtypeStruct((count, width // 2), BF16)] * 2 + [pltpu.HBM((count, width), BF16)],
        (inputs, *weight.arrays, bias),
        name="hidden_layer",
    )


def last_layer(place, inputs, weight, bias, base):
    count, half = inputs[0].shape
    width = base.shape[1]
    steps = 4 if place.relative else 1
    size = half // steps

    def body(_, inputs_own, inputs_other, own_ref, other_ref, bias_ref, base_ref, out_ref, total_ref):
        step = pl.program_id(0)
        part = nn(inputs_own[...], rows_of(own_ref)) + nn(inputs_other[...], rows_of(other_ref))

        @pl.when(step == 0)
        def _():
            total_ref[...] = part

        @pl.when((step > 0) & (step < steps - 1))
        def _():
            total_ref[...] += part

        @pl.when(step == steps - 1)
        def _():
            total = total_ref[...] + part if steps > 1 else part
            out_ref[...] = (base_ref[...] + (total + bias_ref[...])).astype(BF16)

    column = pl.BlockSpec((count, size), lambda n, s: (0, n))
    rest = pl.BlockSpec((count, width), lambda n, s: (0, 0))
    return call(
        place, body, (steps,),
        [column, column]
        + weight.specs(weight.lines // steps, width, lambda n: (n, 0))
        + [pl.BlockSpec((1, width), lambda n, s: (0, 0)), rest],
        rest, jax.ShapeDtypeStruct((count, width), BF16), (*inputs, *weight.arrays, bias, base),
        scratch=[pltpu.VMEM((count, width), F32)],
        name="last_layer",
    )


def hidden_grad(place, grads, weight, slope):
    count, width = grads.shape
    hidden = slope.shape[1]
    pairs = place.blocks // 2
    size = hidden // place.blocks

    def body(flip_ref, grads_ref, own_ref, other_ref, slope_ref, out_ref, sum_ref):
        for k, weight_ref in enumerate((own_ref, other_ref)):
            at = block_slice(k ^ flip_ref[0], size)
            value = (nt(grads_ref[...], rows_of(weight_ref)) * slope_ref[:, at].astype(F32)).astype(BF16)
            out_ref[:, at] = value
            sum_ref[:, at] = jnp.sum(value.astype(F32), axis=0, keepdims=True)

    column = pl.BlockSpec((count, 2 * size), lambda n, s: (0, n))
    return call(
        place, body, (pairs,),
        [pl.BlockSpec((count, width), lambda n, s: (0, 0))]
        + weight.specs(1, width, lambda n: (n, 0))
        + [column],
        [column, pl.BlockSpec((1, 2 * size), lambda n, s: (0, n))],
        [jax.ShapeDtypeStruct((count, hidden), BF16), jax.ShapeDtypeStruct((1, hidden), F32)],
        (grads, *weight.arrays, pinned(slope)),
        name="hidden_grad",
    )


def back_project(place, grads, weight, start, name):
    count, width = grads.shape
    half = weight.half
    block = 256

    def body(_, grads_ref, own_ref, other_ref, out_ref):
        out_ref[:, :half] = nt(grads_ref[...], rows_of(own_ref)).astype(BF16)
        out_ref[:, half:] = nt(grads_ref[...], rows_of(other_ref)).astype(BF16)

    return call(
        place, body, (count // block,),
        [pl.BlockSpec((block, width), lambda m, s: (m, 0))]
        + weight.specs(weight.lines, width, lambda m: (0, start // width)),
        pl.BlockSpec((block, 2 * half), lambda m, s: (m, 0)),
        jax.ShapeDtypeStruct((count, 2 * half), BF16), (grads, *weight.arrays),
        name=name,
    )


def back_project_natural(place, grads, weight, start, name):
    count, width = grads.shape
    half = weight.half
    block = 256
    blocks = place.blocks
    size = 2 * half // blocks

    def body(flip_ref, grads_ref, own_ref, other_ref, out_ref):
        for k, weight_ref in enumerate((own_ref, other_ref)):
            total = nt(grads_ref[...], rows_of(weight_ref)).astype(BF16)
            for b in range(blocks // 2):
                at = natural_block(k * (blocks // 2) + b, flip_ref[0], blocks) if blocks > 2 else k
                out_ref[:, block_slice(at, size)] = total[:, b * size : (b + 1) * size]

    return call(
        place, body, (count // block,),
        [pl.BlockSpec((block, width), lambda m, s: (m, 0))]
        + weight.specs(weight.lines, width, lambda m: (0, start // width)),
        pl.BlockSpec((block, 2 * half), lambda m, s: (m, 0)),
        jax.ShapeDtypeStruct((count, 2 * half), BF16), (grads, *weight.arrays),
        name=name,
    )


def back_project_norm(place, grads, weight, start, values, gain, base, kinds, name):
    count, width = grads.shape
    half = weight.half
    features = 2 * half
    block = 256
    blocks = place.blocks
    size = features // blocks

    def body(flip_ref, grads_ref, own_ref, other_ref, values_ref, gain_ref, base_ref, *refs):
        outs, sums_ref, upstream_ref = refs[: len(kinds)], refs[len(kinds)], refs[len(kinds) + 1]
        for k, weight_ref in enumerate((own_ref, other_ref)):
            total = nt(grads_ref[...], rows_of(weight_ref))
            for b in range(blocks // 2):
                at = natural_block(k * (blocks // 2) + b, flip_ref[0], blocks) if blocks > 2 else k
                upstream_ref[:, block_slice(at, size)] = total[:, b * size : (b + 1) * size]
        upstream = upstream_ref[...]
        hat, inverse = normalized(values_ref[...].astype(F32))
        weighted = upstream * gain_ref[...]
        base_values = base_ref[...].astype(F32)
        grad = base_values + inverse * (
            weighted
            - jnp.mean(weighted, axis=1, keepdims=True)
            - hat * jnp.mean(weighted * hat, axis=1, keepdims=True)
        )
        for out in outs:
            out[...] = grad.astype(out.dtype)

        @pl.when(pl.program_id(0) == 0)
        def _():
            sums_ref[...] = jnp.zeros_like(sums_ref)

        sums_ref[0:1] += jnp.sum(upstream * hat, axis=0, keepdims=True)
        sums_ref[1:2] += jnp.sum(upstream, axis=0, keepdims=True)
        sums_ref[2:3] += jnp.sum(base_values, axis=0, keepdims=True)

    row = pl.BlockSpec((block, features), lambda m, s: (m, 0))
    sums = pl.BlockSpec((8, features), lambda m, s: (0, 0))
    return call(
        place, body, (count // block,),
        [pl.BlockSpec((block, width), lambda m, s: (m, 0))]
        + weight.specs(
            weight.lines, width, lambda m: (0, start // width), pipeline_mode=pl.Buffered(1)
        )
        + [row, pl.BlockSpec((1, features), lambda m, s: (0, 0)), row],
        [row] * len(kinds) + [sums],
        [(pltpu.HBM if kind == F32 else jax.ShapeDtypeStruct)((count, features), kind) for kind in kinds]
        + [jax.ShapeDtypeStruct((8, features), F32)],
        (pinned(grads) if width > 2 * features else grads, *weight.arrays, pinned(values), gain, pinned(base)),
        scratch=[pltpu.VMEM((block, features), F32)],
        name=name,
    )


def part_of(inputs, part):
    if isinstance(inputs, tuple):
        return inputs[part], 0, inputs[part].shape[1]
    return inputs, part, inputs.shape[1] // 2


def weight_part(place, inputs, grads, part, name, total=None, start=0, into=None):
    inputs, part, depth = part_of(inputs, part)
    count, width = grads.shape
    rows = min(1024, depth)
    tile = width if width <= 1024 else width // 2
    steps = depth // rows

    def body(_, inputs_ref, grads_ref, *refs):
        refs[-1][...] = tn(inputs_ref[...], grads_ref[...]).astype(BF16)

    return call(
        place, body, (steps, width // tile),
        [
            pl.BlockSpec((count, rows), lambda k, n, s: (0, part * steps + k)),
            pl.BlockSpec((count, tile), lambda k, n, s: (0, n)),
        ]
        + [pl.BlockSpec(memory_space=pl.ANY)] * (into is not None),
        pl.BlockSpec((rows, tile), lambda k, n, s: (k, start // tile + n)),
        jax.ShapeDtypeStruct((depth, total or width), BF16),
        (inputs, grads) + ((into,) if into is not None else ()),
        name=name, aliases={3: 0} if into is not None else {},
    )


def weight_sums(place, inputs, grads, arrived, name, total=None, start=0, into=None):
    inputs, _, depth = part_of(inputs, 0)
    count, width = grads.shape
    planes, lines = place.planes, place.lines
    each = depth // (lines * planes)
    tile = width if width * depth <= 2**19 else width // 2
    first, arrived = arrived
    pieces = planes // 2 * lines

    def body(slots_ref, inputs_ref, grads_ref, arrived_ref, *refs):
        kept_ref, sent_ref, total_ref = refs[-3:]
        total_ref[...] = tn(inputs_ref[...], grads_ref[...]) + arrived_ref[...].astype(F32)
        for k in range(planes):
            out_ref = kept_ref if k < planes // 2 else sent_ref
            for n in range(lines):
                line = slots_ref[place.at_lines + n]
                here = pl.multiple_of((line * planes + slots_ref[place.at_plane + k]) * each, each)
                out_ref[k % (planes // 2) * lines + n] = total_ref[pl.ds(here, each)].astype(BF16)

    block = pl.BlockSpec((pieces, each, tile), lambda n, s: (0, 0, start // tile + n))
    out = jax.ShapeDtypeStruct((pieces, each, total or width), BF16)
    return call(
        place, body, (width // tile,),
        [
            pl.BlockSpec((count, depth), lambda n, s: (0, 0)),
            pl.BlockSpec((count, tile), lambda n, s: (0, n)),
            pl.BlockSpec((depth, tile), lambda n, s: (0, first // tile + n)),
        ]
        + [pl.BlockSpec(memory_space=pl.ANY)] * (2 if into is not None else 0),
        [block, block], [out, out], (inputs, grads, arrived) + (tuple(into) if into is not None else ()),
        scratch=[pltpu.VMEM((depth, tile), F32)],
        name=name, aliases={4: 0, 5: 1} if into is not None else {},
    )


class WeightGrad:
    def __init__(self, place, inputs, grads, names):
        if not isinstance(inputs, list):
            inputs, grads, names = [inputs], [grads], [names]
        self.place = place
        self.inputs, self.grads, self.names = inputs, grads, names
        self.starts = [sum(grad.shape[1] for grad in grads[:k]) for k in range(len(grads))]
        total = sum(grad.shape[1] for grad in grads)
        sides = []
        for part in (1,) if place.relative else (1, 0):
            into = None
            for k, name in enumerate(names):
                into = weight_part(
                    place, inputs[k], grads[k], part, name + ("_own", "_other")[part], total,
                    self.starts[k], into,
                )
            sides.append(into)
        first = sides[0]
        if not place.relative:
            each = first.shape[0] // place.lines
            both = jnp.concatenate(sides[::-1]).reshape(place.lines, 2, each, -1)
            self.own = lax.dynamic_index_in_dim(both, place.core, 1, keepdims=False)
            first = lax.dynamic_index_in_dim(both, 1 - place.core, 1, keepdims=False)
            first = first.reshape(-1, total)
        self.arrived = place.swap_core(first)

    def sums(self, more=None):
        place = self.place
        parts = [self] if more is None else [self, more]
        arrived = [place.wait(part.arrived) for part in parts]
        total = sum(value.shape[1] for value in arrived)
        if place.relative:
            into, before = None, 0
            for part, value in zip(parts, arrived):
                for k, name in enumerate(part.names):
                    into = weight_sums(
                        place, part.inputs[k], part.grads[k], (part.starts[k], value), name + "_own",
                        total, before + part.starts[k], into,
                    )
                before += value.shape[1]
            return into
        own = jnp.concatenate([part.own for part in parts], axis=2)
        sums = own.astype(F32) + jnp.concatenate(arrived, axis=1).astype(F32).reshape(own.shape)
        sums = sums.astype(BF16).reshape(place.lines, place.planes, -1, total)
        sums = sums.transpose(1, 0, 2, 3)[place.plane_slots]
        sums = sums[:, place.line ^ jnp.array(place.reversed_lines())]
        return jnp.split(sums.reshape(place.planes * place.lines, -1, total), 2)


def own_lanes(head, values, scaling=None):
    lane = lax.broadcasted_iota(jnp.int32, values.shape, 1)
    size = values.shape[1] // 2
    scaled = values if scaling is None else values * scaling
    return jnp.where((lane >= head * size) & (lane < (head + 1) * size), scaled, 0).astype(BF16)


def softmax(scores):
    weights = jnp.exp(scores - jnp.max(scores, axis=1, keepdims=True))
    return weights * (1.0 / jnp.sum(weights, axis=1, keepdims=True))


def relative_lanes(place, width):
    per = width // place.blocks // LANES

    def column(p, flip):
        return relative_block(p // per, flip, place.blocks) * per + p % per

    return column


def lane_block(k):
    return slice(k * LANES, (k + 1) * LANES)


def attention(place, query, key_value, starts, items, per, masked, name):
    count = query.shape[0]
    rows, keys = count // items, key_value.shape[0] // items
    pairs = HEADS // 2
    width = pairs * LANES
    scaling = (width // HEADS) ** (-0.5)
    column = relative_lanes(place, width)

    def body(scalars_ref, query_ref, key_ref, value_ref, out_ref, prob_ref):
        for k in range(per):
            total = 0.0
            for head in range(2):
                scores = nt(own_lanes(head, query_ref[:, lane_block(k)], scaling), key_ref[:, lane_block(k)])
                weights = softmax(masked(scores, scalars_ref, pl.program_id(0))).astype(BF16)
                prob_ref[0, 2 * k + head] = weights
                total = total + nn(weights, own_lanes(head, value_ref[:, lane_block(k)]))
            at = column(pl.program_id(1) * per + k, scalars_ref[0])
            out_ref[:, block_slice(at, LANES)] = total.astype(BF16)

    spec = lambda size, start: pl.BlockSpec((size, per * LANES), lambda b, p, s: (b, start // per + p))
    return call(
        place, body, (items, pairs // per),
        [spec(rows, 0), spec(keys, starts[0]), spec(keys, starts[1])],
        [
            pl.BlockSpec((rows, width), lambda b, p, s: (b, 0)),
            pl.BlockSpec((1, 2 * per, rows, keys), lambda b, p, s: (b, p, 0, 0)),
        ],
        [
            jax.ShapeDtypeStruct((count, width), BF16),
            pltpu.HBM((items, HEADS, rows, keys), BF16),
        ],
        (query, key_value, key_value),
        name=name,
    )


def attention_grads(
    place, query, key_value, starts, probability, attended, grad, out_widths, items, per, name
):
    count = query.shape[0]
    rows, keys = count // items, key_value.shape[0] // items
    pairs = HEADS // 2
    width = pairs * LANES
    scaling = (width // HEADS) ** (-0.5)
    column = relative_lanes(place, width)
    alone = len(out_widths) == 1

    def body(scalars_ref, query_ref, key_ref, value_ref, prob_ref, attended_ref, grad_ref, *outs):
        for k in range(per):
            pair = pl.program_id(1) * per + k
            at = block_slice(column(pair, scalars_ref[0]), LANES)
            query_total = key_total = value_total = 0.0
            for head in range(2):
                weights = prob_ref[0, 2 * k + head]
                own_grad = own_lanes(head, grad_ref[:, at])
                prob_grad = nt(own_grad, value_ref[:, lane_block(k)])
                centre = jnp.sum(
                    own_grad.astype(F32) * attended_ref[:, at].astype(F32), axis=1, keepdims=True
                )
                score_grad = (weights.astype(F32) * (prob_grad - centre)).astype(BF16)
                query_total = query_total + nn(
                    score_grad, own_lanes(head, key_ref[:, lane_block(k)], scaling)
                )
                key_total = key_total + tn(
                    score_grad, own_lanes(head, query_ref[:, lane_block(k)], scaling)
                )
                value_total = value_total + tn(weights, own_grad)
            first = pairs if alone else 0
            outs[0][:, block_slice(pair, LANES)] = query_total.astype(BF16)
            outs[-1][:, block_slice(first + pair, LANES)] = key_total.astype(BF16)
            outs[-1][:, block_slice(first + pairs + pair, LANES)] = value_total.astype(BF16)

    spec = lambda size, start: pl.BlockSpec((size, per * LANES), lambda b, p, s: (b, start // per + p))
    heights = [rows] if alone else [rows, keys]
    return call(
        place, body, (items, pairs // per),
        [
            spec(rows, 0), spec(keys, starts[0]), spec(keys, starts[1]),
            pl.BlockSpec((1, 2 * per, rows, keys), lambda b, p, s: (b, p, 0, 0)),
            pl.BlockSpec((rows, width), lambda b, p, s: (b, 0)),
            pl.BlockSpec((rows, width), lambda b, p, s: (b, 0)),
        ],
        [
            pl.BlockSpec((height, wide), lambda b, p, s: (b, 0))
            for height, wide in zip(heights, out_widths)
        ],
        [
            jax.ShapeDtypeStruct((items * height, wide), BF16)
            for height, wide in zip(heights, out_widths)
        ],
        (query, key_value, key_value, pinned(probability), attended, grad),
        name=name,
    )


def causal(scores, scalars_ref, item):
    row = lax.broadcasted_iota(jnp.int32, scores.shape, 0)
    column = lax.broadcasted_iota(jnp.int32, scores.shape, 1)
    return jnp.where(column <= row, scores, NEGATIVE)


def visible(first_length):
    def masked(scores, scalars_ref, item):
        column = lax.broadcasted_iota(jnp.int32, scores.shape, 1)
        return jnp.where(column < scalars_ref[first_length + item], scores, NEGATIVE)

    return masked


def per_device(
    tokens,
    text_states,
    caption_len,
    out_grad,
    norm1_gain,
    norm1_bias,
    qkv_weight,
    self_out,
    norm2_gain,
    norm2_bias,
    cross_query,
    cross_kv,
    cross_out,
    norm3_gain,
    norm3_bias,
    ff_in,
    ff_in_bias,
    ff_out,
    ff_out_bias,
):
    place = Place(lax.axis_size("dp") // 2, lax.axis_size("fsdp"), qkv_weight.shape[0], caption_len)
    items, rows, width = tokens.shape
    text = text_states.shape[1]
    count = items * rows
    values0 = tokens.reshape(count, width)
    text_rows = text_states.reshape(items * text, width)
    cot = out_grad.reshape(count, width)

    small = (
        norm1_gain, norm1_bias, norm2_gain, norm2_bias, norm3_gain, norm3_bias, ff_in_bias, ff_out_bias
    )
    sizes = [vector.shape[0] for vector in small]
    middle_group = jnp.concatenate([cross_kv, cross_query, cross_out, self_out], axis=1)
    at_kv, at_query, at_cross, at_self = 0, 2 * width, 3 * width, 4 * width

    shard_rows = qkv_weight.shape[0]
    mid_group = Gather(place, middle_group)
    full_qkv = lax.all_gather(
        jnp.concatenate([qkv_weight, as_columns(place, small, shard_rows)], axis=1),
        AXES, axis=0, tiled=True,
    )
    mid_group.join_line()
    full_out = lax.all_gather(place.wait(ff_out), AXES, axis=0, tiled=True)
    in_group = Gather(place, ff_in)
    text_relative = relabel(place, text_rows)
    mid_group.swap()
    in_group.join_line()
    mid_group.join_plane()
    w_qkv = Weight(place, place.wait(full_qkv))
    normed1, table = norm(place, values0, w_qkv, 3 * width)
    (gain1, bias1, gain2, bias2, gain3, bias3, in_bias, out_bias) = from_table(
        place, table, sizes, shard_rows
    )
    projected = project(place, normed1, w_qkv, 0, 3 * width, name="project_qkv")
    w_mid = mid_group.weight()
    text_kv = project(place, text_relative, w_mid, at_kv, 2 * width, name="project_text")
    in_group.swap()
    pairs = HEADS // 2
    attended1, probs1 = attention(
        place, projected, projected, (pairs, 2 * pairs), items, 4, causal, "self_attention"
    )
    values1, normed2 = project_norm(
        place, attended1, w_mid, at_self, values0, gain2, bias2, "self_out_norm"
    )
    query2 = project(place, normed2, w_mid, at_query, width, name="project_query")
    attended2, probs2 = attention(
        place, query2, text_kv, (0, pairs), items, 4, visible(place.at_length), "cross_attention"
    )
    in_group.join_plane()
    values2, normed3 = project_norm(
        place, attended2, w_mid, at_cross, values1, gain3, bias3, "cross_out_norm"
    )
    w_in = in_group.weight()
    *middle, slope = hidden_layer(place, normed3, w_in, in_bias)
    ff_out_terms = WeightGrad(place, tuple(middle), cot, "ff_out_grad")
    w_out = Weight(place, place.wait(full_out))

    before_grad, in_bias_sum = hidden_grad(place, cot, w_out, slope)
    ff_out_own = ff_out_terms.sums()
    ff_in_terms = WeightGrad(place, normed3, before_grad, "ff_in_grad")

    ff_out_sums = Scatter(place, *ff_out_own)
    cross_grad, cross_round, sums3 = back_project_norm(
        place, before_grad, w_in, 0, values2, gain3, cot, (F32, BF16), "norm3_grad"
    )
    ff_in_own = ff_in_terms.sums()
    attended2_grad = back_project(place, cross_round, w_mid, at_cross, "attended2_grad")
    query2_grad, text_kv_grad = attention_grads(
        place, query2, text_kv, (0, pairs), probs2, attended2, attended2_grad, (width, 2 * width), items, 4,
        "cross_attention_grads",
    )
    ff_out_sums.next()
    middle_terms = WeightGrad(
        place,
        [text_relative, normed2, attended2],
        [text_kv_grad, query2_grad, cross_round],
        ["cross_kv_grad", "cross_query_grad", "cross_out_grad"],
    )

    ff_in_sums = Scatter(place, *ff_in_own)
    self_grad, self_round, sums2 = back_project_norm(
        place, query2_grad, w_mid, at_query, values1, gain2, cross_grad, (F32, BF16), "norm2_grad"
    )
    middle_own = middle_terms.sums()
    attended1_grad = back_project(place, self_round, w_mid, at_self, "attended1_grad")
    (projected_grad,) = attention_grads(
        place, projected, projected, (pairs, 2 * pairs), probs1, attended1, attended1_grad, (3 * width,), items, 4,
        "self_attention_grads",
    )
    ff_out_sums.next()
    ff_in_sums.next()
    last_terms = WeightGrad(
        place, [normed1, attended1], [projected_grad, self_round], ["qkv_grad", "self_out_grad"]
    )

    middle_sums = Scatter(place, *middle_own)
    text_grad = back_project_natural(place, text_kv_grad, w_mid, at_kv, "text_grad")
    last_own = last_terms.sums()
    result = last_layer(place, middle, w_out, out_bias, values2)
    ff_out_sums.next()
    ff_in_sums.next()
    middle_sums.next()

    last_sums = Scatter(place, *last_own)
    tokens_grad, sums1 = back_project_norm(
        place, projected_grad, w_qkv, 0, values0, gain1, self_grad, (BF16,), "norm1_grad"
    )
    table = relabel(place, as_table(place, (
        sums1[0], sums1[1], sums2[0], sums2[1], sums3[0], sums3[1], in_bias_sum[0], sums3[2]
    ), shard_rows))
    small_terms = WeightGrad(place, table, jnp.eye(LANES, dtype=BF16), "small_grad")
    ff_in_sums.next()
    (ff_out_grad,) = ff_out_sums.result(width)
    small_sums = Scatter(place, *small_terms.sums())
    middle_sums.next()
    last_sums.next()
    last_sums.next()
    small_sums.next()
    middle_sums.next()
    (ff_in_grad,) = ff_in_sums.result(ff_in.shape[1])
    small_sums.next()
    last_sums.next()
    small_sums.next()
    cross_kv_grad, cross_query_grad, cross_out_grad = middle_sums.result(2 * width, width, width)
    small_grads = small_sums.result(LANES)[0].T
    qkv_grad, self_out_grad = last_sums.result(3 * width, width)
    own, at = [], 0
    for size in sizes:
        own.append(small_grads[at : at + size // shard_rows].reshape(-1))
        at += size // shard_rows
    return (
        result.reshape(items, rows, width),
        tokens_grad.reshape(items, rows, width),
        text_grad.reshape(items, text, width),
        own[0],
        own[1],
        qkv_grad,
        self_out_grad,
        own[2],
        own[3],
        cross_query_grad,
        cross_kv_grad,
        cross_out_grad,
        own[4],
        own[5],
        ff_in_grad,
        own[6],
        ff_out_grad,
        own[7],
    )


def solution(mesh):
    whole = P(AXES, None, None)
    matrix = P(AXES, None)
    vector = P(AXES)
    weights = (
        vector, vector, matrix, matrix, vector, vector, matrix, matrix, matrix, vector, vector, matrix,
        vector, matrix, vector,
    )
    return jax.shard_map(
        per_device,
        mesh=mesh,
        in_specs=(whole, whole, vector, whole) + weights,
        out_specs=(whole, whole, whole) + weights,
        check_vma=False,
    )
```

```python
import functools

import jax
import jax.numpy as jnp
from jax import lax
from jax.experimental import pallas as pl
from jax.experimental.pallas import tpu as pltpu
from jax.sharding import PartitionSpec as P

HEADS = 16
EPSILON = 1e-05
NEGATIVE = -1e30
AXES = ("dp", "fsdp")
F32 = jnp.float32
BF16 = jnp.bfloat16
LANES = 128
HBM_BYTES = 6400000
VMEM_MIB = {
    "project_qkv": 14,
    "self_attention": 11,
    "self_out_norm": 10,
    "project_query": 11,
    "cross_out_norm": 11,
    "hidden_layer": 14,
    "last_layer": 20,
    "hidden_grad": 14,
    "norm3_grad": 25,
    "cross_attention_grads": 13,
    "norm2_grad": 17,
    "self_attention_grads": 25,
    "norm1_grad": 20,
    "qkv_grad_other": 11,
    "qkv_grad_own": 17,
    "self_out_grad_own": 10,
    "cross_kv_grad_own": 10,
    "cross_query_grad_own": 10,
    "cross_out_grad_own": 10,
    "ff_in_grad_other": 14,
    "ff_in_grad_own": 22,
    "ff_out_grad_other": 11,
    "ff_out_grad_own": 23,
}


def nt(first, second):
    return lax.dot_general(first, second, (((1,), (1,)), ((), ())), preferred_element_type=F32)


def tn(first, second):
    return lax.dot_general(first, second, (((0,), (0,)), ((), ())), preferred_element_type=F32)


def nn(first, second):
    return lax.dot_general(first, second, (((1,), (0,)), ((), ())), preferred_element_type=F32)


def call(place, body, grid, in_specs, out_specs, out_shape, args, scratch=(), name=None, aliases=None):
    spec = pltpu.PrefetchScalarGridSpec(
        num_scalar_prefetch=1, grid=grid, in_specs=in_specs, out_specs=out_specs,
        scratch_shapes=list(scratch),
    )
    out_shape = jax.tree.map(
        lambda o: pltpu.HBM(o.shape, o.dtype) if is_large(o) else o, out_shape
    )
    out = pl.pallas_call(
        body, grid_spec=spec, out_shape=out_shape, name=name, input_output_aliases=aliases or {},
        cost_estimate=pl.CostEstimate(flops=1, bytes_accessed=1, transcendentals=0),
        compiler_params=pltpu.CompilerParams(vmem_limit_bytes=(VMEM_MIB.get(name, 8) if place.relative else 48) * 2**20),
    )(place.scalars, *[in_hbm(arg) for arg in args])
    return place.wait(out)


def is_large(value):
    return isinstance(value, (jax.Array, jax.ShapeDtypeStruct)) and (
        value.size * value.dtype.itemsize >= HBM_BYTES
    )


def pinned(value):
    return pltpu.with_memory_space_constraint(value, pltpu.HBM)


def in_hbm(value):
    if not is_large(value):
        return value
    return pinned(value)


class Place:
    def __init__(self, lines, planes, rows, lengths):
        self.lines = lines
        self.planes = planes
        self.bits = [1 << k for k in range(planes.bit_length() - 1)]
        self.line_bits = [1 << k for k in range(lines.bit_length() - 1)]
        dp = lax.axis_index("dp")
        self.line = dp // 2
        self.core = dp % 2
        self.plane = lax.axis_index("fsdp")
        self.relative = planes * rows % LANES == 0
        self.flip = (self.core if self.relative else jnp.zeros_like(self.core)).astype(jnp.int32)
        self.blocks = 2 * lines if self.relative else 2
        stages = len(self.bits)
        self.masks = [[0], [0]]
        for core in range(2):
            for stage in range(stages):
                bit = self.stage_bit(stage, core)
                self.masks[core] = self.masks[core] + [m ^ bit for m in self.masks[core]]
        masks = jnp.where(self.core == 0, jnp.array(self.masks[0]), jnp.array(self.masks[1]))
        self.plane_slots = (masks ^ self.plane).astype(jnp.int32)
        self.line_slots = ((self.line - jnp.arange(lines)) % lines).astype(jnp.int32)
        self.core_slots = (jnp.arange(2) ^ self.core).astype(jnp.int32)
        parts = [
            self.flip[None], lengths, self.plane_slots, self.line_slots, self.core_slots,
            (self.line ^ jnp.array(self.reversed_lines())).astype(jnp.int32),
        ]
        starts = [0]
        for part in parts:
            starts.append(starts[-1] + part.shape[0])
        _, self.at_length, self.at_plane, self.at_line, self.at_core, self.at_lines, _ = starts
        self.scalars = jnp.concatenate(parts)

    def wait(self, values):
        values, self.scalars = lax.optimization_barrier((values, self.scalars))
        return values

    def reversed_lines(self):
        order = [0]
        for bit in reversed(self.line_bits):
            order = order + [mask ^ bit for mask in order]
        return order

    def stage_bit(self, stage, core):
        return self.bits[(stage + core) % len(self.bits)]

    def _permute(self, value, target):
        pairs = []
        for line in range(self.lines):
            for core in range(2):
                for plane in range(self.planes):
                    l, c, p = target(line, core, plane)
                    pairs.append(
                        ((line * 2 + core) * self.planes + plane, (l * 2 + c) * self.planes + p)
                    )
        return lax.ppermute(value, AXES, pairs)

    def shift_line(self, value, step):
        return self._permute(value, lambda l, c, p: ((l + step) % self.lines, c, p))

    def swap_plane(self, value, stage):
        return self._permute(value, lambda l, c, p: (l, c, p ^ self.stage_bit(stage, c)))

    def swap_line(self, value, bit):
        return self._permute(value, lambda l, c, p: (l ^ bit, c, p))

    def swap_core(self, value):
        return self._permute(value, lambda l, c, p: (l, 1 - c, p))


def interleave(place, pieces, first):
    count = len(pieces)
    outer, rows, width = pieces[0].shape
    tile = width

    def body(slots_ref, *refs):
        out_ref = refs[count]
        for k in range(count):
            out_ref[0, pl.ds(slots_ref[first + k], 1)] = refs[k][...]

    moved = 2 * count * pieces[0].size * pieces[0].dtype.itemsize
    return call(
        place, body,
        (outer, width // tile),
        [pl.BlockSpec((1, rows, tile), lambda a, n, s: (a, 0, n))] * count,
        pl.BlockSpec((1, count, rows, tile), lambda a, n, s: (a, 0, 0, n)),
        jax.ShapeDtypeStruct((outer, count, rows, width), pieces[0].dtype),
        pieces,
        name="interleave",
    )


class Gather:
    def __init__(self, place, shard):
        self.place = place
        self.rows, self.width = shard.shape
        shard = place.wait(shard)
        self.pieces = [shard] + [place.shift_line(shard, s) for s in range(1, place.lines)]
        self.stage = 0

    def wait(self):
        self.pieces = self.place.wait(self.pieces)

    def join_line(self):
        place = self.place
        self.wait()
        held = interleave(place, [piece[None] for piece in self.pieces], place.at_line)
        self.pieces = [held.reshape(place.lines, self.rows, self.width)]
        self.swap()

    def swap(self):
        if self.stage:
            self.wait()
        self.pieces = self.pieces + [
            self.place.swap_plane(piece, self.stage) for piece in self.pieces
        ]
        self.stage += 1

    def join_plane(self):
        place = self.place
        while self.stage < len(place.bits):
            self.swap()
        self.wait()
        half = interleave(place, self.pieces, place.at_plane)
        self.own = half.reshape(place.lines, place.planes * self.rows, self.width)
        self.other = place.swap_core(self.own)

    def weight(self):
        place = self.place
        self.other = place.wait(self.other)
        if place.relative:
            return Weight(place, self.own[:, None], self.other[:, None])
        both = interleave(place, [self.own, self.other], place.at_core)
        return Weight(place, both.reshape(-1, self.width))


class Weight:
    def __init__(self, place, *arrays):
        self.full = len(arrays) == 1
        self.width = arrays[0].shape[-1]
        if self.full:
            arrays = (arrays[0].reshape(place.blocks // 2, 2, -1, self.width),) * 2
        self.arrays = arrays
        self.lines, _, self.rows, _ = arrays[0].shape
        self.half = self.lines * self.rows

    def specs(self, lines, columns, index, **more):
        def make(part):
            def index_map(*args):
                line, column = index(*args[:-1])
                which = args[-1][0] ^ part if self.full else 0
                return line, which, 0, column

            return pl.BlockSpec((lines, 1, self.rows, columns), index_map, **more)

        return [make(0), make(1)]


def rows_of(ref):
    lines, _, rows, columns = ref.shape
    return ref[...].reshape(lines * rows, columns)


def as_columns(place, vectors, rows):
    parts = jnp.concatenate([vector.reshape(-1, rows) for vector in vectors])
    return jnp.pad(parts, ((0, LANES - parts.shape[0]), (0, 0))).T


def as_table(place, sums, rows):
    owners = place.lines * 2 * place.planes
    parts = [
        vector.reshape(owners, -1, rows).transpose(1, 0, 2).reshape(-1, owners * rows)
        for vector in sums
    ]
    table = jnp.concatenate(parts)
    return jnp.pad(table, ((0, LANES - table.shape[0]), (0, 0))).astype(BF16)


def from_table(place, table, sizes, rows):
    owners = place.lines * 2 * place.planes
    vectors, at = [], 0
    for size in sizes:
        each = size // rows
        part = table[at : at + each]
        if each > 1:
            part = part.reshape(each, owners, rows).transpose(1, 0, 2)
        vectors.append(part.reshape(1, -1))
        at += each
    return vectors


class Scatter:
    def __init__(self, place, kept, sent):
        self.place = place
        self.kept = kept
        self.stages = [
            functools.partial(place.swap_plane, stage=stage)
            for stage in reversed(range(len(place.bits)))
        ] + [functools.partial(place.swap_line, bit=bit) for bit in place.line_bits]
        self.arrived = self.stages.pop(0)(place.wait(sent))

    def next(self):
        self.kept, sent = combine(self.place, self.kept, self.place.wait(self.arrived))
        self.arrived = self.stages.pop(0)(sent)

    def result(self, *widths):
        while self.stages:
            self.next()
        arrived = self.place.wait(self.arrived)
        parts, at = [], 0
        for width in widths:
            here = slice(at, at + width)
            parts.append(self.kept[0][:, here].astype(F32) + arrived[0][:, here].astype(F32))
            at += width
        return parts


def combine(place, kept, arrived):
    count, rows, width = kept.shape
    each = count // 2
    outs = count // each
    steps = 2 if kept.size > 2**18 and width % 256 == 0 else 1
    tile = width // steps

    def body(_, kept_ref, arrived_ref, *refs):
        total = (kept_ref[...].astype(F32) + arrived_ref[...].astype(F32)).astype(BF16)
        for k in range(outs):
            refs[k][...] = total[k * each : (k + 1) * each]

    def block(size):
        return pl.BlockSpec((size, rows, tile), lambda n, s: (0, 0, n))

    out = jax.ShapeDtypeStruct((each, rows, width), BF16)
    return call(
        place, body, (steps,), [block(count), block(count)], [block(each)] * outs, [out] * outs,
        (kept, arrived), name="combine",
    )


def relative_block(index, flip, blocks):
    return (index % 2 ^ flip) * (blocks // 2) + index // 2


def natural_block(index, flip, blocks):
    half = blocks // 2
    return index % half * 2 + (index // half ^ flip)


def block_slice(index, size):
    return pl.ds(pl.multiple_of(index * size, size), size)


def store_relative(ref, values, flip, blocks):
    size = values.shape[1] // blocks
    for k in range(blocks):
        at = relative_block(k, flip, blocks) if blocks > 2 else k
        ref[:, block_slice(at, size)] = values[:, k * size : (k + 1) * size].astype(ref.dtype)


def normalized(values):
    center = values - jnp.mean(values, axis=1, keepdims=True)
    inverse = lax.rsqrt(jnp.mean(center * center, axis=1, keepdims=True) + EPSILON)
    return center * inverse, inverse


def norm(place, values, weight, start):
    count, width = values.shape
    block = 256
    blocks = place.blocks

    def body(flip_ref, values_ref, columns_ref, out_ref, table_ref):
        @pl.when(pl.program_id(0) == 0)
        def _():
            table_ref[...] = columns_ref[...].reshape(width, LANES).astype(F32).T

        hat, _ = normalized(values_ref[...].astype(F32))
        store_relative(out_ref, hat * table_ref[0:1] + table_ref[1:2], flip_ref[0], blocks)

    row = pl.BlockSpec((block, width), lambda m, s: (m, 0))
    lines, _, rows, _ = weight.arrays[0].shape
    return call(
        place, body, (count // block,),
        [row, pl.BlockSpec((lines, 2, rows, LANES), lambda m, s: (0, 0, 0, start // LANES))],
        [row, pl.BlockSpec((LANES, width), lambda m, s: (0, 0))],
        [jax.ShapeDtypeStruct((count, width), BF16), jax.ShapeDtypeStruct((LANES, width), F32)],
        (values, weight.arrays[0]), name="norm",
    )


def relabel(place, values):
    count, width = values.shape
    blocks = place.blocks
    if blocks == 2:
        return values
    size = width // blocks

    def body(_, values_ref, out_ref):
        out_ref[...] = values_ref[...]

    return call(
        place, body, (blocks,),
        [pl.BlockSpec((count, size), lambda k, s: (0, k))],
        pl.BlockSpec((count, size), lambda k, s: (0, relative_block(k, s[0], blocks))),
        jax.ShapeDtypeStruct((count, width), values.dtype), (values,),
        name="relabel",
    )


def project(place, inputs, weight, start, width, tile=1024, name="project"):
    count, depth = inputs.shape
    half = depth // 2

    def body(_, inputs_ref, own_ref, other_ref, out_ref):
        total = nn(inputs_ref[:, :half], rows_of(own_ref)) + nn(inputs_ref[:, half:], rows_of(other_ref))
        out_ref[...] = total.astype(BF16)

    return call(
        place, body, (width // tile,),
        [pl.BlockSpec((count, depth), lambda n, s: (0, 0))]
        + weight.specs(weight.lines, tile, lambda n: (0, start // tile + n)),
        pl.BlockSpec((count, tile), lambda n, s: (0, n)),
        jax.ShapeDtypeStruct((count, width), BF16), (inputs, *weight.arrays),
        name=name,
    )


def project_norm(place, inputs, weight, start, base, gain, bias, name):
    count, depth = inputs.shape
    half = depth // 2
    width = base.shape[1]
    block = 256
    blocks = place.blocks

    def body(flip_ref, inputs_ref, own_ref, other_ref, base_ref, gain_ref, bias_ref, after_ref, out_ref):
        total = nn(inputs_ref[:, :half], rows_of(own_ref)) + nn(inputs_ref[:, half:], rows_of(other_ref))
        total = total + base_ref[...].astype(F32)
        after_ref[...] = total
        hat, _ = normalized(total)
        store_relative(out_ref, hat * gain_ref[...] + bias_ref[...], flip_ref[0], blocks)

    row = pl.BlockSpec((block, width), lambda m, s: (m, 0))
    vector = pl.BlockSpec((1, width), lambda m, s: (0, 0))
    return call(
        place, body, (count // block,),
        [pl.BlockSpec((block, depth), lambda m, s: (m, 0))]
        + weight.specs(weight.lines, width, lambda m: (0, start // width))
        + [row, vector, vector],
        [row, row],
        [pltpu.HBM((count, width), F32), jax.ShapeDtypeStruct((count, width), BF16)],
        (inputs, *weight.arrays, pinned(base), gain, bias),
        name=name,
    )


def hidden_layer(place, inputs, weight, bias):
    count, depth = inputs.shape
    half = depth // 2
    width = weight.width
    size = width // place.blocks

    def body(flip_ref, inputs_ref, own_ref, other_ref, bias_ref, middle_own, middle_other, slope_ref):
        scale = 0.7978845608028654
        for k, middle_ref in enumerate((middle_own, middle_other)):
            at = block_slice(k ^ flip_ref[0], size)
            upper = own_ref[:, 0, :, at].reshape(half, size)
            lower = other_ref[:, 0, :, at].reshape(half, size)
            before = nn(inputs_ref[:, :half], upper) + nn(inputs_ref[:, half:], lower)
            before = before + bias_ref[:, at]
            square = before * before
            half_sum = 0.5 + 0.5 * jnp.tanh(before * (scale + scale * 0.044715 * square))
            middle = before * half_sum
            middle_ref[...] = middle.astype(BF16)
            slope = half_sum + middle * (1.0 - half_sum) * (2.0 * scale + 6.0 * scale * 0.044715 * square)
            slope_ref[:, at] = slope.astype(BF16)

    column = pl.BlockSpec((count, size), lambda n, s: (0, n))
    return call(
        place, body, (place.blocks // 2,),
        [pl.BlockSpec((count, depth), lambda n, s: (0, 0))]
        + weight.specs(weight.lines, 2 * size, lambda n: (0, n))
        + [pl.BlockSpec((1, 2 * size), lambda n, s: (0, n))],
        [column, column, pl.BlockSpec((count, 2 * size), lambda n, s: (0, n))],
        [jax.ShapeDtypeStruct((count, width // 2), BF16)] * 2 + [pltpu.HBM((count, width), BF16)],
        (inputs, *weight.arrays, bias),
        name="hidden_layer",
    )


def last_layer(place, inputs, weight, bias, base):
    count, half = inputs[0].shape
    width = base.shape[1]
    steps = 4 if place.relative else 1
    size = half // steps

    def body(_, inputs_own, inputs_other, own_ref, other_ref, bias_ref, base_ref, out_ref, total_ref):
        step = pl.program_id(0)
        part = nn(inputs_own[...], rows_of(own_ref)) + nn(inputs_other[...], rows_of(other_ref))

        @pl.when(step == 0)
        def _():
            total_ref[...] = part

        @pl.when((step > 0) & (step < steps - 1))
        def _():
            total_ref[...] += part

        @pl.when(step == steps - 1)
        def _():
            total = total_ref[...] + part if steps > 1 else part
            out_ref[...] = (base_ref[...] + (total + bias_ref[...])).astype(BF16)

    column = pl.BlockSpec((count, size), lambda n, s: (0, n))
    rest = pl.BlockSpec((count, width), lambda n, s: (0, 0))
    return call(
        place, body, (steps,),
        [column, column]
        + weight.specs(weight.lines // steps, width, lambda n: (n, 0))
        + [pl.BlockSpec((1, width), lambda n, s: (0, 0)), rest],
        rest, jax.ShapeDtypeStruct((count, width), BF16), (*inputs, *weight.arrays, bias, base),
        scratch=[pltpu.VMEM((count, width), F32)],
        name="last_layer",
    )


def hidden_grad(place, grads, weight, slope):
    count, width = grads.shape
    hidden = slope.shape[1]
    pairs = place.blocks // 2
    size = hidden // place.blocks

    def body(flip_ref, grads_ref, own_ref, other_ref, slope_ref, out_ref, sum_ref):
        for k, weight_ref in enumerate((own_ref, other_ref)):
            at = block_slice(k ^ flip_ref[0], size)
            value = (nt(grads_ref[...], rows_of(weight_ref)) * slope_ref[:, at].astype(F32)).astype(BF16)
            out_ref[:, at] = value
            sum_ref[:, at] = jnp.sum(value.astype(F32), axis=0, keepdims=True)

    column = pl.BlockSpec((count, 2 * size), lambda n, s: (0, n))
    return call(
        place, body, (pairs,),
        [pl.BlockSpec((count, width), lambda n, s: (0, 0))]
        + weight.specs(1, width, lambda n: (n, 0))
        + [column],
        [column, pl.BlockSpec((1, 2 * size), lambda n, s: (0, n))],
        [jax.ShapeDtypeStruct((count, hidden), BF16), jax.ShapeDtypeStruct((1, hidden), F32)],
        (pinned(grads), *weight.arrays, pinned(slope)),
        name="hidden_grad",
    )


def back_project(place, grads, weight, start, name):
    count, width = grads.shape
    half = weight.half
    block = 256

    def body(_, grads_ref, own_ref, other_ref, out_ref):
        out_ref[:, :half] = nt(grads_ref[...], rows_of(own_ref)).astype(BF16)
        out_ref[:, half:] = nt(grads_ref[...], rows_of(other_ref)).astype(BF16)

    return call(
        place, body, (count // block,),
        [pl.BlockSpec((block, width), lambda m, s: (m, 0))]
        + weight.specs(weight.lines, width, lambda m: (0, start // width)),
        pl.BlockSpec((block, 2 * half), lambda m, s: (m, 0)),
        jax.ShapeDtypeStruct((count, 2 * half), BF16), (grads, *weight.arrays),
        name=name,
    )


def back_project_natural(place, grads, weight, start, name):
    count, width = grads.shape
    half = weight.half
    block = 256
    blocks = place.blocks
    size = 2 * half // blocks

    def body(flip_ref, grads_ref, own_ref, other_ref, out_ref):
        for k, weight_ref in enumerate((own_ref, other_ref)):
            total = nt(grads_ref[...], rows_of(weight_ref)).astype(BF16)
            for b in range(blocks // 2):
                at = natural_block(k * (blocks // 2) + b, flip_ref[0], blocks) if blocks > 2 else k
                out_ref[:, block_slice(at, size)] = total[:, b * size : (b + 1) * size]

    return call(
        place, body, (count // block,),
        [pl.BlockSpec((block, width), lambda m, s: (m, 0))]
        + weight.specs(weight.lines, width, lambda m: (0, start // width)),
        pl.BlockSpec((block, 2 * half), lambda m, s: (m, 0)),
        jax.ShapeDtypeStruct((count, 2 * half), BF16), (grads, *weight.arrays),
        name=name,
    )


def back_project_norm(place, grads, weight, start, values, gain, base, kinds, name):
    count, width = grads.shape
    half = weight.half
    features = 2 * half
    block = 256
    blocks = place.blocks
    size = features // blocks

    def body(flip_ref, grads_ref, own_ref, other_ref, values_ref, gain_ref, base_ref, *refs):
        outs, sums_ref, upstream_ref = refs[: len(kinds)], refs[len(kinds)], refs[len(kinds) + 1]
        for k, weight_ref in enumerate((own_ref, other_ref)):
            total = nt(grads_ref[...], rows_of(weight_ref))
            for b in range(blocks // 2):
                at = natural_block(k * (blocks // 2) + b, flip_ref[0], blocks) if blocks > 2 else k
                upstream_ref[:, block_slice(at, size)] = total[:, b * size : (b + 1) * size]
        upstream = upstream_ref[...]
        hat, inverse = normalized(values_ref[...].astype(F32))
        weighted = upstream * gain_ref[...]
        base_values = base_ref[...].astype(F32)
        grad = base_values + inverse * (
            weighted
            - jnp.mean(weighted, axis=1, keepdims=True)
            - hat * jnp.mean(weighted * hat, axis=1, keepdims=True)
        )
        for out in outs:
            out[...] = grad.astype(out.dtype)

        @pl.when(pl.program_id(0) == 0)
        def _():
            sums_ref[...] = jnp.zeros_like(sums_ref)

        sums_ref[0:1] += jnp.sum(upstream * hat, axis=0, keepdims=True)
        sums_ref[1:2] += jnp.sum(upstream, axis=0, keepdims=True)
        sums_ref[2:3] += jnp.sum(base_values, axis=0, keepdims=True)

    row = pl.BlockSpec((block, features), lambda m, s: (m, 0))
    sums = pl.BlockSpec((8, features), lambda m, s: (0, 0))
    return call(
        place, body, (count // block,),
        [pl.BlockSpec((block, width), lambda m, s: (m, 0))]
        + weight.specs(
            weight.lines, width, lambda m: (0, start // width), pipeline_mode=pl.Buffered(1)
        )
        + [row, pl.BlockSpec((1, features), lambda m, s: (0, 0)), row],
        [row] * len(kinds) + [sums],
        [(pltpu.HBM if kind == F32 else jax.ShapeDtypeStruct)((count, features), kind) for kind in kinds]
        + [jax.ShapeDtypeStruct((8, features), F32)],
        (pinned(grads) if width > 2 * features else grads, *weight.arrays, pinned(values), gain, pinned(base)),
        scratch=[pltpu.VMEM((block, features), F32)],
        name=name,
    )


def part_of(inputs, part):
    if isinstance(inputs, tuple):
        return inputs[part], 0, inputs[part].shape[1]
    return inputs, part, inputs.shape[1] // 2


def weight_part(place, inputs, grads, part, name, total=None, start=0, into=None):
    inputs, part, depth = part_of(inputs, part)
    count, width = grads.shape
    rows = min(1024, depth)
    tile = width if width <= 1024 else width // 2
    steps = depth // rows

    def body(_, inputs_ref, grads_ref, *refs):
        refs[-1][...] = tn(inputs_ref[...], grads_ref[...]).astype(BF16)

    return call(
        place, body, (steps, width // tile),
        [
            pl.BlockSpec((count, rows), lambda k, n, s: (0, part * steps + k)),
            pl.BlockSpec((count, tile), lambda k, n, s: (0, n)),
        ]
        + [pl.BlockSpec(memory_space=pl.ANY)] * (into is not None),
        pl.BlockSpec((rows, tile), lambda k, n, s: (k, start // tile + n)),
        jax.ShapeDtypeStruct((depth, total or width), BF16),
        (inputs, grads) + ((into,) if into is not None else ()),
        name=name, aliases={3: 0} if into is not None else {},
    )


def weight_sums(place, inputs, grads, arrived, name, total=None, start=0, into=None):
    inputs, _, depth = part_of(inputs, 0)
    count, width = grads.shape
    planes, lines = place.planes, place.lines
    each = depth // (lines * planes)
    tile = width if width * depth <= 2**19 else width // 2
    first, arrived = arrived
    pieces = planes // 2 * lines

    def body(slots_ref, inputs_ref, grads_ref, arrived_ref, *refs):
        kept_ref, sent_ref, total_ref = refs[-3:]
        total_ref[...] = tn(inputs_ref[...], grads_ref[...]) + arrived_ref[...].astype(F32)
        for k in range(planes):
            out_ref = kept_ref if k < planes // 2 else sent_ref
            for n in range(lines):
                line = slots_ref[place.at_lines + n]
                here = pl.multiple_of((line * planes + slots_ref[place.at_plane + k]) * each, each)
                out_ref[k % (planes // 2) * lines + n] = total_ref[pl.ds(here, each)].astype(BF16)

    block = pl.BlockSpec((pieces, each, tile), lambda n, s: (0, 0, start // tile + n))
    out = jax.ShapeDtypeStruct((pieces, each, total or width), BF16)
    return call(
        place, body, (width // tile,),
        [
            pl.BlockSpec((count, depth), lambda n, s: (0, 0)),
            pl.BlockSpec((count, tile), lambda n, s: (0, n)),
            pl.BlockSpec((depth, tile), lambda n, s: (0, first // tile + n)),
        ]
        + [pl.BlockSpec(memory_space=pl.ANY)] * (2 if into is not None else 0),
        [block, block], [out, out], (inputs, grads, arrived) + (tuple(into) if into is not None else ()),
        scratch=[pltpu.VMEM((depth, tile), F32)],
        name=name, aliases={4: 0, 5: 1} if into is not None else {},
    )


class WeightGrad:
    def __init__(self, place, inputs, grads, names):
        if not isinstance(inputs, list):
            inputs, grads, names = [inputs], [grads], [names]
        self.place = place
        self.inputs, self.grads, self.names = inputs, grads, names
        self.starts = [sum(grad.shape[1] for grad in grads[:k]) for k in range(len(grads))]
        total = sum(grad.shape[1] for grad in grads)
        sides = []
        for part in (1,) if place.relative else (1, 0):
            into = None
            for k, name in enumerate(names):
                into = weight_part(
                    place, inputs[k], grads[k], part, name + ("_own", "_other")[part], total,
                    self.starts[k], into,
                )
            sides.append(into)
        first = sides[0]
        if not place.relative:
            each = first.shape[0] // place.lines
            both = jnp.concatenate(sides[::-1]).reshape(place.lines, 2, each, -1)
            self.own = lax.dynamic_index_in_dim(both, place.core, 1, keepdims=False)
            first = lax.dynamic_index_in_dim(both, 1 - place.core, 1, keepdims=False)
            first = first.reshape(-1, total)
        self.arrived = place.swap_core(first)

    def sums(self, more=None):
        place = self.place
        parts = [self] if more is None else [self, more]
        arrived = [place.wait(part.arrived) for part in parts]
        total = sum(value.shape[1] for value in arrived)
        if place.relative:
            into, before = None, 0
            for part, value in zip(parts, arrived):
                for k, name in enumerate(part.names):
                    into = weight_sums(
                        place, part.inputs[k], part.grads[k], (part.starts[k], value), name + "_own",
                        total, before + part.starts[k], into,
                    )
                before += value.shape[1]
            return into
        own = jnp.concatenate([part.own for part in parts], axis=2)
        sums = own.astype(F32) + jnp.concatenate(arrived, axis=1).astype(F32).reshape(own.shape)
        sums = sums.astype(BF16).reshape(place.lines, place.planes, -1, total)
        sums = sums.transpose(1, 0, 2, 3)[place.plane_slots]
        sums = sums[:, place.line ^ jnp.array(place.reversed_lines())]
        return jnp.split(sums.reshape(place.planes * place.lines, -1, total), 2)


def own_lanes(head, values, scaling=None):
    lane = lax.broadcasted_iota(jnp.int32, values.shape, 1)
    size = values.shape[1] // 2
    scaled = values if scaling is None else values * scaling
    return jnp.where((lane >= head * size) & (lane < (head + 1) * size), scaled, 0).astype(BF16)


def softmax(scores):
    weights = jnp.exp(scores - jnp.max(scores, axis=1, keepdims=True))
    return weights * (1.0 / jnp.sum(weights, axis=1, keepdims=True))


def relative_lanes(place, width):
    per = width // place.blocks // LANES

    def column(p, flip):
        return relative_block(p // per, flip, place.blocks) * per + p % per

    return column


def lane_block(k):
    return slice(k * LANES, (k + 1) * LANES)


def attention(place, query, key_value, starts, items, per, masked, name):
    count = query.shape[0]
    rows, keys = count // items, key_value.shape[0] // items
    pairs = HEADS // 2
    width = pairs * LANES
    scaling = (width // HEADS) ** (-0.5)
    column = relative_lanes(place, width)

    def body(scalars_ref, query_ref, key_ref, value_ref, out_ref, prob_ref):
        for k in range(per):
            total = 0.0
            for head in range(2):
                scores = nt(own_lanes(head, query_ref[:, lane_block(k)], scaling), key_ref[:, lane_block(k)])
                weights = softmax(masked(scores, scalars_ref, pl.program_id(0))).astype(BF16)
                prob_ref[0, 2 * k + head] = weights
                total = total + nn(weights, own_lanes(head, value_ref[:, lane_block(k)]))
            at = column(pl.program_id(1) * per + k, scalars_ref[0])
            out_ref[:, block_slice(at, LANES)] = total.astype(BF16)

    spec = lambda size, start: pl.BlockSpec((size, per * LANES), lambda b, p, s: (b, start // per + p))
    return call(
        place, body, (items, pairs // per),
        [spec(rows, 0), spec(keys, starts[0]), spec(keys, starts[1])],
        [
            pl.BlockSpec((rows, width), lambda b, p, s: (b, 0)),
            pl.BlockSpec((1, 2 * per, rows, keys), lambda b, p, s: (b, p, 0, 0)),
        ],
        [
            jax.ShapeDtypeStruct((count, width), BF16),
            pltpu.HBM((items, HEADS, rows, keys), BF16),
        ],
        (query, key_value, key_value),
        name=name,
    )


def attention_grads(
    place, query, key_value, starts, probability, attended, grad, out_widths, items, per, name
):
    count = query.shape[0]
    rows, keys = count // items, key_value.shape[0] // items
    pairs = HEADS // 2
    width = pairs * LANES
    scaling = (width // HEADS) ** (-0.5)
    column = relative_lanes(place, width)
    alone = len(out_widths) == 1

    def body(scalars_ref, query_ref, key_ref, value_ref, prob_ref, attended_ref, grad_ref, *outs):
        for k in range(per):
            pair = pl.program_id(1) * per + k
            at = block_slice(column(pair, scalars_ref[0]), LANES)
            query_total = key_total = value_total = 0.0
            for head in range(2):
                weights = prob_ref[0, 2 * k + head]
                own_grad = own_lanes(head, grad_ref[:, at])
                prob_grad = nt(own_grad, value_ref[:, lane_block(k)])
                centre = jnp.sum(
                    own_grad.astype(F32) * attended_ref[:, at].astype(F32), axis=1, keepdims=True
                )
                score_grad = (weights.astype(F32) * (prob_grad - centre)).astype(BF16)
                query_total = query_total + nn(
                    score_grad, own_lanes(head, key_ref[:, lane_block(k)], scaling)
                )
                key_total = key_total + tn(
                    score_grad, own_lanes(head, query_ref[:, lane_block(k)], scaling)
                )
                value_total = value_total + tn(weights, own_grad)
            first = pairs if alone else 0
            outs[0][:, block_slice(pair, LANES)] = query_total.astype(BF16)
            outs[-1][:, block_slice(first + pair, LANES)] = key_total.astype(BF16)
            outs[-1][:, block_slice(first + pairs + pair, LANES)] = value_total.astype(BF16)

    spec = lambda size, start: pl.BlockSpec((size, per * LANES), lambda b, p, s: (b, start // per + p))
    heights = [rows] if alone else [rows, keys]
    return call(
        place, body, (items, pairs // per),
        [
            spec(rows, 0), spec(keys, starts[0]), spec(keys, starts[1]),
            pl.BlockSpec((1, 2 * per, rows, keys), lambda b, p, s: (b, p, 0, 0)),
            pl.BlockSpec((rows, width), lambda b, p, s: (b, 0)),
            pl.BlockSpec((rows, width), lambda b, p, s: (b, 0)),
        ],
        [
            pl.BlockSpec((height, wide), lambda b, p, s: (b, 0))
            for height, wide in zip(heights, out_widths)
        ],
        [
            jax.ShapeDtypeStruct((items * height, wide), BF16)
            for height, wide in zip(heights, out_widths)
        ],
        (query, key_value, key_value, pinned(probability), attended, grad),
        name=name,
    )


def causal(scores, scalars_ref, item):
    row = lax.broadcasted_iota(jnp.int32, scores.shape, 0)
    column = lax.broadcasted_iota(jnp.int32, scores.shape, 1)
    return jnp.where(column <= row, scores, NEGATIVE)


def visible(first_length):
    def masked(scores, scalars_ref, item):
        column = lax.broadcasted_iota(jnp.int32, scores.shape, 1)
        return jnp.where(column < scalars_ref[first_length + item], scores, NEGATIVE)

    return masked


def per_device(
    tokens,
    text_states,
    caption_len,
    out_grad,
    norm1_gain,
    norm1_bias,
    qkv_weight,
    self_out,
    norm2_gain,
    norm2_bias,
    cross_query,
    cross_kv,
    cross_out,
    norm3_gain,
    norm3_bias,
    ff_in,
    ff_in_bias,
    ff_out,
    ff_out_bias,
):
    place = Place(lax.axis_size("dp") // 2, lax.axis_size("fsdp"), qkv_weight.shape[0], caption_len)
    items, rows, width = tokens.shape
    text = text_states.shape[1]
    count = items * rows
    values0 = tokens.reshape(count, width)
    text_rows = text_states.reshape(items * text, width)
    cot = out_grad.reshape(count, width)

    small = (
        norm1_gain, norm1_bias, norm2_gain, norm2_bias, norm3_gain, norm3_bias, ff_in_bias, ff_out_bias
    )
    sizes = [vector.shape[0] for vector in small]
    middle_group = jnp.concatenate([cross_kv, cross_query, cross_out, self_out], axis=1)
    at_kv, at_query, at_cross, at_self = 0, 2 * width, 3 * width, 4 * width

    shard_rows = qkv_weight.shape[0]
    mid_group = Gather(place, middle_group)
    full_qkv = lax.all_gather(
        jnp.concatenate([qkv_weight, as_columns(place, small, shard_rows)], axis=1),
        AXES, axis=0, tiled=True,
    )
    mid_group.join_line()
    full_out = lax.all_gather(place.wait(ff_out), AXES, axis=0, tiled=True)
    in_group = Gather(place, ff_in)
    text_relative = relabel(place, text_rows)
    mid_group.swap()
    in_group.join_line()
    mid_group.join_plane()
    w_qkv = Weight(place, place.wait(full_qkv))
    normed1, table = norm(place, values0, w_qkv, 3 * width)
    (gain1, bias1, gain2, bias2, gain3, bias3, in_bias, out_bias) = from_table(
        place, table, sizes, shard_rows
    )
    projected = project(place, normed1, w_qkv, 0, 3 * width, name="project_qkv")
    w_mid = mid_group.weight()
    text_kv = project(place, text_relative, w_mid, at_kv, 2 * width, name="project_text")
    in_group.swap()
    pairs = HEADS // 2
    attended1, probs1 = attention(
        place, projected, projected, (pairs, 2 * pairs), items, 4, causal, "self_attention"
    )
    values1, normed2 = project_norm(
        place, attended1, w_mid, at_self, values0, gain2, bias2, "self_out_norm"
    )
    query2 = project(place, normed2, w_mid, at_query, width, name="project_query")
    attended2, probs2 = attention(
        place, query2, text_kv, (0, pairs), items, 4, visible(place.at_length), "cross_attention"
    )
    in_group.join_plane()
    values2, normed3 = project_norm(
        place, attended2, w_mid, at_cross, values1, gain3, bias3, "cross_out_norm"
    )
    w_in = in_group.weight()
    *middle, slope = hidden_layer(place, normed3, w_in, in_bias)
    ff_out_terms = WeightGrad(place, tuple(middle), cot, "ff_out_grad")
    w_out = Weight(place, place.wait(full_out))

    before_grad, in_bias_sum = hidden_grad(place, cot, w_out, slope)
    ff_out_own = ff_out_terms.sums()
    ff_in_terms = WeightGrad(place, normed3, before_grad, "ff_in_grad")

    ff_out_sums = Scatter(place, *ff_out_own)
    cross_grad, cross_round, sums3 = back_project_norm(
        place, before_grad, w_in, 0, values2, gain3, cot, (F32, BF16), "norm3_grad"
    )
    ff_in_own = ff_in_terms.sums()
    attended2_grad = back_project(place, cross_round, w_mid, at_cross, "attended2_grad")
    query2_grad, text_kv_grad = attention_grads(
        place, query2, text_kv, (0, pairs), probs2, attended2, attended2_grad, (width, 2 * width), items, 4,
        "cross_attention_grads",
    )
    ff_out_sums.next()
    middle_terms = WeightGrad(
        place,
        [text_relative, normed2, attended2],
        [text_kv_grad, query2_grad, cross_round],
        ["cross_kv_grad", "cross_query_grad", "cross_out_grad"],
    )

    ff_in_sums = Scatter(place, *ff_in_own)
    self_grad, self_round, sums2 = back_project_norm(
        place, query2_grad, w_mid, at_query, values1, gain2, cross_grad, (F32, BF16), "norm2_grad"
    )
    middle_own = middle_terms.sums()
    attended1_grad = back_project(place, self_round, w_mid, at_self, "attended1_grad")
    (projected_grad,) = attention_grads(
        place, projected, projected, (pairs, 2 * pairs), probs1, attended1, attended1_grad, (3 * width,), items, 4,
        "self_attention_grads",
    )
    ff_out_sums.next()
    ff_in_sums.next()
    last_terms = WeightGrad(
        place, [normed1, attended1], [projected_grad, self_round], ["qkv_grad", "self_out_grad"]
    )

    middle_sums = Scatter(place, *middle_own)
    text_grad = back_project_natural(place, text_kv_grad, w_mid, at_kv, "text_grad")
    last_own = last_terms.sums()
    result = last_layer(place, middle, w_out, out_bias, values2)
    ff_out_sums.next()
    ff_in_sums.next()
    middle_sums.next()

    last_sums = Scatter(place, *last_own)
    tokens_grad, sums1 = back_project_norm(
        place, projected_grad, w_qkv, 0, values0, gain1, self_grad, (BF16,), "norm1_grad"
    )
    table = relabel(place, as_table(place, (
        sums1[0], sums1[1], sums2[0], sums2[1], sums3[0], sums3[1], in_bias_sum[0], sums3[2]
    ), shard_rows))
    small_terms = WeightGrad(place, table, jnp.eye(LANES, dtype=BF16), "small_grad")
    ff_in_sums.next()
    (ff_out_grad,) = ff_out_sums.result(width)
    small_sums = Scatter(place, *small_terms.sums())
    middle_sums.next()
    last_sums.next()
    last_sums.next()
    small_sums.next()
    middle_sums.next()
    (ff_in_grad,) = ff_in_sums.result(ff_in.shape[1])
    small_sums.next()
    last_sums.next()
    small_sums.next()
    cross_kv_grad, cross_query_grad, cross_out_grad = middle_sums.result(2 * width, width, width)
    small_grads = small_sums.result(LANES)[0].T
    qkv_grad, self_out_grad = last_sums.result(3 * width, width)
    own, at = [], 0
    for size in sizes:
        own.append(small_grads[at : at + size // shard_rows].reshape(-1))
        at += size // shard_rows
    return (
        result.reshape(items, rows, width),
        tokens_grad.reshape(items, rows, width),
        text_grad.reshape(items, text, width),
        own[0],
        own[1],
        qkv_grad,
        self_out_grad,
        own[2],
        own[3],
        cross_query_grad,
        cross_kv_grad,
        cross_out_grad,
        own[4],
        own[5],
        ff_in_grad,
        own[6],
        ff_out_grad,
        own[7],
    )


def solution(mesh):
    whole = P(AXES, None, None)
    matrix = P(AXES, None)
    vector = P(AXES)
    weights = (
        vector, vector, matrix, matrix, vector, vector, matrix, matrix, matrix, vector, vector, matrix,
        vector, matrix, vector,
    )
    return jax.shard_map(
        per_device,
        mesh=mesh,
        in_specs=(whole, whole, vector, whole) + weights,
        out_specs=(whole, whole, whole) + weights,
        check_vma=False,
    )
```
